128 devices in a mesh: ctx: 16 (over y_hi, x, core), grp: 8 (over z, y_lo).
Axes of the slice: x: 4, y: 4 (y_hi: 2, y_lo: 2; y = y_hi * 2 + y_lo), z: 4, core: 2. Of those that a mesh axis runs over, the one named last changes fastest.
Arguments:
- queries: bfloat16 [8, 8192, 32, 128], P('grp', 'ctx'), may hold values from -6 to 6
- keys: bfloat16 [8, 8192, 32, 128], P('grp', 'ctx'), may hold values from -0.0625 to 0.0625
- values: bfloat16 [8, 8192, 32, 128], P('grp', 'ctx'), may hold values from -6 to 6
- prefill_decay: float32 [8, 8192, 32], P('grp', 'ctx'), may hold values from -0.8 to 0, as said below
- start_states: float32 [8, 32, 128, 128], P('grp', 'ctx'), may hold values from -3 to 3
- resident_states: float32 [64, 32, 128, 128], P(None, 'ctx', None, 'grp'), may hold values from -3 to 3
- slot_of_prompt: int32 [8], replicated, may hold values from 0 to 63, as said below
- decode_queries: bfloat16 [64, 4, 32, 128], P(None, None, 'ctx'), may hold values from -6 to 6
- decode_keys: bfloat16 [64, 4, 32, 128], P(None, None, 'ctx'), may hold values from -1.75 to 1.75
- decode_values: bfloat16 [64, 4, 32, 128], P(None, None, 'ctx', 'grp'), may hold values from -6 to 6
- decode_gate: bfloat16 [64, 4, 32, 128], P(None, None, 'ctx', 'grp'), may hold values from -8 to 8
- decode_decay: float32 [64, 4, 32], P(None, None, 'ctx'), may hold values from -0.8 to 0, as said below
- norm_gain: float32 [32, 128], P('ctx', 'grp'), may hold values from 0.5 to 1.5
- out_weight: bfloat16 [32, 128, 6144], P('ctx', 'grp'), may hold values from -0.09375 to 0.09375
Outputs:
- prefill_out: bfloat16 [8, 8192, 32, 128], P('grp', 'ctx')
- decode_states: float32 [64, 32, 128, 128], P(None, 'ctx', None, 'grp')
- decoded: float32 [256, 6144], P(('ctx', 'grp'))
The draws below stay inside these ranges and needn't reach their ends.
Inputs may be any that keep to these rules, and one draw needn't show every extreme that they name: `slot_of_prompt`: distinct decode rows; rows 0 and 63 are always among them. `prefill_decay`: strictly negative. `decode_decay`: strictly negative.
All inputs are finite; a program needn't handle non-finite values.
Results may differ from the reference program's by a relative error of at most 0.0029.
Values sent between devices are 32-bit elements; how exact they have to be, the bound alone decides.
A program may use at most 192 MiB of HBM per device.

```python
import jax
import jax.numpy as jnp
from jax import lax

D = 6144
H = 32
HS = 128
SLOTS = 64
STEPS = 4
PROMPTS = 8
LEN = 8192
BLOCK = 512


def head_rates(key, lowest, highest):
    spread = jax.random.uniform(key, (H,), jnp.float32)
    return jnp.exp(jnp.log(lowest) + spread * (jnp.log(highest) - jnp.log(lowest)))


def decay_field(key, tensor_dimensions, decay_rate_values, spike_probability):
    first, secondary_entry, third = jax.random.split(key, 3)
    jagged_decay = jax.random.uniform(first, tensor_dimensions, jnp.float32, 0.5, 1.5)
    spike_draw = jax.random.bernoulli(secondary_entry, spike_probability, tensor_dimensions[:-1] + (1,)).astype(jnp.float32)
    layer_depth_count = jax.random.uniform(third, tensor_dimensions, jnp.float32, 0.22, 0.7)
    return -(decay_rate_values * jagged_decay + spike_draw * layer_depth_count)


def draw_prefill_decay(key, part):
    decay_rate_values = head_rates(key, 0.3 / LEN, 1.0 / 30.0)
    key = jax.random.fold_in(key, 11)
    return decay_field(key, (PROMPTS, LEN, H), decay_rate_values, 3.0 / LEN)


def draw_decode_decay(key, part):
    decay_rate_values = head_rates(key, 0.3 / LEN, 1.0 / 30.0)
    key = jax.random.fold_in(key, 23)
    return decay_field(key, (SLOTS, STEPS, H), decay_rate_values, 0.1)


def draw_slot_of_prompt(key, part):
    key = jax.random.fold_in(key, 37)
    first, secondary_entry = jax.random.split(key)
    middle = 1 + jax.random.permutation(first, SLOTS - 2)[:PROMPTS - 2]
    chosen = jnp.concatenate([jnp.array([0, SLOTS - 1], jnp.int32), middle.astype(jnp.int32)])
    return jax.random.permutation(secondary_entry, chosen).astype(jnp.int32)


def level_of(key, dims, cuts, low, high):
    def one(axis_at, shards_of):
        steps = jax.random.uniform(jax.random.fold_in(jax.random.fold_in(key, 6), axis_at), (shards_of,), jnp.float32, low / len(cuts), high / len(cuts))
        return jnp.repeat(jnp.exp(steps), dims[axis_at] // shards_of).reshape((-1,) + (1,) * (len(dims) - axis_at - 1))

    factor_of = one(*cuts[0])
    for cut in cuts[1:]:
        factor_of = factor_of * one(*cut)
    return factor_of


def centred(stream_key, dims, scale, bound, pieces=(), held_as=jnp.bfloat16):
    entries = jax.random.normal(stream_key, dims, jnp.float32) * scale
    if len(pieces) > 0:
        entries = level_of(stream_key, dims, pieces, -0.22, 0.18) * entries
    return jnp.clip(entries, min=-bound, max=bound).astype(held_as)


def setup_inputs(seed: int = 0) -> dict:
    seeds = jax.random.split(jax.random.key(seed), 15)
    queries = centred(seeds[0], (PROMPTS, LEN, H, HS), 1.0, 6.0, ((0, 8), (1, 16)))
    keys = centred(seeds[1], (PROMPTS, LEN, H, HS), 0.01, 0.0625, ((0, 8), (1, 16)))
    values = centred(seeds[2], (PROMPTS, LEN, H, HS), 1.0, 6.0, ((0, 8), (1, 16)))
    prefill_decay = draw_prefill_decay(jax.random.fold_in(seeds[14], 71), 0)
    start_states = centred(seeds[4], (PROMPTS, H, HS, HS), 0.5, 3.0, ((0, 8), (1, 16)), jnp.float32)
    resident_states = centred(seeds[5], (SLOTS, H, HS, HS), 0.5, 3.0, ((1, 16), (3, 8)), jnp.float32)
    slot_of_prompt = draw_slot_of_prompt(jax.random.fold_in(seeds[14], 71), 0)
    decode_queries = centred(seeds[7], (SLOTS, STEPS, H, HS), 1.0, 6.0, ((2, 16),))
    decode_keys = centred(seeds[8], (SLOTS, STEPS, H, HS), 0.3, 1.75, ((2, 16),))
    decode_values = centred(seeds[9], (SLOTS, STEPS, H, HS), 1.0, 6.0, ((2, 16), (3, 8)))
    decode_gate = centred(seeds[10], (SLOTS, STEPS, H, HS), 1.5, 8.0, ((2, 16), (3, 8)))
    decode_decay = draw_decode_decay(jax.random.fold_in(seeds[14], 71), 0)
    norm_gain = jnp.clip(0.5 + 1.0 * jax.random.uniform(seeds[12], (H, HS), jnp.float32) ** level_of(seeds[12], (H, HS), ((0, 16), (1, 8)), -0.2, 0.2), 0.5, 1.5)
    out_weight = centred(seeds[13], (H, HS, D), (H * HS) ** -0.5, 0.09375, ((0, 16), (1, 8)))
    return dict(queries=queries, keys=keys, values=values, prefill_decay=prefill_decay, start_states=start_states, resident_states=resident_states, slot_of_prompt=slot_of_prompt, decode_queries=decode_queries, decode_keys=decode_keys, decode_values=decode_values, decode_gate=decode_gate, decode_decay=decode_decay, norm_gain=norm_gain, out_weight=out_weight)


def normalize(field):
    mean_sq = lax.optimization_barrier(jnp.mean(field * field, axis=(-2, -1), keepdims=True))
    return field * lax.rsqrt(mean_sq + 1e-06)

def prefill_prompt(query, key_in, value, decay, start):
    blocks = LEN // BLOCK
    q_all = query.reshape(blocks, BLOCK, H, HS)
    k_all = key_in.reshape(blocks, BLOCK, H, HS)
    v_all = value.reshape(blocks, BLOCK, H, HS)
    d_all = decay.reshape(blocks, BLOCK, H)
    hi = lax.Precision.HIGHEST
    places = jnp.arange(BLOCK)
    causal = places[:, None] >= places[None, :]

    def advance(state, inputs):
        q_blk, k_blk, v_blk, d_blk = inputs
        cumul = jnp.cumsum(d_blk, axis=0)
        trans = jnp.transpose(cumul, (1, 0))
        diff = trans[:, :, None] - trans[:, None, :]
        factor = jnp.exp(jnp.where(causal[None, :, :], diff, -1e+30))
        scores = jnp.einsum('thd,shd->hts', q_blk.astype(jnp.float32), k_blk.astype(jnp.float32), precision=hi)
        weights = (scores * factor).astype(jnp.bfloat16)
        inner = jnp.einsum('hts,shd->thd', weights.astype(jnp.float32), v_blk.astype(jnp.float32), precision=hi)
        scaled = q_blk.astype(jnp.float32) * jnp.exp(cumul)[:, :, None]
        outer = jnp.einsum('thd,hde->the', scaled, state, precision=hi)
        ending = cumul[-1]
        k_weighted = k_blk.astype(jnp.float32) * jnp.exp(ending[None, :] - cumul)[:, :, None]
        state = jnp.exp(ending)[:, None, None] * state + jnp.einsum('shd,she->hde', k_weighted, v_blk.astype(jnp.float32), precision=hi)
        return (state, inner + outer)
    final, outputs = lax.scan(advance, start, (q_all, k_all, v_all, d_all))
    return (final, outputs.reshape(LEN, H, HS))

def reference(queries, keys, values, prefill_decay, start_states, resident_states, slot_of_prompt, decode_queries, decode_keys, decode_values, decode_gate, decode_decay, norm_gain, out_weight):
    finals, attention = lax.map(lambda inputs: prefill_prompt(*inputs), (queries, keys, values, prefill_decay, start_states))
    prefill_out = normalize(attention).astype(jnp.bfloat16)
    cache = resident_states.at[slot_of_prompt.astype(jnp.int32)].set(finals)
    outputs = []
    for step in range(STEPS):
        k_now = decode_keys[:, step].astype(jnp.float32)
        v_now = decode_values[:, step].astype(jnp.float32)
        cache = jnp.exp(decode_decay[:, step])[:, :, None, None] * cache + k_now[:, :, :, None] * v_now[:, :, None, :]
        outputs.append(jnp.einsum('shd,shde->she', decode_queries[:, step].astype(jnp.float32), cache, precision=lax.Precision.HIGHEST))
    y_all = jnp.stack(outputs, axis=1)
    normed = (normalize(y_all) * norm_gain * jax.nn.sigmoid(decode_gate.astype(jnp.float32))).astype(jnp.bfloat16)
    decoded = jnp.dot(normed.reshape(SLOTS * STEPS, H * HS), out_weight.reshape(H * HS, D), preferred_element_type=jnp.float32)
    return (prefill_out, cache, decoded)
```

```python
import jax
import jax.numpy as jnp
from jax import lax
from jax.experimental import pallas as pl
from jax.experimental.pallas import tpu as pltpu
from jax.sharding import PartitionSpec as P

H = 32
HS = 128
LOG2E = 1.4426950408889634
MESH = pl.DeviceIdType.MESH
F32 = jnp.float32
BF16 = jnp.bfloat16
VMEM_LIMIT = 60 * 1024 * 1024
T = 512
CH = 128
ROWS = 136
FIRST_HEADS = 16


def dot(a, b):
    return lax.dot_general(a, b, (((1,), (0,)), ((), ())), preferred_element_type=F32)


def split(x):
    hi = x.astype(BF16)
    return hi, (x - hi.astype(F32)).astype(BF16)


def head_of(half, i):
    return 4 * lax.div(i, 2) + 2 * half + lax.rem(i, 2)


def remote(src, dst, send, recv, where):
    return pltpu.make_async_remote_copy(
        src_ref=src, dst_ref=dst, send_sem=send, recv_sem=recv, device_id=where, device_id_type=MESH
    )


def prefill_kernel(
    q_hbm, k_hbm, v_hbm, dec_ref, start_ref, w_ref,
    att_hbm, qh_hbm, p_ref, hand_ref, wt_ref, ec_ref,
    raw, stage, qh, kt, vh, cum2, cum, s_ref, xbuf, tbuf, rbuf, pbuf, qbuf, obuf, pcur, fbuf, hbuf, wf, wr, abuf,
    load_sem, q_sem, att_sem, sa, ra, s1, r1, s2, r2, sb, rb, sh, rh, sw, rw,
):
    c, g = lax.axis_index("ctx"), lax.axis_index("grp")
    core, chip = lax.rem(c, 2), lax.div(c, 2)
    other = 1 - core
    partner = (2 * chip + other, g)

    def peer(j):
        return (2 * j + core, g)

    def load(which, hbm, at):
        return pltpu.make_async_copy(
            hbm.at[pl.ds(at * CH, CH)], raw.at[which, pl.ds(at * CH, CH)], load_sem.at[which, at]
        )

    for which, hbm in ((0, k_hbm), (1, v_hbm), (2, q_hbm)):
        for at in range(T // CH):
            load(which, hbm, at).start()

    bar = pltpu.get_barrier_semaphore()
    pl.semaphore_signal(bar, inc=1, device_id=partner, device_id_type=MESH)

    def greet(d, _):
        pl.semaphore_signal(bar, inc=1, device_id=peer(lax.rem(chip + d, 8)), device_id_type=MESH)
        pl.semaphore_signal(bar, inc=1, device_id=(c, lax.rem(g + d, 8)), device_id_type=MESH)
        return 0

    lax.fori_loop(1, 8, greet, 0)

    lane = lax.broadcasted_iota(jnp.int32, (H, T), 1)
    x = dec_ref[...]
    step = 1
    while step < T:
        x = x + jnp.where(lane >= step, pltpu.roll(x, step, 1), 0.0)
        step *= 2
    cum[...] = x
    cum2[...] = x * LOG2E
    ec_ref[...] = jnp.concatenate([jnp.exp(x), jnp.zeros((HS - H, T), F32)], axis=0).T

    def relay(which, hbm, at, put):
        load(which, hbm, at).wait()
        stage[...] = raw[which, pl.ds(at * CH, CH)].astype(F32).reshape(CH * H, HS)
        for h in range(H):
            put(h, pl.ds(pl.multiple_of(at * CH, CH), CH), stage[pl.ds(h, CH, stride=H), :])

    def put_k(h, span, block):
        kt[h, :, span] = block.T.astype(BF16)

    def put_v(h, span, block):
        vh[h, span, :] = block.astype(BF16)

    def put_q(h, span, block):
        qh[h, span, :] = block.astype(BF16)

    def relay_kv(at, _):
        relay(0, k_hbm, at, put_k)
        relay(1, v_hbm, at, put_v)
        return 0

    lax.fori_loop(0, T // CH, relay_kv, 0)

    def local_state(half, i):
        h = head_of(half, i)
        row = cum[pl.ds(h, 1), :]
        end = row[:, T - 1 : T]
        hi, lo = split(kt[h].astype(F32) * jnp.exp(end - row))
        both = dot(jnp.concatenate([hi, lo], axis=0), vh[h])
        s_ref[half, i, 0:HS, :] = both[:HS] + both[HS:]
        s_ref[half, i, HS:ROWS, :] = jnp.broadcast_to(end, (ROWS - HS, HS))

    def copy_a(m):
        return remote(s_ref.at[other, pl.ds(4 * m, 4)], xbuf.at[pl.ds(4 * m, 4)], sa.at[m], ra.at[m], partner)

    pl.semaphore_wait(bar, 15)

    def other_half(m, _):
        def one(i, _):
            local_state(other, 4 * m + i)
            return 0

        lax.fori_loop(0, 4, one, 0)
        copy_a(m).start()
        return 0

    lax.fori_loop(0, 4, other_half, 0)

    def own_half(i, _):
        local_state(core, i)
        return 0

    lax.fori_loop(0, 16, own_half, 0)

    def wait_a(m, _):
        copy_a(m).wait_recv()
        return 0

    lax.fori_loop(0, 4, wait_a, 0)

    def copy_1(j):
        return remote(tbuf.at[j], rbuf.at[chip], s1.at[j], r1.at[chip], peer(j))

    def arrival_1(j):
        return remote(tbuf.at[j], rbuf.at[j], s1.at[j], r1.at[j], peer(j))

    def chip_total(j):
        for r in range(2):
            i = 2 * j + r
            mine, theirs = s_ref[core, i], xbuf[i]
            end_mine, end_theirs = mine[HS : HS + 1], theirs[HS : HS + 1]
            on_mine = jnp.where(core == 0, jnp.exp(end_theirs), 1.0)
            on_theirs = jnp.where(core == 0, 1.0, jnp.exp(end_mine))
            tbuf[j, r, 0:HS, :] = on_mine * mine[:HS] + on_theirs * theirs[:HS]
            tbuf[j, r, HS:ROWS, :] = mine[HS:] + theirs[HS:]

    def send_total(d, _):
        j = lax.rem(chip + d, 8)
        chip_total(j)
        copy_1(j).start()
        return 0

    lax.fori_loop(1, 8, send_total, 0)
    chip_total(chip)
    rbuf[chip] = tbuf[chip]

    for to in range(8):
        wf[to] = w_ref[:, to * 768 : (to + 1) * 768].astype(F32)

    def copy_w(to):
        return remote(wf.at[to], wr.at[g], sw.at[to], rw.at[g], (c, to))

    def arrival_w(frm):
        return remote(wf.at[frm], wr.at[frm], sw.at[frm], rw.at[frm], (c, frm))

    def send_w(d, _):
        copy_w(lax.rem(g + d, 8)).start()
        return 0

    lax.fori_loop(1, 8, send_w, 0)
    wr[g] = wf[g]

    def relay_q(at, _):
        relay(2, q_hbm, at, put_q)
        return 0

    lax.fori_loop(0, T // CH, relay_q, 0)
    qh_copy = pltpu.make_async_copy(qh, qh_hbm, q_sem)
    qh_copy.start()

    causal = lax.broadcasted_iota(jnp.int32, (HS, HS), 0) >= lax.broadcasted_iota(jnp.int32, (HS, HS), 1)

    def att_copy(h, slot):
        return pltpu.make_async_copy(abuf.at[slot], att_hbm.at[h], att_sem.at[slot])

    def attend(h, slot):
        row = cum2[pl.ds(h, 1), :]
        col = jnp.broadcast_to(row, (HS, T)).T
        left = dot(qh[h], kt[h, :, 0:256])
        right = dot(qh[h, 256:512, :], kt[h, :, 256:512])

        def weigh(a, b):
            scores = left if b < 2 else right
            first = a if b < 2 else a - 2
            part = scores[first * HS : (first + 1) * HS, (b % 2) * HS : (b % 2 + 1) * HS]
            diff = col[a * HS : (a + 1) * HS] - row[:, b * HS : (b + 1) * HS]
            if a == b:
                diff = jnp.where(causal, diff, -1e30)
            return (part * jnp.exp2(diff)).astype(BF16)

        v = vh[h]
        none = jnp.zeros((HS, HS), BF16)
        top = jnp.concatenate([
            jnp.concatenate([weigh(0, 0), none], axis=1),
            jnp.concatenate([weigh(1, 0), weigh(1, 1)], axis=1),
        ], axis=0)
        low = jnp.concatenate([
            jnp.concatenate([weigh(2, 0), weigh(2, 1), weigh(2, 2), none], axis=1),
            jnp.concatenate([weigh(3, 0), weigh(3, 1), weigh(3, 2), weigh(3, 3)], axis=1),
        ], axis=0)
        abuf[slot, 0:256, :] = dot(top, v[0:256])
        abuf[slot, 256:512, :] = dot(low, v)

    def pair(n, _):
        for slot in range(2):

            @pl.when(n > 0)
            def _():
                att_copy(2 * n - 2 + slot, slot).wait()

            attend(2 * n + slot, slot)
            att_copy(2 * n + slot, slot).start()
        return 0

    lax.fori_loop(0, FIRST_HEADS // 2, pair, 0)

    def copy_2(j):
        return remote(pbuf.at[j], qbuf.at[chip], s2.at[j], r2.at[chip], peer(j))

    def arrival_2(j):
        return remote(pbuf.at[j], qbuf.at[j], s2.at[j], r2.at[j], peer(j))

    pcur[...] = start_ref[...]

    def scan(j, _):
        pbuf[j] = pcur[...]

        @pl.when(j != chip)
        def _():
            copy_2(j).start()
            arrival_1(j).wait_recv()

        for r in range(2):
            pcur[r] = jnp.exp(rbuf[j, r, HS : HS + 1, :]) * pcur[r] + rbuf[j, r, 0:HS, :]
        return 0

    lax.fori_loop(0, 8, scan, 0)
    qbuf[chip] = pbuf[chip]

    for r in range(2):
        fbuf[:, r] = pcur[r].T.reshape(8, 16, HS)

    def copy_h(to):
        return remote(fbuf.at[to], hbuf.at[g], sh.at[to], rh.at[g], (c, to))

    def arrival_h(frm):
        return remote(fbuf.at[frm], hbuf.at[frm], sh.at[frm], rh.at[frm], (c, frm))

    def send_h(d, _):
        copy_h(lax.rem(g + d, 8)).start()
        return 0

    lax.fori_loop(1, 8, send_h, 0)
    hbuf[g] = fbuf[g]

    lax.fori_loop(FIRST_HEADS // 2, H // 2, pair, 0)

    def copy_b(m):
        return remote(obuf.at[pl.ds(4 * m, 4)], p_ref.at[core, pl.ds(4 * m, 4)], sb.at[m], rb.at[m], partner)

    def arrival_b(m):
        return remote(obuf.at[pl.ds(4 * m, 4)], p_ref.at[other, pl.ds(4 * m, 4)], sb.at[m], rb.at[m], partner)

    def spread(m, _):
        for n in range(2):
            j = 2 * m + n

            @pl.when(j != chip)
            def _():
                arrival_2(j).wait_recv()

            for r in range(2):
                i = 2 * j + r
                before = qbuf[j, r]
                first = jnp.where(core == 0, s_ref[core, i], xbuf[i])
                after = jnp.exp(first[HS : HS + 1]) * before + first[:HS]
                p_ref[core, i] = jnp.where(core == 0, before, after)
                obuf[i] = jnp.where(core == 0, after, before)
        copy_b(m).start()
        return 0

    lax.fori_loop(0, 4, spread, 0)

    def take_w(d, _):
        frm = lax.rem(g + d, 8)
        arrival_w(frm).wait_recv()
        arrival_h(frm).wait_recv()
        return 0

    lax.fori_loop(1, 8, take_w, 0)
    for frm in range(8):
        wt_ref[frm * 32 : (frm + 1) * 32, :] = wr[frm].astype(BF16)
    hand_ref[...] = hbuf[...]

    for slot in range(2):
        att_copy(H - 2 + slot, slot).wait()
    qh_copy.wait()

    def finish_pair(m, _):
        arrival_b(m).wait_recv()
        copy_b(m).wait_send()
        copy_a(m).wait_send()
        return 0

    lax.fori_loop(0, 4, finish_pair, 0)

    def finish(d, _):
        j = lax.rem(chip + d, 8)
        copy_1(j).wait_send()
        copy_2(j).wait_send()
        to = lax.rem(g + d, 8)
        copy_w(to).wait_send()
        copy_h(to).wait_send()
        return 0

    lax.fori_loop(1, 8, finish, 0)


def prefill(q, k, v, decay, start, weight):
    dma = pltpu.SemaphoreType.DMA
    anywhere = pl.BlockSpec(memory_space=pl.ANY)
    vmem = pl.BlockSpec(memory_space=pltpu.VMEM)
    return pl.pallas_call(
        prefill_kernel,
        name="prefill",
        out_shape=(
            jax.ShapeDtypeStruct((H, T, HS), F32),
            jax.ShapeDtypeStruct((H, T, HS), BF16),
            jax.ShapeDtypeStruct((2, 16, HS, HS), F32),
            jax.ShapeDtypeStruct((8, 2, 16, HS), F32),
            jax.ShapeDtypeStruct((256, 768), BF16),
            jax.ShapeDtypeStruct((T, HS), F32),
        ),
        in_specs=[anywhere, anywhere, anywhere, vmem, vmem, vmem],
        out_specs=(anywhere, anywhere, vmem, vmem, vmem, vmem),
        scratch_shapes=[
            pltpu.VMEM((3, T, H, HS), BF16),
            pltpu.VMEM((CH * H, HS), F32),
            pltpu.VMEM((H, T, HS), BF16),
            pltpu.VMEM((H, HS, T), BF16),
            pltpu.VMEM((H, T, HS), BF16),
            pltpu.VMEM((H, T), F32),
            pltpu.VMEM((H, T), F32),
            pltpu.VMEM((2, 16, ROWS, HS), F32),
            pltpu.VMEM((16, ROWS, HS), F32),
            pltpu.VMEM((8, 2, ROWS, HS), F32),
            pltpu.VMEM((8, 2, ROWS, HS), F32),
            pltpu.VMEM((8, 2, HS, HS), F32),
            pltpu.VMEM((8, 2, HS, HS), F32),
            pltpu.VMEM((16, HS, HS), F32),
            pltpu.VMEM((2, HS, HS), F32),
            pltpu.VMEM((8, 2, 16, HS), F32),
            pltpu.VMEM((8, 2, 16, HS), F32),
            pltpu.VMEM((8, 32, 768), F32),
            pltpu.VMEM((8, 32, 768), F32),
            pltpu.VMEM((2, T, HS), F32),
            dma((3, T // CH)), dma, dma((2,)),
            dma((4,)), dma((4,)), dma((8,)), dma((8,)), dma((8,)), dma((8,)),
            dma((4,)), dma((4,)), dma((8,)), dma((8,)), dma((8,)), dma((8,)),
        ],
        compiler_params=pltpu.CompilerParams(
            collective_id=0, has_side_effects=True, vmem_limit_bytes=VMEM_LIMIT
        ),
    )(q, k, v, decay, start, weight)


def finish_kernel(att_ref, q_ref, p_ref, ec_ref, out_ref, wide, field, stage):
    @pl.when(pl.program_id(0) == 0)
    def _():
        for h in range(H):
            hi, lo = split(p_ref[(h // 2) % 2, 2 * (h // 4) + h % 2])
            wide[h, :, 0:HS] = hi
            wide[h, :, HS:] = lo

    squares = jnp.zeros((CH, HS), F32)
    for h in range(H):
        both = dot(q_ref[h], wide[h])
        x = att_ref[h] + (both[:, :HS] + both[:, HS:]) * ec_ref[:, h : h + 1]
        field[h] = x
        squares = squares + x * x
    mean = jnp.sum(squares, axis=1, keepdims=True) / (H * HS)
    scale = jnp.broadcast_to(lax.rsqrt(mean + 1e-06), (CH, HS))
    for h in range(H):
        stage[pl.ds(h, CH, stride=H), :] = field[h] * scale
    out_ref[...] = stage[...].reshape(CH, H, HS).astype(BF16)


def finish(att, qh, states, ec):
    return pl.pallas_call(
        finish_kernel,
        name="finish",
        grid=(T // CH,),
        out_shape=jax.ShapeDtypeStruct((T, H, HS), BF16),
        in_specs=[
            pl.BlockSpec((H, CH, HS), lambda i: (0, i, 0)),
            pl.BlockSpec((H, CH, HS), lambda i: (0, i, 0)),
            pl.BlockSpec((2, 16, HS, HS), lambda i: (0, 0, 0, 0)),
            pl.BlockSpec((CH, HS), lambda i: (i, 0)),
        ],
        out_specs=pl.BlockSpec((CH, H, HS), lambda i: (i, 0, 0)),
        scratch_shapes=[
            pltpu.VMEM((H, HS, 2 * HS), BF16),
            pltpu.VMEM((H, CH, HS), F32),
            pltpu.VMEM((CH * H, HS), F32),
        ],
        compiler_params=pltpu.CompilerParams(vmem_limit_bytes=VMEM_LIMIT),
    )(att, qh, states, ec)


def decode_kernel(
    slot_ref, cache_in, hand_ref, q_ref, k_ref, v_ref, gate_ref, decay_ref, gain_ref,
    cache_ref, z_ref, rows,
):
    cache_ref[...] = cache_in[...]
    for p in range(8):
        cache_ref[slot_ref[p]] = hand_ref[p]
    lane = lax.broadcasted_iota(jnp.int32, (16, 64), 1)
    pick = lax.broadcasted_iota(jnp.int32, (8, 64), 1)
    scale = jnp.exp(decay_ref[...])

    def one(s, ys):
        here = lane == s
        q, k = q_ref[s].astype(F32), k_ref[s].astype(F32)
        factor = jnp.sum(jnp.where(pick == s, scale, 0.0), axis=1, keepdims=True)
        ys = list(ys)
        for h in range(2):
            state = cache_ref[s, h]
            for i in range(4):
                value = jnp.sum(jnp.where(here, v_ref[i, h].astype(F32), 0.0), axis=1, keepdims=True)
                state = factor[2 * i + h : 2 * i + h + 1] * state + value * k[i, h : h + 1, :]
                y = jnp.sum(state * q[i, h : h + 1, :], axis=1, keepdims=True)
                ys[2 * i + h] = jnp.where(here, y, ys[2 * i + h])
            cache_ref[s, h] = state
        return tuple(ys)

    ys = lax.fori_loop(0, 64, one, tuple(jnp.zeros((16, 64), F32) for _ in range(8)), unroll=2)
    for i in range(4):
        squares = jnp.zeros((1, 64), F32)
        parts = []
        for h in range(2):
            y = ys[2 * i + h]
            squares = squares + jnp.sum(y * y, axis=0, keepdims=True)
            parts.append(y * gain_ref[h] * jax.nn.sigmoid(gate_ref[i, h].astype(F32)))
        parts.append(jnp.broadcast_to(squares, (8, 64)))
        parts.append(jnp.zeros((HS - 40, 64), F32))
        rows[pl.ds(i, 64, stride=4), :] = jnp.concatenate(parts, axis=0).T
    z_ref[...] = rows[...].T[:40]


def decode(slot, cache, hand, q, k, v, gate, decay, gain):
    vmem = pl.BlockSpec(memory_space=pltpu.VMEM)
    return pl.pallas_call(
        decode_kernel,
        name="decode",
        out_shape=(
            jax.ShapeDtypeStruct((64, 2, 16, HS), F32),
            jax.ShapeDtypeStruct((40, 256), F32),
        ),
        in_specs=[pl.BlockSpec(memory_space=pltpu.SMEM)] + [vmem] * 8,
        out_specs=(vmem, vmem),
        scratch_shapes=[pltpu.VMEM((256, HS), F32)],
        compiler_params=pltpu.CompilerParams(vmem_limit_bytes=VMEM_LIMIT),
    )(slot, cache, hand, q, k, v, gate, decay, gain)


def project_kernel(z_ref, w_ref, out_ref, zbuf, part, take, done, last, s1, r1, s2, r2, s3, r3):
    c, g = lax.axis_index("ctx"), lax.axis_index("grp")
    bar = pltpu.get_barrier_semaphore()

    def greet_grp(d, _):
        pl.semaphore_signal(bar, inc=1, device_id=(c, lax.rem(g + d, 8)), device_id_type=MESH)
        return 0

    def greet_ctx(d, _):
        pl.semaphore_signal(bar, inc=1, device_id=(lax.rem(c + d, 16), g), device_id_type=MESH)
        return 0

    lax.fori_loop(1, 8, greet_grp, 0)
    lax.fori_loop(1, 16, greet_ctx, 0)
    pl.semaphore_wait(bar, 22)

    def copy_1(to):
        return remote(z_ref, zbuf.at[g], s1.at[to], r1.at[g], (c, to))

    def arrival_1(frm):
        return remote(z_ref, zbuf.at[frm], s1.at[frm], r1.at[frm], (c, frm))

    def send_1(d, _):
        copy_1(lax.rem(g + d, 8)).start()
        return 0

    lax.fori_loop(1, 8, send_1, 0)
    zbuf[g] = z_ref[...]

    def wait_1(d, _):
        arrival_1(lax.rem(g + d, 8)).wait_recv()
        return 0

    lax.fori_loop(1, 8, wait_1, 0)

    z = jnp.concatenate([zbuf[n, 0:32, :] for n in range(8)], axis=0).T
    squares = zbuf[0, 32:40, :]
    for n in range(1, 8):
        squares = squares + zbuf[n, 32:40, :]
    squares = jnp.concatenate([squares] * 16, axis=0).T
    hi, lo = split(z)
    for n in range(3):
        span = slice(n * 256, (n + 1) * 256)
        w = w_ref[:, span]
        part[:, :, span] = (dot(hi, w) + dot(lo, w)).reshape(16, 16, 256)
    part[:, :, 768:896] = squares.reshape(16, 16, HS)

    def copy_2(to):
        return remote(part.at[to], take.at[c], s2.at[to], r2.at[c], (to, g))

    def arrival_2(frm):
        return remote(part.at[frm], take.at[frm], s2.at[frm], r2.at[frm], (frm, g))

    def send_2(d, _):
        copy_2(lax.rem(c + d, 16)).start()
        return 0

    lax.fori_loop(1, 16, send_2, 0)
    take[c] = part[c]

    def wait_2(d, _):
        arrival_2(lax.rem(c + d, 16)).wait_recv()
        return 0

    lax.fori_loop(1, 16, wait_2, 0)
    total = take[0]
    for n in range(1, 16):
        total = total + take[n]
    scale = lax.rsqrt(total[:, 768:769] / (H * HS) + 1e-06)
    total = total[:, :768] * scale
    for n in range(8):
        done[n] = total[2 * n : 2 * n + 2]

    def copy_3(to):
        return remote(done.at[to], last.at[g], s3.at[to], r3.at[g], (c, to))

    def arrival_3(frm):
        return remote(done.at[frm], last.at[frm], s3.at[frm], r3.at[frm], (c, frm))

    def send_3(d, _):
        copy_3(lax.rem(g + d, 8)).start()
        return 0

    lax.fori_loop(1, 8, send_3, 0)
    last[g] = done[g]

    def wait_3(d, _):
        arrival_3(lax.rem(g + d, 8)).wait_recv()
        return 0

    lax.fori_loop(1, 8, wait_3, 0)
    for n in range(8):
        out_ref[:, n * 768 : (n + 1) * 768] = last[n]

    def end_grp(d, _):
        to = lax.rem(g + d, 8)
        copy_1(to).wait_send()
        copy_3(to).wait_send()
        return 0

    def end_ctx(d, _):
        copy_2(lax.rem(c + d, 16)).wait_send()
        return 0

    lax.fori_loop(1, 8, end_grp, 0)
    lax.fori_loop(1, 16, end_ctx, 0)


def project(z, weight):
    dma = pltpu.SemaphoreType.DMA
    vmem = pl.BlockSpec(memory_space=pltpu.VMEM)
    return pl.pallas_call(
        project_kernel,
        name="project",
        out_shape=jax.ShapeDtypeStruct((2, 6144), F32),
        in_specs=[vmem, vmem],
        out_specs=vmem,
        scratch_shapes=[
            pltpu.VMEM((8, 40, 256), F32),
            pltpu.VMEM((16, 16, 896), F32),
            pltpu.VMEM((16, 16, 896), F32),
            pltpu.VMEM((8, 2, 768), F32),
            pltpu.VMEM((8, 2, 768), F32),
            dma((8,)), dma((8,)), dma((16,)), dma((16,)), dma((8,)), dma((8,)),
        ],
        compiler_params=pltpu.CompilerParams(
            collective_id=1, has_side_effects=True, vmem_limit_bytes=VMEM_LIMIT
        ),
    )(z, weight)


def per_device(
    queries, keys, values, prefill_decay, start_states, resident_states, slot_of_prompt,
    decode_queries, decode_keys, decode_values, decode_gate, decode_decay, norm_gain, out_weight,
):
    att, qh, states, hand, weight, ec = prefill(
        queries[0],
        keys[0],
        values[0],
        jnp.swapaxes(prefill_decay[0], 0, 1),
        start_states[0],
        out_weight.reshape(32, 6144),
    )
    cache, z = decode(
        slot_of_prompt,
        jnp.swapaxes(resident_states, 2, 3),
        hand,
        decode_queries,
        decode_keys,
        jnp.transpose(decode_values, (1, 2, 3, 0)),
        jnp.transpose(decode_gate, (1, 2, 3, 0)),
        jnp.transpose(decode_decay, (1, 2, 0)).reshape(8, 64),
        norm_gain[:, :, None],
    )
    decoded = project(z, weight)
    prefill_out = finish(att, qh, states, ec)
    return prefill_out[None], jnp.swapaxes(cache, 2, 3), decoded


def solution(mesh):
    return jax.shard_map(
        per_device,
        mesh=mesh,
        in_specs=(
            P("grp", "ctx", None, None),
            P("grp", "ctx", None, None),
            P("grp", "ctx", None, None),
            P("grp", "ctx", None),
            P("grp", "ctx", None, None),
            P(None, "ctx", None, "grp"),
            P(),
            P(None, None, "ctx", None),
            P(None, None, "ctx", None),
            P(None, None, "ctx", "grp"),
            P(None, None, "ctx", "grp"),
            P(None, None, "ctx"),
            P("ctx", "grp"),
            P("ctx", "grp", None),
        ),
        out_specs=(
            P("grp", "ctx", None, None),
            P(None, "ctx", None, "grp"),
            P(("ctx", "grp"), None),
        ),
        check_vma=False,
    )
```

```python
import jax
import jax.numpy as jnp
from jax import lax
from jax.experimental import pallas as pl
from jax.experimental.pallas import tpu as pltpu
from jax.sharding import PartitionSpec as P

H = 32
HS = 128
LOG2E = 1.4426950408889634
MESH = pl.DeviceIdType.MESH
F32 = jnp.float32
BF16 = jnp.bfloat16
VMEM_LIMIT = 60 * 1024 * 1024
T = 512
CH = 128
ROWS = 136
FIRST_HEADS = 28
UNROLL = 4


def dot(a, b):
    return lax.dot_general(a, b, (((1,), (0,)), ((), ())), preferred_element_type=F32)


def split(x):
    hi = x.astype(BF16)
    return hi, (x - hi.astype(F32)).astype(BF16)


def head_of(half, i):
    return 4 * lax.div(i, 2) + 2 * half + lax.rem(i, 2)


def remote(src, dst, send, recv, where):
    return pltpu.make_async_remote_copy(
        src_ref=src, dst_ref=dst, send_sem=send, recv_sem=recv, device_id=where, device_id_type=MESH
    )


def prefill_kernel(
    q_hbm, k_hbm, v_hbm, dec_ref, start_ref, w_ref,
    att_hbm, qh_hbm, p_ref, hand_ref, wt_ref, ec_ref,
    raw, qh, kt, vh, cum2, cum, s_ref, xbuf, tbuf, rbuf, pbuf, qbuf, obuf, pcur, fbuf, hbuf, wf, wr, att,
    load_sem, q_sem, att_sem, sa, ra, s1, r1, s2, r2, sb, rb, sh, rh, sw, rw,
):
    c, g = lax.axis_index("ctx"), lax.axis_index("grp")
    core, chip = lax.rem(c, 2), lax.div(c, 2)
    other = 1 - core
    partner = (2 * chip + other, g)

    def peer(j):
        return (2 * j + core, g)

    x, own_row = lax.rem(chip, 4), lax.div(chip, 4)
    rows = (1 - own_row, own_row)

    def load(which, hbm, row):
        heads = pl.ds(pl.multiple_of(16 * row, 16), 16)
        return pltpu.make_async_copy(hbm.at[:, heads], raw.at[which, row], load_sem.at[which, row])

    for row in rows:
        load(0, k_hbm, row).start()
        load(1, v_hbm, row).start()
    for row in rows:
        load(2, q_hbm, row).start()

    bar = pltpu.get_barrier_semaphore()
    pl.semaphore_signal(bar, inc=1, device_id=partner, device_id_type=MESH)

    def greet(d, _):
        pl.semaphore_signal(bar, inc=1, device_id=peer(lax.rem(chip + d, 8)), device_id_type=MESH)
        pl.semaphore_signal(bar, inc=1, device_id=(c, lax.rem(g + d, 8)), device_id_type=MESH)
        return 0

    lax.fori_loop(1, 8, greet, 0)

    lane = lax.broadcasted_iota(jnp.int32, (H, T), 1)
    total = dec_ref[...]
    step = 1
    while step < T:
        total = total + jnp.where(lane >= step, pltpu.roll(total, step, 1), 0.0)
        step *= 2
    cum[...] = total
    cum2[...] = total * LOG2E
    ec_ref[...] = jnp.concatenate([jnp.exp(total), jnp.zeros((HS - H, T), F32)], axis=0).T

    def heads_first(which, row, at):
        return jnp.swapaxes(raw[which, row, pl.ds(at * CH, CH)], 0, 1)

    def relay_kv(row):
        load(0, k_hbm, row).wait()
        load(1, v_hbm, row).wait()

        def chunk(at, _):
            span = pl.ds(pl.multiple_of(at * CH, CH), CH)
            vh[pl.ds(16 * row, 16), span, :] = heads_first(1, row, at)
            block = heads_first(0, row, at)
            for h in range(16):
                kt[16 * row + h, :, span] = block[h].T
            return 0

        lax.fori_loop(0, T // CH, chunk, 0)

    def local_state(half, i):
        h = head_of(half, i)
        row = cum[pl.ds(h, 1), :]
        end = row[:, T - 1 : T]
        hi, lo = split(kt[h].astype(F32) * jnp.exp(end - row))
        both = dot(jnp.concatenate([hi, lo], axis=0), vh[h])
        s_ref[half, i, 0:HS, :] = both[:HS] + both[HS:]
        s_ref[half, i, HS:ROWS, :] = jnp.broadcast_to(end, (ROWS - HS, HS))

    def copy_a(row):
        part = pl.ds(8 * row, 8)
        return remote(s_ref.at[other, part], xbuf.at[part], sa.at[row], ra.at[row], partner)

    for row in rows:
        relay_kv(row)
        for i in range(8):
            local_state(other, 8 * row + i)
        if row is rows[0]:
            pl.semaphore_wait(bar, 15)
        copy_a(row).start()
        for i in range(8):
            local_state(core, 8 * row + i)

    def copy_1(j):
        return remote(tbuf.at[j], rbuf.at[chip], s1.at[j], r1.at[chip], peer(j))

    def arrival_1(j):
        return remote(tbuf.at[j], rbuf.at[j], s1.at[j], r1.at[j], peer(j))

    def chip_total(j):
        for r in range(2):
            i = 2 * j + r
            mine, theirs = s_ref[core, i], xbuf[i]
            end_mine, end_theirs = mine[HS : HS + 1], theirs[HS : HS + 1]
            on_mine = jnp.where(core == 0, jnp.exp(end_theirs), 1.0)
            on_theirs = jnp.where(core == 0, 1.0, jnp.exp(end_mine))
            tbuf[j, r, 0:HS, :] = on_mine * mine[:HS] + on_theirs * theirs[:HS]
            tbuf[j, r, HS:ROWS, :] = mine[HS:] + theirs[HS:]

    def send_total(row):
        def one(d, _):
            j = 4 * row + lax.rem(x + d, 4)
            chip_total(j)
            copy_1(j).start()
            return 0

        return one

    copy_a(rows[0]).wait_recv()
    lax.fori_loop(0, 4, send_total(rows[0]), 0)
    copy_a(rows[1]).wait_recv()
    lax.fori_loop(1, 4, send_total(rows[1]), 0)
    chip_total(chip)
    rbuf[chip] = tbuf[chip]

    for to in range(8):
        wf[to] = w_ref[:, to * 768 : (to + 1) * 768].astype(F32)

    def copy_w(to):
        return remote(wf.at[to], wr.at[g], sw.at[to], rw.at[g], (c, to))

    def arrival_w(frm):
        return remote(wf.at[frm], wr.at[frm], sw.at[frm], rw.at[frm], (c, frm))

    def send_w(d, _):
        copy_w(lax.rem(g + d, 8)).start()
        return 0

    lax.fori_loop(1, 8, send_w, 0)
    wr[g] = wf[g]

    for row in rows:
        load(2, q_hbm, row).wait()

        def relay_q(at, _):
            span = pl.ds(pl.multiple_of(at * CH, CH), CH)
            qh[pl.ds(16 * row, 16), span, :] = heads_first(2, row, at)
            return 0

        lax.fori_loop(0, T // CH, relay_q, 0)
    qh_copy = pltpu.make_async_copy(qh, qh_hbm, q_sem)
    qh_copy.start()

    causal = lax.broadcasted_iota(jnp.int32, (HS, HS), 0) >= lax.broadcasted_iota(jnp.int32, (HS, HS), 1)

    def att_copy(n):
        part = pl.ds(UNROLL * n, UNROLL)
        return pltpu.make_async_copy(att.at[part], att_hbm.at[part], att_sem.at[n])

    def attend(h):
        row = cum2[pl.ds(h, 1), :]
        col = jnp.broadcast_to(row, (HS, T)).T
        left = dot(qh[h], kt[h, :, 0:256])
        right = dot(qh[h, 256:512, :], kt[h, :, 256:512])

        def weigh(a, b):
            scores = left if b < 2 else right
            first = a if b < 2 else a - 2
            part = scores[first * HS : (first + 1) * HS, (b % 2) * HS : (b % 2 + 1) * HS]
            diff = col[a * HS : (a + 1) * HS] - row[:, b * HS : (b + 1) * HS]
            if a == b:
                diff = jnp.where(causal, diff, -1e30)
            return (part * jnp.exp2(diff)).astype(BF16)

        v = vh[h]
        none = jnp.zeros((HS, HS), BF16)
        top = jnp.concatenate([
            jnp.concatenate([weigh(0, 0), none], axis=1),
            jnp.concatenate([weigh(1, 0), weigh(1, 1)], axis=1),
        ], axis=0)
        low = jnp.concatenate([
            jnp.concatenate([weigh(2, 0), weigh(2, 1), weigh(2, 2), none], axis=1),
            jnp.concatenate([weigh(3, 0), weigh(3, 1), weigh(3, 2), weigh(3, 3)], axis=1),
        ], axis=0)
        att[h, 0:256, :] = dot(top, v[0:256])
        att[h, 256:512, :] = dot(low, v)

    def some(n, _):
        for u in range(UNROLL):
            attend(UNROLL * n + u)
        att_copy(n).start()
        return 0

    lax.fori_loop(0, FIRST_HEADS // UNROLL, some, 0)

    def copy_2(j):
        return remote(pbuf.at[j], qbuf.at[chip], s2.at[j], r2.at[chip], peer(j))

    def arrival_2(j):
        return remote(pbuf.at[j], qbuf.at[j], s2.at[j], r2.at[j], peer(j))

    pcur[...] = start_ref[...]

    def scan(j, _):
        pbuf[j] = pcur[...]

        @pl.when(j != chip)
        def _():
            copy_2(j).start()
            arrival_1(j).wait_recv()

        for r in range(2):
            pcur[r] = jnp.exp(rbuf[j, r, HS : HS + 1, :]) * pcur[r] + rbuf[j, r, 0:HS, :]
        return 0

    lax.fori_loop(0, 8, scan, 0)
    qbuf[chip] = pbuf[chip]

    for r in range(2):
        fbuf[:, r] = pcur[r].T.reshape(8, 16, HS)

    def copy_h(to):
        return remote(fbuf.at[to], hbuf.at[g], sh.at[to], rh.at[g], (c, to))

    def arrival_h(frm):
        return remote(fbuf.at[frm], hbuf.at[frm], sh.at[frm], rh.at[frm], (c, frm))

    def send_h(d, _):
        copy_h(lax.rem(g + d, 8)).start()
        return 0

    lax.fori_loop(1, 8, send_h, 0)
    hbuf[g] = fbuf[g]

    lax.fori_loop(FIRST_HEADS // UNROLL, H // UNROLL, some, 0)

    def copy_b(m):
        return remote(obuf.at[pl.ds(4 * m, 4)], p_ref.at[core, pl.ds(4 * m, 4)], sb.at[m], rb.at[m], partner)

    def arrival_b(m):
        return remote(obuf.at[pl.ds(4 * m, 4)], p_ref.at[other, pl.ds(4 * m, 4)], sb.at[m], rb.at[m], partner)

    def spread(m, _):
        for n in range(2):
            j = 2 * m + n

            @pl.when(j != chip)
            def _():
                arrival_2(j).wait_recv()

            for r in range(2):
                i = 2 * j + r
                before = qbuf[j, r]
                first = jnp.where(core == 0, s_ref[core, i], xbuf[i])
                after = jnp.exp(first[HS : HS + 1]) * before + first[:HS]
                p_ref[core, i] = jnp.where(core == 0, before, after)
                obuf[i] = jnp.where(core == 0, after, before)
        copy_b(m).start()
        return 0

    lax.fori_loop(0, 4, spread, 0)

    def take_w(d, _):
        frm = lax.rem(g + d, 8)
        arrival_w(frm).wait_recv()
        arrival_h(frm).wait_recv()
        return 0

    lax.fori_loop(1, 8, take_w, 0)
    for frm in range(8):
        wt_ref[frm * 32 : (frm + 1) * 32, :] = wr[frm].astype(BF16)
    hand_ref[...] = hbuf[...]

    for n in range(H // UNROLL):
        att_copy(n).wait()
    qh_copy.wait()

    def finish_pair(m, _):
        arrival_b(m).wait_recv()
        copy_b(m).wait_send()
        return 0

    lax.fori_loop(0, 4, finish_pair, 0)
    for row in rows:
        copy_a(row).wait_send()

    def finish(d, _):
        j = lax.rem(chip + d, 8)
        copy_1(j).wait_send()
        copy_2(j).wait_send()
        to = lax.rem(g + d, 8)
        copy_w(to).wait_send()
        copy_h(to).wait_send()
        return 0

    lax.fori_loop(1, 8, finish, 0)


def prefill(q, k, v, decay, start, weight):
    dma = pltpu.SemaphoreType.DMA
    anywhere = pl.BlockSpec(memory_space=pl.ANY)
    vmem = pl.BlockSpec(memory_space=pltpu.VMEM)
    return pl.pallas_call(
        prefill_kernel,
        name="prefill",
        out_shape=(
            jax.ShapeDtypeStruct((H, T, HS), F32),
            jax.ShapeDtypeStruct((H, T, HS), BF16),
            jax.ShapeDtypeStruct((2, 16, HS, HS), F32),
            jax.ShapeDtypeStruct((8, 2, 16, HS), F32),
            jax.ShapeDtypeStruct((256, 768), BF16),
            jax.ShapeDtypeStruct((T, HS), F32),
        ),
        in_specs=[anywhere, anywhere, anywhere, vmem, vmem, vmem],
        out_specs=(anywhere, anywhere, vmem, vmem, vmem, vmem),
        scratch_shapes=[
            pltpu.VMEM((3, 2, T, 16, HS), BF16),
            pltpu.VMEM((H, T, HS), BF16),
            pltpu.VMEM((H, HS, T), BF16),
            pltpu.VMEM((H, T, HS), BF16),
            pltpu.VMEM((H, T), F32),
            pltpu.VMEM((H, T), F32),
            pltpu.VMEM((2, 16, ROWS, HS), F32),
            pltpu.VMEM((16, ROWS, HS), F32),
            pltpu.VMEM((8, 2, ROWS, HS), F32),
            pltpu.VMEM((8, 2, ROWS, HS), F32),
            pltpu.VMEM((8, 2, HS, HS), F32),
            pltpu.VMEM((8, 2, HS, HS), F32),
            pltpu.VMEM((16, HS, HS), F32),
            pltpu.VMEM((2, HS, HS), F32),
            pltpu.VMEM((8, 2, 16, HS), F32),
            pltpu.VMEM((8, 2, 16, HS), F32),
            pltpu.VMEM((8, 32, 768), F32),
            pltpu.VMEM((8, 32, 768), F32),
            pltpu.VMEM((H, T, HS), F32),
            dma((3, 2)), dma, dma((H // UNROLL,)),
            dma((2,)), dma((2,)), dma((8,)), dma((8,)), dma((8,)), dma((8,)),
            dma((4,)), dma((4,)), dma((8,)), dma((8,)), dma((8,)), dma((8,)),
        ],
        compiler_params=pltpu.CompilerParams(
            collective_id=0, has_side_effects=True, vmem_limit_bytes=VMEM_LIMIT
        ),
    )(q, k, v, decay, start, weight)


def finish_kernel(att_ref, q_ref, p_ref, ec_ref, out_ref, wide, field):
    @pl.when(pl.program_id(0) == 0)
    def _():
        for h in range(H):
            hi, lo = split(p_ref[(h // 2) % 2, 2 * (h // 4) + h % 2])
            wide[h, :, 0:HS] = hi
            wide[h, :, HS:] = lo

    squares = jnp.zeros((CH, HS), F32)
    for h in range(H):
        both = dot(q_ref[h], wide[h])
        x = att_ref[h] + (both[:, :HS] + both[:, HS:]) * ec_ref[:, h : h + 1]
        field[h] = x
        squares = squares + x * x
    mean = jnp.sum(squares, axis=1, keepdims=True) / (H * HS)
    scale = jnp.broadcast_to(lax.rsqrt(mean + 1e-06), (CH, HS))
    out_ref[...] = jnp.swapaxes((field[...] * scale[None]).astype(BF16), 0, 1)


def finish(att, qh, states, ec):
    return pl.pallas_call(
        finish_kernel,
        name="finish",
        grid=(T // CH,),
        out_shape=jax.ShapeDtypeStruct((T, H, HS), BF16),
        in_specs=[
            pl.BlockSpec((H, CH, HS), lambda i: (0, i, 0)),
            pl.BlockSpec((H, CH, HS), lambda i: (0, i, 0)),
            pl.BlockSpec((2, 16, HS, HS), lambda i: (0, 0, 0, 0)),
            pl.BlockSpec((CH, HS), lambda i: (i, 0)),
        ],
        out_specs=pl.BlockSpec((CH, H, HS), lambda i: (i, 0, 0)),
        scratch_shapes=[
            pltpu.VMEM((H, HS, 2 * HS), BF16),
            pltpu.VMEM((H, CH, HS), F32),
        ],
        compiler_params=pltpu.CompilerParams(vmem_limit_bytes=VMEM_LIMIT),
    )(att, qh, states, ec)


def decode_kernel(
    slot_ref, cache_in, hand_ref, q_ref, k_ref, v_ref, gate_ref, decay_ref, gain_ref,
    cache_ref, z_ref, rows,
):
    cache_ref[...] = cache_in[...]
    for p in range(8):
        cache_ref[slot_ref[p]] = hand_ref[p]
    lane = lax.broadcasted_iota(jnp.int32, (16, 64), 1)
    pick = lax.broadcasted_iota(jnp.int32, (8, 64), 1)
    scale = jnp.exp(decay_ref[...])

    def one(s, ys):
        here = lane == s
        q, k = q_ref[s].astype(F32), k_ref[s].astype(F32)
        factor = jnp.sum(jnp.where(pick == s, scale, 0.0), axis=1, keepdims=True)
        ys = list(ys)
        for h in range(2):
            state = cache_ref[s, h]
            for i in range(4):
                value = jnp.sum(jnp.where(here, v_ref[i, h].astype(F32), 0.0), axis=1, keepdims=True)
                state = factor[2 * i + h : 2 * i + h + 1] * state + value * k[i, h : h + 1, :]
                y = jnp.sum(state * q[i, h : h + 1, :], axis=1, keepdims=True)
                ys[2 * i + h] = jnp.where(here, y, ys[2 * i + h])
            cache_ref[s, h] = state
        return tuple(ys)

    ys = lax.fori_loop(0, 64, one, tuple(jnp.zeros((16, 64), F32) for _ in range(8)), unroll=2)
    for i in range(4):
        squares = jnp.zeros((1, 64), F32)
        parts = []
        for h in range(2):
            y = ys[2 * i + h]
            squares = squares + jnp.sum(y * y, axis=0, keepdims=True)
            parts.append(y * gain_ref[h] * jax.nn.sigmoid(gate_ref[i, h].astype(F32)))
        parts.append(jnp.broadcast_to(squares, (8, 64)))
        parts.append(jnp.zeros((HS - 40, 64), F32))
        rows[pl.ds(i, 64, stride=4), :] = jnp.concatenate(parts, axis=0).T
    z_ref[...] = rows[...].T[:40]


def decode(slot, cache, hand, q, k, v, gate, decay, gain):
    vmem = pl.BlockSpec(memory_space=pltpu.VMEM)
    return pl.pallas_call(
        decode_kernel,
        name="decode",
        out_shape=(
            jax.ShapeDtypeStruct((64, 2, 16, HS), F32),
            jax.ShapeDtypeStruct((40, 256), F32),
        ),
        in_specs=[pl.BlockSpec(memory_space=pltpu.SMEM)] + [vmem] * 8,
        out_specs=(vmem, vmem),
        scratch_shapes=[pltpu.VMEM((256, HS), F32)],
        compiler_params=pltpu.CompilerParams(vmem_limit_bytes=VMEM_LIMIT),
    )(slot, cache, hand, q, k, v, gate, decay, gain)


def project_kernel(z_ref, w_ref, out_ref, zbuf, part, half, take, done, last, s1, r1, sa, ra, s2, r2, s3, r3):
    c, g = lax.axis_index("ctx"), lax.axis_index("grp")
    core, chip = lax.rem(c, 2), lax.div(c, 2)
    partner = (2 * chip + 1 - core, g)

    def peer(j):
        return (2 * j + core, g)

    bar = pltpu.get_barrier_semaphore()

    def greet_grp(d, _):
        pl.semaphore_signal(bar, inc=1, device_id=(c, lax.rem(g + d, 8)), device_id_type=MESH)
        return 0

    def greet_ctx(d, _):
        pl.semaphore_signal(bar, inc=1, device_id=peer(lax.rem(chip + d, 8)), device_id_type=MESH)
        return 0

    lax.fori_loop(1, 8, greet_grp, 0)
    lax.fori_loop(1, 8, greet_ctx, 0)
    pl.semaphore_signal(bar, inc=1, device_id=partner, device_id_type=MESH)
    pl.semaphore_wait(bar, 15)

    def copy_1(to):
        return remote(z_ref, zbuf.at[g], s1.at[to], r1.at[g], (c, to))

    def arrival_1(frm):
        return remote(z_ref, zbuf.at[frm], s1.at[frm], r1.at[frm], (c, frm))

    def send_1(d, _):
        copy_1(lax.rem(g + d, 8)).start()
        return 0

    lax.fori_loop(1, 8, send_1, 0)
    zbuf[g] = z_ref[...]

    def wait_1(d, _):
        arrival_1(lax.rem(g + d, 8)).wait_recv()
        return 0

    lax.fori_loop(1, 8, wait_1, 0)

    z = jnp.concatenate([zbuf[n, 0:32, :] for n in range(8)], axis=0).T
    squares = zbuf[0, 32:40, :]
    for n in range(1, 8):
        squares = squares + zbuf[n, 32:40, :]
    squares = jnp.concatenate([squares] * 16, axis=0).T
    hi, lo = split(z)
    for n in range(3):
        span = slice(n * 256, (n + 1) * 256)
        w = w_ref[:, span]
        both = (dot(hi, w) + dot(lo, w)).reshape(8, 2, 16, 256)
        for k in range(2):
            part[k, :, :, span] = both[:, k]
    both = squares.reshape(8, 2, 16, HS)
    for k in range(2):
        part[k, :, :, 768:896] = both[:, k]

    copy_a = remote(part.at[1 - core], half, sa, ra, partner)
    copy_a.start()
    copy_a.wait_recv()
    half[...] = half[...] + part[core]

    def copy_2(to):
        return remote(half.at[to], take.at[chip], s2.at[to], r2.at[chip], peer(to))

    def arrival_2(frm):
        return remote(half.at[frm], take.at[frm], s2.at[frm], r2.at[frm], peer(frm))

    def send_2(d, _):
        copy_2(lax.rem(chip + d, 8)).start()
        return 0

    lax.fori_loop(1, 8, send_2, 0)
    take[chip] = half[chip]

    def wait_2(d, _):
        arrival_2(lax.rem(chip + d, 8)).wait_recv()
        return 0

    lax.fori_loop(1, 8, wait_2, 0)
    total = take[0]
    for n in range(1, 8):
        total = total + take[n]
    scale = lax.rsqrt(total[:, 768:769] / (H * HS) + 1e-06)
    total = total[:, :768] * scale
    for n in range(8):
        done[n] = total[2 * n : 2 * n + 2]

    def copy_3(to):
        return remote(done.at[to], last.at[g], s3.at[to], r3.at[g], (c, to))

    def arrival_3(frm):
        return remote(done.at[frm], last.at[frm], s3.at[frm], r3.at[frm], (c, frm))

    def send_3(d, _):
        copy_3(lax.rem(g + d, 8)).start()
        return 0

    lax.fori_loop(1, 8, send_3, 0)
    last[g] = done[g]

    def wait_3(d, _):
        arrival_3(lax.rem(g + d, 8)).wait_recv()
        return 0

    lax.fori_loop(1, 8, wait_3, 0)
    for n in range(8):
        out_ref[:, n * 768 : (n + 1) * 768] = last[n]

    def end_grp(d, _):
        to = lax.rem(g + d, 8)
        copy_1(to).wait_send()
        copy_3(to).wait_send()
        return 0

    def end_ctx(d, _):
        copy_2(lax.rem(chip + d, 8)).wait_send()
        return 0

    lax.fori_loop(1, 8, end_grp, 0)
    lax.fori_loop(1, 8, end_ctx, 0)
    copy_a.wait_send()


def project(z, weight):
    dma = pltpu.SemaphoreType.DMA
    vmem = pl.BlockSpec(memory_space=pltpu.VMEM)
    return pl.pallas_call(
        project_kernel,
        name="project",
        out_shape=jax.ShapeDtypeStruct((2, 6144), F32),
        in_specs=[vmem, vmem],
        out_specs=vmem,
        scratch_shapes=[
            pltpu.VMEM((8, 40, 256), F32),
            pltpu.VMEM((2, 8, 16, 896), F32),
            pltpu.VMEM((8, 16, 896), F32),
            pltpu.VMEM((8, 16, 896), F32),
            pltpu.VMEM((8, 2, 768), F32),
            pltpu.VMEM((8, 2, 768), F32),
            dma((8,)), dma((8,)), dma, dma, dma((8,)), dma((8,)), dma((8,)), dma((8,)),
        ],
        compiler_params=pltpu.CompilerParams(
            collective_id=1, has_side_effects=True, vmem_limit_bytes=VMEM_LIMIT
        ),
    )(z, weight)


def per_device(
    queries, keys, values, prefill_decay, start_states, resident_states, slot_of_prompt,
    decode_queries, decode_keys, decode_values, decode_gate, decode_decay, norm_gain, out_weight,
):
    att, qh, states, hand, weight, ec = prefill(
        queries[0],
        keys[0],
        values[0],
        jnp.swapaxes(prefill_decay[0], 0, 1),
        start_states[0],
        out_weight.reshape(32, 6144),
    )
    cache, z = decode(
        slot_of_prompt,
        jnp.swapaxes(resident_states, 2, 3),
        hand,
        decode_queries,
        decode_keys,
        jnp.transpose(decode_values, (1, 2, 3, 0)),
        jnp.transpose(decode_gate, (1, 2, 3, 0)),
        jnp.transpose(decode_decay, (1, 2, 0)).reshape(8, 64),
        norm_gain[:, :, None],
    )
    decoded = project(z, weight)
    prefill_out = finish(att, qh, states, ec)
    return prefill_out[None], jnp.swapaxes(cache, 2, 3), decoded


def solution(mesh):
    return jax.shard_map(
        per_device,
        mesh=mesh,
        in_specs=(
            P("grp", "ctx", None, None),
            P("grp", "ctx", None, None),
            P("grp", "ctx", None, None),
            P("grp", "ctx", None),
            P("grp", "ctx", None, None),
            P(None, "ctx", None, "grp"),
            P(),
            P(None, None, "ctx", None),
            P(None, None, "ctx", None),
            P(None, None, "ctx", "grp"),
            P(None, None, "ctx", "grp"),
            P(None, None, "ctx"),
            P("ctx", "grp"),
            P("ctx", "grp", None),
        ),
        out_specs=(
            P("grp", "ctx", None, None),
            P(None, "ctx", None, "grp"),
            P(("ctx", "grp"), None),
        ),
        check_vma=False,
    )
```

```python
import jax
import jax.numpy as jnp
from jax import lax
from jax.experimental import pallas as pl
from jax.experimental.pallas import tpu as pltpu
from jax.sharding import PartitionSpec as P

H = 32
HS = 128
LOG2E = 1.4426950408889634
MESH = pl.DeviceIdType.MESH
F32 = jnp.float32
BF16 = jnp.bfloat16
VMEM_LIMIT = 60 * 1024 * 1024
T = 512
CH = 128
ROWS = 136
HEADS_AT_SCAN = 12
HEADS_AT_HAND = 24
UNROLL = 4


def dot(a, b):
    return lax.dot_general(a, b, (((1,), (0,)), ((), ())), preferred_element_type=F32)


def split(x):
    hi = x.astype(BF16)
    return hi, (x - hi.astype(F32)).astype(BF16)


def head_of(half, i):
    return 4 * lax.div(i, 2) + 2 * half + lax.rem(i, 2)


def remote(src, dst, send, recv, where):
    return pltpu.make_async_remote_copy(
        src_ref=src, dst_ref=dst, send_sem=send, recv_sem=recv, device_id=where, device_id_type=MESH
    )


def kernel(
    slot_ref, q_hbm, k_hbm, v_hbm, dec_ref, start_ref, w_ref, cache_hbm, dq_ref, dk_ref, dv_ref, gate_ref, decay_ref, gain_ref,
    out_hbm, new_hbm, decoded_ref,
    raw, qh, kt, vh, cum2, cum, ec, s_ref, xbuf, tbuf, rbuf, pbuf, qbuf, obuf, states, pcur, fbuf, hbuf, wf, wr, wt, att,
    wide, outs, cache, merged, zrow, zmine, zbuf, part, half, take, done, last,
    load_sem, cache_sem, new_sem, out_sem, sa, ra, s1, r1, s2, r2, sb, rb, sh, rh, sw, rw, sz, rz, sc, rc, sp, rp, sd, rd,
):
    c, g = lax.axis_index("ctx"), lax.axis_index("grp")
    core, chip = lax.rem(c, 2), lax.div(c, 2)
    other = 1 - core
    partner = (2 * chip + other, g)

    def peer(j):
        return (2 * j + core, g)

    x, own_row = lax.rem(chip, 4), lax.div(chip, 4)
    rows = (1 - own_row, own_row)

    def load(which, hbm, row):
        heads = pl.ds(pl.multiple_of(16 * row, 16), 16)
        return pltpu.make_async_copy(hbm.at[:, heads], raw.at[which, row], load_sem.at[which, row])

    for row in rows:
        load(0, k_hbm, row).start()
        load(1, v_hbm, row).start()
    for row in rows:
        load(2, q_hbm, row).start()
    cache_load = pltpu.make_async_copy(cache_hbm, cache.at[pl.ds(0, 64)], cache_sem)
    cache_load.start()

    bar = pltpu.get_barrier_semaphore()
    pl.semaphore_signal(bar, inc=1, device_id=partner, device_id_type=MESH)

    def greet(d, _):
        pl.semaphore_signal(bar, inc=1, device_id=peer(lax.rem(chip + d, 8)), device_id_type=MESH)
        pl.semaphore_signal(bar, inc=1, device_id=(c, lax.rem(g + d, 8)), device_id_type=MESH)
        return 0

    lax.fori_loop(1, 8, greet, 0)

    lane = lax.broadcasted_iota(jnp.int32, (H, T), 1)
    total = dec_ref[...]
    step = 1
    while step < T:
        total = total + jnp.where(lane >= step, pltpu.roll(total, step, 1), 0.0)
        step *= 2
    cum[...] = total
    cum2[...] = total * LOG2E
    ec[...] = jnp.concatenate([jnp.exp(total), jnp.zeros((HS - H, T), F32)], axis=0).T

    def heads_first(which, row, at):
        return jnp.swapaxes(raw[which, row, pl.ds(at * CH, CH)], 0, 1)

    def relay_kv(row):
        load(0, k_hbm, row).wait()
        load(1, v_hbm, row).wait()

        def chunk(at, _):
            span = pl.ds(pl.multiple_of(at * CH, CH), CH)
            vh[pl.ds(16 * row, 16), span, :] = heads_first(1, row, at)
            block = heads_first(0, row, at)
            for h in range(16):
                kt[16 * row + h, :, span] = block[h].T
            return 0

        lax.fori_loop(0, T // CH, chunk, 0)

    def local_state(half, i):
        h = head_of(half, i)
        row = cum[pl.ds(h, 1), :]
        end = row[:, T - 1 : T]
        hi, lo = split(kt[h].astype(F32) * jnp.exp(end - row))
        both = dot(jnp.concatenate([hi, lo], axis=0), vh[h])
        s_ref[half, i, 0:HS, :] = both[:HS] + both[HS:]
        s_ref[half, i, HS:ROWS, :] = jnp.broadcast_to(end, (ROWS - HS, HS))

    def copy_a(row):
        part = pl.ds(8 * row, 8)
        return remote(s_ref.at[other, part], xbuf.at[part], sa.at[row], ra.at[row], partner)

    for row in rows:
        relay_kv(row)
        for i in range(8):
            local_state(other, 8 * row + i)
        if row is rows[0]:
            pl.semaphore_wait(bar, 15)
        copy_a(row).start()
        for i in range(8):
            local_state(core, 8 * row + i)

    def copy_1(j):
        return remote(tbuf.at[j], rbuf.at[chip], s1.at[j], r1.at[chip], peer(j))

    def arrival_1(j):
        return remote(tbuf.at[j], rbuf.at[j], s1.at[j], r1.at[j], peer(j))

    def chip_total(j):
        for r in range(2):
            i = 2 * j + r
            mine, theirs = s_ref[core, i], xbuf[i]
            end_mine, end_theirs = mine[HS : HS + 1], theirs[HS : HS + 1]
            on_mine = jnp.where(core == 0, jnp.exp(end_theirs), 1.0)
            on_theirs = jnp.where(core == 0, 1.0, jnp.exp(end_mine))
            tbuf[j, r, 0:HS, :] = on_mine * mine[:HS] + on_theirs * theirs[:HS]
            tbuf[j, r, HS:ROWS, :] = mine[HS:] + theirs[HS:]

    def send_total(row):
        def one(d, _):
            j = 4 * row + lax.rem(x + d, 4)
            chip_total(j)
            copy_1(j).start()
            return 0

        return one

    copy_a(rows[0]).wait_recv()
    lax.fori_loop(0, 4, send_total(rows[0]), 0)
    copy_a(rows[1]).wait_recv()
    lax.fori_loop(1, 4, send_total(rows[1]), 0)
    chip_total(chip)
    rbuf[chip] = tbuf[chip]

    for to in range(8):
        wf[to] = w_ref[:, to * 768 : (to + 1) * 768].astype(F32)

    def copy_w(to):
        return remote(wf.at[to], wr.at[g], sw.at[to], rw.at[g], (c, to))

    def arrival_w(frm):
        return remote(wf.at[frm], wr.at[frm], sw.at[frm], rw.at[frm], (c, frm))

    def send_w(d, _):
        copy_w(lax.rem(g + d, 8)).start()
        return 0

    lax.fori_loop(1, 8, send_w, 0)
    wr[g] = wf[g]

    for row in rows:
        load(2, q_hbm, row).wait()

        def relay_q(at, _):
            span = pl.ds(pl.multiple_of(at * CH, CH), CH)
            qh[pl.ds(16 * row, 16), span, :] = heads_first(2, row, at)
            return 0

        lax.fori_loop(0, T // CH, relay_q, 0)

    lane = lax.broadcasted_iota(jnp.int32, (16, 64), 1)
    pick = lax.broadcasted_iota(jnp.int32, (8, 64), 1)
    scale = jnp.exp(decay_ref[...])

    def decode_row(at, s, ys):
        here = lane == s
        q, k = dq_ref[s].astype(F32), dk_ref[s].astype(F32)
        factor = jnp.sum(jnp.where(pick == s, scale, 0.0), axis=1, keepdims=True)
        ys = list(ys)
        for h in range(2):
            state = cache[at, h]
            for i in range(4):
                value = jnp.sum(jnp.where(here, dv_ref[i, h].astype(F32), 0.0), axis=1, keepdims=True)
                state = factor[2 * i + h : 2 * i + h + 1] * state + value * k[i, h : h + 1, :]
                y = jnp.sum(state * q[i, h : h + 1, :], axis=1, keepdims=True)
                ys[2 * i + h] = jnp.where(here, y, ys[2 * i + h])
            cache[at, h] = state
        return tuple(ys)

    cache_load.wait()
    ys = lax.fori_loop(
        0, 64, lambda s, ys: decode_row(s, s, ys), tuple(jnp.zeros((16, 64), F32) for _ in range(8)), unroll=2
    )

    causal = lax.broadcasted_iota(jnp.int32, (HS, HS), 0) >= lax.broadcasted_iota(jnp.int32, (HS, HS), 1)

    def attend(h):
        row = cum2[pl.ds(h, 1), :]
        col = jnp.broadcast_to(row, (HS, T)).T
        left = dot(qh[h], kt[h, :, 0:256])
        right = dot(qh[h, 256:512, :], kt[h, :, 256:512])

        def weigh(a, b):
            scores = left if b < 2 else right
            first = a if b < 2 else a - 2
            part = scores[first * HS : (first + 1) * HS, (b % 2) * HS : (b % 2 + 1) * HS]
            diff = col[a * HS : (a + 1) * HS] - row[:, b * HS : (b + 1) * HS]
            if a == b:
                diff = jnp.where(causal, diff, -1e30)
            return (part * jnp.exp2(diff)).astype(BF16)

        v = vh[h]
        none = jnp.zeros((HS, HS), BF16)
        top = jnp.concatenate([
            jnp.concatenate([weigh(0, 0), none], axis=1),
            jnp.concatenate([weigh(1, 0), weigh(1, 1)], axis=1),
        ], axis=0)
        low = jnp.concatenate([
            jnp.concatenate([weigh(2, 0), weigh(2, 1), weigh(2, 2), none], axis=1),
            jnp.concatenate([weigh(3, 0), weigh(3, 1), weigh(3, 2), weigh(3, 3)], axis=1),
        ], axis=0)
        att[h, 0:256, :] = dot(top, v[0:256])
        att[h, 256:512, :] = dot(low, v)

    def some(n, _):
        for u in range(UNROLL):
            attend(UNROLL * n + u)
        return 0

    lax.fori_loop(0, HEADS_AT_SCAN // UNROLL, some, 0)

    def copy_2(j):
        return remote(pbuf.at[j], qbuf.at[chip], s2.at[j], r2.at[chip], peer(j))

    def arrival_2(j):
        return remote(pbuf.at[j], qbuf.at[j], s2.at[j], r2.at[j], peer(j))

    pcur[...] = start_ref[...]

    def scan(j, _):
        pbuf[j] = pcur[...]

        @pl.when(j != chip)
        def _():
            copy_2(j).start()
            arrival_1(j).wait_recv()

        for r in range(2):
            pcur[r] = jnp.exp(rbuf[j, r, HS : HS + 1, :]) * pcur[r] + rbuf[j, r, 0:HS, :]
        return 0

    lax.fori_loop(0, 8, scan, 0)
    qbuf[chip] = pbuf[chip]

    for r in range(2):
        fbuf[:, r] = pcur[r].T.reshape(8, 16, HS)

    def copy_h(to):
        return remote(fbuf.at[to], hbuf.at[g], sh.at[to], rh.at[g], (c, to))

    def arrival_h(frm):
        return remote(fbuf.at[frm], hbuf.at[frm], sh.at[frm], rh.at[frm], (c, frm))

    def send_h(d, _):
        copy_h(lax.rem(g + d, 8)).start()
        return 0

    lax.fori_loop(1, 8, send_h, 0)
    hbuf[g] = fbuf[g]

    lax.fori_loop(HEADS_AT_SCAN // UNROLL, HEADS_AT_HAND // UNROLL, some, 0)

    def take_h(d, _):
        frm = lax.rem(g + d, 8)
        arrival_h(frm).wait_recv()
        arrival_w(frm).wait_recv()
        return 0

    lax.fori_loop(1, 8, take_h, 0)
    cache[64:72] = hbuf[...]
    ys = lax.fori_loop(0, 8, lambda p, ys: decode_row(64 + p, slot_ref[p], ys), ys, unroll=2)
    for i in range(4):
        squares = jnp.zeros((1, 64), F32)
        parts = []
        for h in range(2):
            y = ys[2 * i + h]
            squares = squares + jnp.sum(y * y, axis=0, keepdims=True)
            parts.append(y * gain_ref[h] * jax.nn.sigmoid(gate_ref[i, h].astype(F32)))
        parts.append(jnp.broadcast_to(squares, (8, 64)))
        parts.append(jnp.zeros((HS - 40, 64), F32))
        zrow[pl.ds(i, 64, stride=4), :] = jnp.concatenate(parts, axis=0).T
    zmine[...] = zrow[...].T[:40]

    def copy_z(to):
        return remote(zmine, zbuf.at[g], sz.at[to], rz.at[g], (c, to))

    def arrival_z(frm):
        return remote(zmine, zbuf.at[frm], sz.at[frm], rz.at[frm], (c, frm))

    def send_z(d, _):
        copy_z(lax.rem(g + d, 8)).start()
        return 0

    lax.fori_loop(1, 8, send_z, 0)
    zbuf[g] = zmine[...]

    for frm in range(8):
        wt[frm * 32 : (frm + 1) * 32, :] = wr[frm].astype(BF16)
    lax.fori_loop(HEADS_AT_HAND // UNROLL, H // UNROLL, some, 0)

    def wait_z(d, _):
        arrival_z(lax.rem(g + d, 8)).wait_recv()
        return 0

    lax.fori_loop(1, 8, wait_z, 0)
    z = jnp.concatenate([zbuf[n, 0:32, :] for n in range(8)], axis=0).T
    squares = zbuf[0, 32:40, :]
    for n in range(1, 8):
        squares = squares + zbuf[n, 32:40, :]
    squares = jnp.concatenate([squares] * 16, axis=0).T
    hi, lo = split(z)
    for n in range(3):
        span = slice(n * 256, (n + 1) * 256)
        w = wt[:, span]
        both = (dot(hi, w) + dot(lo, w)).reshape(8, 2, 16, 256)
        for k in range(2):
            part[k, :, :, span] = both[:, k]
    both = squares.reshape(8, 2, 16, HS)
    for k in range(2):
        part[k, :, :, 768:896] = both[:, k]
    copy_c = remote(part.at[other], half, sc, rc, partner)
    copy_c.start()

    def copy_b(m):
        return remote(obuf.at[pl.ds(4 * m, 4)], states.at[core, pl.ds(4 * m, 4)], sb.at[m], rb.at[m], partner)

    def arrival_b(m):
        return remote(obuf.at[pl.ds(4 * m, 4)], states.at[other, pl.ds(4 * m, 4)], sb.at[m], rb.at[m], partner)

    def spread(m, _):
        for n in range(2):
            j = 2 * m + n

            @pl.when(j != chip)
            def _():
                arrival_2(j).wait_recv()

            for r in range(2):
                i = 2 * j + r
                before = qbuf[j, r]
                first = jnp.where(core == 0, s_ref[core, i], xbuf[i])
                after = jnp.exp(first[HS : HS + 1]) * before + first[:HS]
                states[core, i] = jnp.where(core == 0, before, after)
                obuf[i] = jnp.where(core == 0, after, before)
        copy_b(m).start()
        return 0

    lax.fori_loop(0, 4, spread, 0)

    copy_c.wait_recv()
    half[...] = half[...] + part[core]

    def copy_p(to):
        return remote(half.at[to], take.at[chip], sp.at[to], rp.at[chip], peer(to))

    def arrival_p(frm):
        return remote(half.at[frm], take.at[frm], sp.at[frm], rp.at[frm], peer(frm))

    def send_p(d, _):
        copy_p(lax.rem(chip + d, 8)).start()
        return 0

    lax.fori_loop(1, 8, send_p, 0)
    take[chip] = half[chip]

    def take_b(m, _):
        arrival_b(m).wait_recv()
        return 0

    lax.fori_loop(0, 4, take_b, 0)
    for h in range(H):
        hi, lo = split(states[(h // 2) % 2, 2 * (h // 4) + h % 2])
        wide[h, :, 0:HS] = hi
        wide[h, :, HS:] = lo

    def out_copy(at, slot):
        return pltpu.make_async_copy(outs.at[slot], out_hbm.at[pl.ds(at * CH, CH)], out_sem.at[slot])

    for at in range(T // CH):
        span = slice(at * CH, (at + 1) * CH)
        squares = jnp.zeros((CH, HS), F32)
        for h in range(H):
            both = dot(qh[h, span, :], wide[h])
            field = att[h, span, :] + (both[:, :HS] + both[:, HS:]) * ec[span, h : h + 1]
            att[h, span, :] = field
            squares = squares + field * field
        mean = jnp.sum(squares, axis=1, keepdims=True) / (H * HS)
        factor = jnp.broadcast_to(lax.rsqrt(mean + 1e-06), (CH, HS))
        if at >= 2:
            out_copy(at - 2, at % 2).wait()
        outs[at % 2] = jnp.swapaxes((att[:, span, :] * factor[None]).astype(BF16), 0, 1)
        out_copy(at, at % 2).start()

    def wait_p(d, _):
        arrival_p(lax.rem(chip + d, 8)).wait_recv()
        return 0

    lax.fori_loop(1, 8, wait_p, 0)
    total = take[0]
    for n in range(1, 8):
        total = total + take[n]
    total = total[:, :768] * lax.rsqrt(total[:, 768:769] / (H * HS) + 1e-06)
    for n in range(8):
        done[n] = total[2 * n : 2 * n + 2]

    def copy_d(to):
        return remote(done.at[to], last.at[g], sd.at[to], rd.at[g], (c, to))

    def arrival_d(frm):
        return remote(done.at[frm], last.at[frm], sd.at[frm], rd.at[frm], (c, frm))

    def send_d(d, _):
        copy_d(lax.rem(g + d, 8)).start()
        return 0

    lax.fori_loop(1, 8, send_d, 0)
    last[g] = done[g]

    def merge(s, _):
        at = s
        for p in range(8):
            at = jnp.where(slot_ref[p] == s, 64 + p, at)
        merged[s] = cache[at]
        return 0

    lax.fori_loop(0, 64, merge, 0)
    new_copy = pltpu.make_async_copy(merged, new_hbm, new_sem)
    new_copy.start()

    def wait_d(d, _):
        arrival_d(lax.rem(g + d, 8)).wait_recv()
        return 0

    lax.fori_loop(1, 8, wait_d, 0)
    for n in range(8):
        decoded_ref[:, n * 768 : (n + 1) * 768] = last[n]

    out_copy(2, 0).wait()
    out_copy(3, 1).wait()
    new_copy.wait()
    for row in rows:
        copy_a(row).wait_send()
    copy_c.wait_send()

    def finish_pair(m, _):
        copy_b(m).wait_send()
        return 0

    lax.fori_loop(0, 4, finish_pair, 0)

    def finish(d, _):
        j = lax.rem(chip + d, 8)
        copy_1(j).wait_send()
        copy_2(j).wait_send()
        copy_p(j).wait_send()
        to = lax.rem(g + d, 8)
        copy_w(to).wait_send()
        copy_h(to).wait_send()
        copy_z(to).wait_send()
        copy_d(to).wait_send()
        return 0

    lax.fori_loop(1, 8, finish, 0)


def per_device(
    queries, keys, values, prefill_decay, start_states, resident_states, slot_of_prompt,
    decode_queries, decode_keys, decode_values, decode_gate, decode_decay, norm_gain, out_weight,
):
    dma = pltpu.SemaphoreType.DMA
    hbm, vmem = pl.BlockSpec(memory_space=pl.ANY), pl.BlockSpec(memory_space=pltpu.VMEM)
    prefill_out, cache, decoded = pl.pallas_call(
        kernel,
        name="lightning",
        out_shape=(
            jax.ShapeDtypeStruct((T, H, HS), BF16),
            jax.ShapeDtypeStruct((64, 2, 16, HS), F32),
            jax.ShapeDtypeStruct((2, 6144), F32),
        ),
        in_specs=[pl.BlockSpec(memory_space=pltpu.SMEM), hbm, hbm, hbm, vmem, vmem, vmem, hbm] + [vmem] * 6,
        out_specs=(hbm, hbm, vmem),
        scratch_shapes=[
            pltpu.VMEM((3, 2, T, 16, HS), BF16),
            pltpu.VMEM((H, T, HS), BF16),
            pltpu.VMEM((H, HS, T), BF16),
            pltpu.VMEM((H, T, HS), BF16),
            pltpu.VMEM((H, T), F32),
            pltpu.VMEM((H, T), F32),
            pltpu.VMEM((T, HS), F32),
            pltpu.VMEM((2, 16, ROWS, HS), F32),
            pltpu.VMEM((16, ROWS, HS), F32),
            pltpu.VMEM((8, 2, ROWS, HS), F32),
            pltpu.VMEM((8, 2, ROWS, HS), F32),
            pltpu.VMEM((8, 2, HS, HS), F32),
            pltpu.VMEM((8, 2, HS, HS), F32),
            pltpu.VMEM((16, HS, HS), F32),
            pltpu.VMEM((2, 16, HS, HS), F32),
            pltpu.VMEM((2, HS, HS), F32),
            pltpu.VMEM((8, 2, 16, HS), F32),
            pltpu.VMEM((8, 2, 16, HS), F32),
            pltpu.VMEM((8, 32, 768), F32),
            pltpu.VMEM((8, 32, 768), F32),
            pltpu.VMEM((256, 768), BF16),
            pltpu.VMEM((H, T, HS), F32),
            pltpu.VMEM((H, HS, 2 * HS), BF16),
            pltpu.VMEM((2, CH, H, HS), BF16),
            pltpu.VMEM((72, 2, 16, HS), F32),
            pltpu.VMEM((64, 2, 16, HS), F32),
            pltpu.VMEM((256, HS), F32),
            pltpu.VMEM((40, 256), F32),
            pltpu.VMEM((8, 40, 256), F32),
            pltpu.VMEM((2, 8, 16, 896), F32),
            pltpu.VMEM((8, 16, 896), F32),
            pltpu.VMEM((8, 16, 896), F32),
            pltpu.VMEM((8, 2, 768), F32),
            pltpu.VMEM((8, 2, 768), F32),
            dma((3, 2)), dma, dma, dma((2,)),
            dma((2,)), dma((2,)), dma((8,)), dma((8,)), dma((8,)), dma((8,)),
            dma((4,)), dma((4,)), dma((8,)), dma((8,)), dma((8,)), dma((8,)),
            dma((8,)), dma((8,)), dma, dma, dma((8,)), dma((8,)), dma((8,)), dma((8,)),
        ],
        compiler_params=pltpu.CompilerParams(
            collective_id=0, has_side_effects=True, vmem_limit_bytes=VMEM_LIMIT
        ),
    )(
        slot_of_prompt,
        queries[0],
        keys[0],
        values[0],
        jnp.swapaxes(prefill_decay[0], 0, 1),
        start_states[0],
        out_weight.reshape(32, 6144),
        jnp.swapaxes(resident_states, 2, 3),
        decode_queries,
        decode_keys,
        jnp.transpose(decode_values, (1, 2, 3, 0)),
        jnp.transpose(decode_gate, (1, 2, 3, 0)),
        jnp.transpose(decode_decay, (1, 2, 0)).reshape(8, 64),
        norm_gain[:, :, None],
    )
    return prefill_out[None], jnp.swapaxes(cache, 2, 3), decoded


def solution(mesh):
    return jax.shard_map(
        per_device,
        mesh=mesh,
        in_specs=(
            P("grp", "ctx", None, None),
            P("grp", "ctx", None, None),
            P("grp", "ctx", None, None),
            P("grp", "ctx", None),
            P("grp", "ctx", None, None),
            P(None, "ctx", None, "grp"),
            P(),
            P(None, None, "ctx", None),
            P(None, None, "ctx", None),
            P(None, None, "ctx", "grp"),
            P(None, None, "ctx", "grp"),
            P(None, None, "ctx"),
            P("ctx", "grp"),
            P("ctx", "grp", None),
        ),
        out_specs=(
            P("grp", "ctx", None, None),
            P(None, "ctx", None, "grp"),
            P(("ctx", "grp"), None),
        ),
        check_vma=False,
    )
```

```python
import jax
import jax.numpy as jnp
from jax import lax
from jax.experimental import pallas as pl
from jax.experimental.pallas import tpu as pltpu
from jax.sharding import PartitionSpec as P

H = 32
HS = 128
LOG2E = 1.4426950408889634
MESH = pl.DeviceIdType.MESH
F32 = jnp.float32
BF16 = jnp.bfloat16
VMEM_LIMIT = 60 * 1024 * 1024
T = 512
CH = 128
ROWS = 136
HEADS_AT_SCAN = 8
HEADS_AT_GATHER = 16
HEADS_AT_SUM = 20
UNROLL = 4


def dot(a, b):
    return lax.dot_general(a, b, (((1,), (0,)), ((), ())), preferred_element_type=F32)


def split(x):
    hi = x.astype(BF16)
    return hi, (x - hi.astype(F32)).astype(BF16)


def head_of(half, i):
    return 4 * lax.div(i, 2) + 2 * half + lax.rem(i, 2)


def remote(src, dst, send, recv, where):
    return pltpu.make_async_remote_copy(
        src_ref=src, dst_ref=dst, send_sem=send, recv_sem=recv, device_id=where, device_id_type=MESH
    )


def kernel(
    slot_ref, q_hbm, k_hbm, v_hbm, dec_ref, start_ref, w_ref, cache_hbm, dq_ref, dk_ref, dv_ref, gate_ref, decay_ref, gain_ref,
    out_hbm, new_hbm, decoded_ref,
    raw, qh, kt, vh, cum2, cum, ec, s_ref, xbuf, tbuf, rbuf, pbuf, qbuf, obuf, states, pcur, fbuf, hbuf, wf, wr, wt, att,
    wide, outs, cache, merged, zrow, zmine, zbuf, part, half, take, done, last,
    gated, given, taken, ymine, ybuf, place,
    load_sem, cache_sem, new_sem, out_sem, sa, ra, s1, r1, s2, r2, sb, rb, sh, rh, sw, rw, sz, rz, sc, rc, sp, rp, sd, rd, sv, rv, sy, ry,
):
    c, g = lax.axis_index("ctx"), lax.axis_index("grp")
    core, chip = lax.rem(c, 2), lax.div(c, 2)
    other = 1 - core
    partner = (2 * chip + other, g)

    def peer(j):
        return (2 * j + core, g)

    x, own_row = lax.rem(chip, 4), lax.div(chip, 4)
    rows = (1 - own_row, own_row)

    def load(which, hbm, row):
        heads = pl.ds(pl.multiple_of(16 * row, 16), 16)
        return pltpu.make_async_copy(hbm.at[:, heads], raw.at[which, row], load_sem.at[which, row])

    for row in rows:
        load(0, k_hbm, row).start()
        load(1, v_hbm, row).start()
    for row in rows:
        load(2, q_hbm, row).start()
    cache_load = pltpu.make_async_copy(cache_hbm, cache.at[pl.ds(0, 64)], cache_sem)
    cache_load.start()

    bar = pltpu.get_barrier_semaphore()
    pl.semaphore_signal(bar, inc=1, device_id=partner, device_id_type=MESH)

    def greet(d, _):
        pl.semaphore_signal(bar, inc=1, device_id=peer(lax.rem(chip + d, 8)), device_id_type=MESH)
        pl.semaphore_signal(bar, inc=1, device_id=(c, lax.rem(g + d, 8)), device_id_type=MESH)
        return 0

    lax.fori_loop(1, 8, greet, 0)

    lane = lax.broadcasted_iota(jnp.int32, (H, T), 1)
    total = dec_ref[...]
    step = 1
    while step < T:
        total = total + jnp.where(lane >= step, pltpu.roll(total, step, 1), 0.0)
        step *= 2
    cum[...] = total
    cum2[...] = total * LOG2E
    ec[...] = jnp.concatenate([jnp.exp(total), jnp.zeros((HS - H, T), F32)], axis=0).T

    def heads_first(which, row, at):
        return jnp.swapaxes(raw[which, row, pl.ds(at * CH, CH)], 0, 1)

    def relay_kv(row):
        load(0, k_hbm, row).wait()
        load(1, v_hbm, row).wait()

        def chunk(at, _):
            span = pl.ds(pl.multiple_of(at * CH, CH), CH)
            vh[pl.ds(16 * row, 16), span, :] = heads_first(1, row, at)
            block = heads_first(0, row, at)
            for h in range(16):
                kt[16 * row + h, :, span] = block[h].T
            return 0

        lax.fori_loop(0, T // CH, chunk, 0)

    def local_state(half, i):
        h = head_of(half, i)
        row = cum[pl.ds(h, 1), :]
        end = row[:, T - 1 : T]
        hi, lo = split(kt[h].astype(F32) * jnp.exp(end - row))
        both = dot(jnp.concatenate([hi, lo], axis=0), vh[h])
        s_ref[half, i, 0:HS, :] = both[:HS] + both[HS:]
        s_ref[half, i, HS:ROWS, :] = jnp.broadcast_to(end, (ROWS - HS, HS))

    def copy_a(row):
        part = pl.ds(8 * row, 8)
        return remote(s_ref.at[other, part], xbuf.at[part], sa.at[row], ra.at[row], partner)

    def copy_1(j):
        return remote(tbuf.at[j], rbuf.at[chip], s1.at[j], r1.at[chip], peer(j))

    def arrival_1(j):
        return remote(tbuf.at[j], rbuf.at[j], s1.at[j], r1.at[j], peer(j))

    def chip_total(j):
        for r in range(2):
            i = 2 * j + r
            mine, theirs = s_ref[core, i], xbuf[i]
            end_mine, end_theirs = mine[HS : HS + 1], theirs[HS : HS + 1]
            on_mine = jnp.where(core == 0, jnp.exp(end_theirs), 1.0)
            on_theirs = jnp.where(core == 0, 1.0, jnp.exp(end_mine))
            tbuf[j, r, 0:HS, :] = on_mine * mine[:HS] + on_theirs * theirs[:HS]
            tbuf[j, r, HS:ROWS, :] = mine[HS:] + theirs[HS:]

    def send_total(row):
        def one(d, _):
            j = 4 * row + lax.rem(x + d, 4)
            chip_total(j)
            copy_1(j).start()
            return 0

        return one

    def local_states(row):
        for i in range(8):
            local_state(other, 8 * row + i)
        copy_a(row).start()
        for i in range(8):
            local_state(core, 8 * row + i)

    pl.semaphore_wait(bar, 15)
    for to in range(8):
        wf[to] = w_ref[:, to * 768 : (to + 1) * 768].astype(F32)

    def copy_w(to):
        return remote(wf.at[to], wr.at[g], sw.at[to], rw.at[g], (c, to))

    def arrival_w(frm):
        return remote(wf.at[frm], wr.at[frm], sw.at[frm], rw.at[frm], (c, frm))

    def send_w(d, _):
        copy_w(lax.rem(g + d, 8)).start()
        return 0

    lax.fori_loop(1, 8, send_w, 0)
    wr[g] = wf[g]

    relay_kv(rows[0])
    local_states(rows[0])
    relay_kv(rows[1])
    copy_a(rows[0]).wait_recv()
    lax.fori_loop(0, 4, send_total(rows[0]), 0)
    local_states(rows[1])
    copy_a(rows[1]).wait_recv()
    lax.fori_loop(1, 4, send_total(rows[1]), 0)
    chip_total(chip)
    rbuf[chip] = tbuf[chip]

    for row in rows:
        load(2, q_hbm, row).wait()

        def relay_q(at, _):
            span = pl.ds(pl.multiple_of(at * CH, CH), CH)
            qh[pl.ds(16 * row, 16), span, :] = heads_first(2, row, at)
            return 0

        lax.fori_loop(0, T // CH, relay_q, 0)

    lane = lax.broadcasted_iota(jnp.int32, (16, 64), 1)
    wide_lane = lax.broadcasted_iota(jnp.int32, (16, HS), 1)
    diagonal = lax.broadcasted_iota(jnp.int32, (16, 16), 0) == lax.broadcasted_iota(jnp.int32, (16, 16), 1)
    for h in range(2):
        spread_gain = jnp.broadcast_to(gain_ref[h : h + 1, :], (16, 16))
        gain = jnp.sum(jnp.where(diagonal, spread_gain, 0.0), axis=1, keepdims=True)
        for i in range(4):
            gated[i, h] = gain * jax.nn.sigmoid(gate_ref[i, h].astype(F32))

    def give(p, _):
        here = lane == slot_ref[p]
        message = jnp.zeros((16, HS), F32)
        for h in range(2):
            for i in range(4):
                value = jnp.sum(jnp.where(here, dv_ref[i, h].astype(F32), 0.0), axis=1, keepdims=True)
                factor = jnp.sum(jnp.where(here, gated[i, h], 0.0), axis=1, keepdims=True)
                message = jnp.where(wide_lane == 4 * h + i, value, message)
                message = jnp.where(wide_lane == 8 + 4 * h + i, factor, message)
        given[p] = message
        return 0

    lax.fori_loop(0, 8, give, 0)

    def copy_v(to):
        return remote(given.at[to], taken.at[g], sv.at[to], rv.at[g], (c, to))

    def arrival_v(frm):
        return remote(given.at[frm], taken.at[frm], sv.at[frm], rv.at[frm], (c, frm))

    def send_v(d, _):
        copy_v(lax.rem(g + d, 8)).start()
        return 0

    lax.fori_loop(1, 8, send_v, 0)
    taken[g] = given[g]

    pick = lax.broadcasted_iota(jnp.int32, (8, 64), 1)
    scale = jnp.exp(decay_ref[...])

    def decode_row(at, s, ys):
        here = lane == s
        q, k = dq_ref[s].astype(F32), dk_ref[s].astype(F32)
        factor = jnp.sum(jnp.where(pick == s, scale, 0.0), axis=1, keepdims=True)
        ys = list(ys)
        for h in range(2):
            state = cache[at, h]
            for i in range(4):
                value = jnp.sum(jnp.where(here, dv_ref[i, h].astype(F32), 0.0), axis=1, keepdims=True)
                state = factor[2 * i + h : 2 * i + h + 1] * state + value * k[i, h : h + 1, :]
                if ys:
                    y = jnp.sum(state * q[i, h : h + 1, :], axis=1, keepdims=True)
                    ys[2 * i + h] = jnp.where(here, y, ys[2 * i + h])
            cache[at, h] = state
        return tuple(ys)

    cache_load.wait()
    ys = lax.fori_loop(
        0, 64, lambda s, ys: decode_row(s, s, ys), tuple(jnp.zeros((16, 64), F32) for _ in range(8)), unroll=2
    )
    fresh = lane < 64
    for p in range(8):
        fresh = jnp.logical_and(fresh, lane != slot_ref[p])
    for i in range(4):
        squares = jnp.zeros((1, 64), F32)
        parts = []
        for h in range(2):
            y = jnp.where(fresh, ys[2 * i + h], 0.0)
            squares = squares + jnp.sum(y * y, axis=0, keepdims=True)
            parts.append(y * gated[i, h])
        parts.append(jnp.broadcast_to(squares, (8, 64)))
        parts.append(jnp.zeros((HS - 40, 64), F32))
        zrow[pl.ds(i, 64, stride=4), :] = jnp.concatenate(parts, axis=0).T
    zmine[...] = zrow[...].T[:40]

    def copy_z(to):
        return remote(zmine, zbuf.at[g], sz.at[to], rz.at[g], (c, to))

    def arrival_z(frm):
        return remote(zmine, zbuf.at[frm], sz.at[frm], rz.at[frm], (c, frm))

    def send_z(d, _):
        copy_z(lax.rem(g + d, 8)).start()
        return 0

    lax.fori_loop(1, 8, send_z, 0)
    zbuf[g] = zmine[...]

    to_row = lax.broadcasted_iota(jnp.int32, (256, HS), 0)
    from_row = lax.broadcasted_iota(jnp.int32, (256, HS), 1)
    target = jnp.zeros((256, HS), jnp.int32)
    for p in range(8):
        target = jnp.where(lax.div(from_row, 16) == p, 4 * slot_ref[p], target)
    hit = to_row == target + lax.rem(from_row, 4)
    for n in range(3):
        kind = lax.rem(lax.div(from_row, 4), 4) == n
        place[n] = jnp.where(jnp.logical_and(hit, kind), 1.0, 0.0).astype(BF16)

    causal = lax.broadcasted_iota(jnp.int32, (HS, HS), 0) >= lax.broadcasted_iota(jnp.int32, (HS, HS), 1)

    def attend(h):
        row = cum2[pl.ds(h, 1), :]
        col = jnp.broadcast_to(row, (HS, T)).T
        left = dot(qh[h], kt[h, :, 0:256])
        right = dot(qh[h, 256:512, :], kt[h, :, 256:512])

        def weigh(a, b):
            scores = left if b < 2 else right
            first = a if b < 2 else a - 2
            part = scores[first * HS : (first + 1) * HS, (b % 2) * HS : (b % 2 + 1) * HS]
            diff = col[a * HS : (a + 1) * HS] - row[:, b * HS : (b + 1) * HS]
            if a == b:
                diff = jnp.where(causal, diff, -1e30)
            return (part * jnp.exp2(diff)).astype(BF16)

        v = vh[h]
        none = jnp.zeros((HS, HS), BF16)
        top = jnp.concatenate([
            jnp.concatenate([weigh(0, 0), none], axis=1),
            jnp.concatenate([weigh(1, 0), weigh(1, 1)], axis=1),
        ], axis=0)
        low = jnp.concatenate([
            jnp.concatenate([weigh(2, 0), weigh(2, 1), weigh(2, 2), none], axis=1),
            jnp.concatenate([weigh(3, 0), weigh(3, 1), weigh(3, 2), weigh(3, 3)], axis=1),
        ], axis=0)
        att[h, 0:256, :] = dot(top, v[0:256])
        att[h, 256:512, :] = dot(low, v)

    def some(n, _):
        for u in range(UNROLL):
            attend(UNROLL * n + u)
        return 0

    lax.fori_loop(0, HEADS_AT_SCAN // UNROLL, some, 0)

    def copy_2(j):
        return remote(pbuf.at[j], qbuf.at[chip], s2.at[j], r2.at[chip], peer(j))

    def arrival_2(j):
        return remote(pbuf.at[j], qbuf.at[j], s2.at[j], r2.at[j], peer(j))

    pcur[...] = start_ref[...]

    def scan(j, _):
        pbuf[j] = pcur[...]

        @pl.when(j != chip)
        def _():
            arrival_1(j).wait_recv()

        for r in range(2):
            pcur[r] = jnp.exp(rbuf[j, r, HS : HS + 1, :]) * pcur[r] + rbuf[j, r, 0:HS, :]
        return 0

    lax.fori_loop(0, 8, scan, 0)
    qbuf[chip] = pbuf[chip]

    def wait_v(d, _):
        arrival_v(lax.rem(g + d, 8)).wait_recv()
        return 0

    lax.fori_loop(1, 8, wait_v, 0)
    columns = jnp.concatenate([taken[n] for n in range(8)], axis=0)
    mine = slot_ref[g]
    q, k = dq_ref[mine].astype(F32), dk_ref[mine].astype(F32)
    step_scale = jnp.sum(jnp.where(pick == mine, scale, 0.0), axis=1, keepdims=True)
    tall_lane = lax.broadcasted_iota(jnp.int32, (HS, HS), 1)
    tall = jnp.zeros((HS, HS), F32)
    for h in range(2):
        state = pcur[h].T
        fbuf[:, h] = state.reshape(8, 16, HS)
        for i in range(4):
            n = 4 * h + i
            state = step_scale[2 * i + h : 2 * i + h + 1] * state + columns[:, n : n + 1] * k[i, h : h + 1, :]
            y = jnp.sum(state * q[i, h : h + 1, :], axis=1, keepdims=True)
            tall = jnp.where(tall_lane == n, y * columns[:, 8 + n : 9 + n], tall)
            squares = jnp.sum(y * y, axis=0, keepdims=True)
            tall = jnp.where(tall_lane == 8 + i, tall + squares, tall)
    ymine[...] = tall.T[:16]

    def copy_y(to):
        return remote(ymine, ybuf.at[g], sy.at[to], ry.at[g], (c, to))

    def arrival_y(frm):
        return remote(ymine, ybuf.at[frm], sy.at[frm], ry.at[frm], (c, frm))

    def send_y(d, _):
        copy_y(lax.rem(g + d, 8)).start()
        return 0

    lax.fori_loop(1, 8, send_y, 0)

    def send_2(d, _):
        copy_2(lax.rem(chip + d, 8)).start()
        return 0

    lax.fori_loop(1, 8, send_2, 0)
    ybuf[g] = ymine[...]

    def copy_h(to):
        return remote(fbuf.at[to], hbuf.at[g], sh.at[to], rh.at[g], (c, to))

    def arrival_h(frm):
        return remote(fbuf.at[frm], hbuf.at[frm], sh.at[frm], rh.at[frm], (c, frm))

    def send_h(d, _):
        copy_h(lax.rem(g + d, 8)).start()
        return 0

    lax.fori_loop(1, 8, send_h, 0)
    hbuf[g] = fbuf[g]

    def wait_z(d, _):
        frm = lax.rem(g + d, 8)
        arrival_z(frm).wait_recv()
        arrival_w(frm).wait_recv()
        return 0

    lax.fori_loop(1, 8, wait_z, 0)
    for h in range(2):
        for frm in range(8):
            at = h * HS + frm * 16
            wt[at : at + 16, :] = wr[frm, h * 16 : (h + 1) * 16, :].astype(BF16)
    z = jnp.concatenate([zbuf[n, 16 * h : 16 * h + 16, :] for h in range(2) for n in range(8)], axis=0).T
    squares = zbuf[0, 32:40, :]
    for n in range(1, 8):
        squares = squares + zbuf[n, 32:40, :]
    squares = jnp.concatenate([squares] * 16, axis=0).T
    hi, lo = split(z)
    for n in range(3):
        span = slice(n * 256, (n + 1) * 256)
        w = wt[:, span]
        both = (dot(hi, w) + dot(lo, w)).reshape(8, 2, 16, 256)
        for k in range(2):
            part[k, :, :, span] = both[:, k]
    both = squares.reshape(8, 2, 16, HS)
    for k in range(2):
        part[k, :, :, 768:896] = both[:, k]
    lax.fori_loop(HEADS_AT_SCAN // UNROLL, HEADS_AT_GATHER // UNROLL, some, 0)

    def wait_y(d, _):
        arrival_y(lax.rem(g + d, 8)).wait_recv()
        return 0

    lax.fori_loop(1, 8, wait_y, 0)
    hi, lo = split(ybuf[...].reshape(HS, HS))
    squares = (dot(place[2], hi) + dot(place[2], lo)).reshape(8, 2, 16, HS)
    hi = [dot(place[h], hi).astype(BF16) for h in range(2)]
    lo = [dot(place[h], lo).astype(BF16) for h in range(2)]
    z = jnp.concatenate([jnp.concatenate(hi, axis=1), jnp.concatenate(lo, axis=1)], axis=0)
    for n in range(3):
        span = slice(n * 256, (n + 1) * 256)
        both = dot(z, wt[:, span])
        both = (both[:256] + both[256:]).reshape(8, 2, 16, 256)
        for k in range(2):
            part[k, :, :, span] = part[k, :, :, span] + both[:, k]
    for k in range(2):
        part[k, :, :, 768:896] = part[k, :, :, 768:896] + squares[:, k]
    copy_c = remote(part.at[other], half, sc, rc, partner)
    copy_c.start()
    lax.fori_loop(HEADS_AT_GATHER // UNROLL, HEADS_AT_SUM // UNROLL, some, 0)

    def copy_b(m):
        return remote(obuf.at[pl.ds(4 * m, 4)], states.at[core, pl.ds(4 * m, 4)], sb.at[m], rb.at[m], partner)

    def arrival_b(m):
        return remote(obuf.at[pl.ds(4 * m, 4)], states.at[other, pl.ds(4 * m, 4)], sb.at[m], rb.at[m], partner)

    def spread(m, _):
        for n in range(2):
            j = 2 * m + n

            @pl.when(j != chip)
            def _():
                arrival_2(j).wait_recv()

            for r in range(2):
                i = 2 * j + r
                before = qbuf[j, r]
                first = jnp.where(core == 0, s_ref[core, i], xbuf[i])
                after = jnp.exp(first[HS : HS + 1]) * before + first[:HS]
                states[core, i] = jnp.where(core == 0, before, after)
                obuf[i] = jnp.where(core == 0, after, before)
        copy_b(m).start()
        return 0

    copy_c.wait_recv()
    half[...] = half[...] + part[core]

    def copy_p(to):
        return remote(half.at[to], take.at[chip], sp.at[to], rp.at[chip], peer(to))

    def arrival_p(frm):
        return remote(half.at[frm], take.at[frm], sp.at[frm], rp.at[frm], peer(frm))

    def send_p(d, _):
        copy_p(lax.rem(chip + d, 8)).start()
        return 0

    lax.fori_loop(1, 8, send_p, 0)
    take[chip] = half[chip]
    lax.fori_loop(0, 4, spread, 0)


    lax.fori_loop(HEADS_AT_SUM // UNROLL, H // UNROLL, some, 0)

    def take_b(m, _):
        arrival_b(m).wait_recv()
        return 0

    lax.fori_loop(0, 4, take_b, 0)
    for h in range(H):
        hi, lo = split(states[(h // 2) % 2, 2 * (h // 4) + h % 2])
        wide[h, :, 0:HS] = hi
        wide[h, :, HS:] = lo

    def out_copy(at, slot):
        return pltpu.make_async_copy(outs.at[slot], out_hbm.at[pl.ds(at * CH, CH)], out_sem.at[slot])

    for at in range(T // CH):
        span = slice(at * CH, (at + 1) * CH)
        squares = jnp.zeros((CH, HS), F32)
        for h in range(H):
            both = dot(qh[h, span, :], wide[h])
            field = att[h, span, :] + (both[:, :HS] + both[:, HS:]) * ec[span, h : h + 1]
            att[h, span, :] = field
            squares = squares + field * field
        mean = jnp.sum(squares, axis=1, keepdims=True) / (H * HS)
        factor = jnp.broadcast_to(lax.rsqrt(mean + 1e-06), (CH, HS))
        if at >= 2:
            out_copy(at - 2, at % 2).wait()
        outs[at % 2] = jnp.swapaxes((att[:, span, :] * factor[None]).astype(BF16), 0, 1)
        out_copy(at, at % 2).start()

    def wait_p(d, _):
        arrival_p(lax.rem(chip + d, 8)).wait_recv()
        return 0

    lax.fori_loop(1, 8, wait_p, 0)
    total = take[0]
    for n in range(1, 8):
        total = total + take[n]
    total = total[:, :768] * lax.rsqrt(total[:, 768:769] / (H * HS) + 1e-06)
    for n in range(8):
        done[n] = total[2 * n : 2 * n + 2]

    def copy_d(to):
        return remote(done.at[to], last.at[g], sd.at[to], rd.at[g], (c, to))

    def arrival_d(frm):
        return remote(done.at[frm], last.at[frm], sd.at[frm], rd.at[frm], (c, frm))

    def send_d(d, _):
        copy_d(lax.rem(g + d, 8)).start()
        return 0

    lax.fori_loop(1, 8, send_d, 0)
    last[g] = done[g]

    def take_h(d, _):
        arrival_h(lax.rem(g + d, 8)).wait_recv()
        return 0

    lax.fori_loop(1, 8, take_h, 0)
    cache[64:72] = hbuf[...]
    lax.fori_loop(0, 8, lambda p, ys: decode_row(64 + p, slot_ref[p], ys), ())

    def merge(s, _):
        at = s
        for p in range(8):
            at = jnp.where(slot_ref[p] == s, 64 + p, at)
        merged[s] = cache[at]
        return 0

    lax.fori_loop(0, 64, merge, 0)
    new_copy = pltpu.make_async_copy(merged, new_hbm, new_sem)
    new_copy.start()

    def wait_d(d, _):
        arrival_d(lax.rem(g + d, 8)).wait_recv()
        return 0

    lax.fori_loop(1, 8, wait_d, 0)
    for n in range(8):
        decoded_ref[:, n * 768 : (n + 1) * 768] = last[n]

    out_copy(2, 0).wait()
    out_copy(3, 1).wait()
    new_copy.wait()
    for row in rows:
        copy_a(row).wait_send()
    copy_c.wait_send()

    def finish_pair(m, _):
        copy_b(m).wait_send()
        return 0

    lax.fori_loop(0, 4, finish_pair, 0)

    def finish(d, _):
        j = lax.rem(chip + d, 8)
        copy_1(j).wait_send()
        copy_2(j).wait_send()
        copy_p(j).wait_send()
        to = lax.rem(g + d, 8)
        copy_w(to).wait_send()
        copy_h(to).wait_send()
        copy_z(to).wait_send()
        copy_d(to).wait_send()
        copy_v(to).wait_send()
        copy_y(to).wait_send()
        return 0

    lax.fori_loop(1, 8, finish, 0)


def per_device(
    queries, keys, values, prefill_decay, start_states, resident_states, slot_of_prompt,
    decode_queries, decode_keys, decode_values, decode_gate, decode_decay, norm_gain, out_weight,
):
    dma = pltpu.SemaphoreType.DMA
    hbm, vmem = pl.BlockSpec(memory_space=pl.ANY), pl.BlockSpec(memory_space=pltpu.VMEM)
    prefill_out, cache, decoded = pl.pallas_call(
        kernel,
        name="lightning",
        out_shape=(
            jax.ShapeDtypeStruct((T, H, HS), BF16),
            jax.ShapeDtypeStruct((64, 2, 16, HS), F32),
            jax.ShapeDtypeStruct((2, 6144), F32),
        ),
        in_specs=[pl.BlockSpec(memory_space=pltpu.SMEM), hbm, hbm, hbm, vmem, vmem, vmem, hbm] + [vmem] * 6,
        out_specs=(hbm, hbm, vmem),
        scratch_shapes=[
            pltpu.VMEM((3, 2, T, 16, HS), BF16),
            pltpu.VMEM((H, T, HS), BF16),
            pltpu.VMEM((H, HS, T), BF16),
            pltpu.VMEM((H, T, HS), BF16),
            pltpu.VMEM((H, T), F32),
            pltpu.VMEM((H, T), F32),
            pltpu.VMEM((T, HS), F32),
            pltpu.VMEM((2, 16, ROWS, HS), F32),
            pltpu.VMEM((16, ROWS, HS), F32),
            pltpu.VMEM((8, 2, ROWS, HS), F32),
            pltpu.VMEM((8, 2, ROWS, HS), F32),
            pltpu.VMEM((8, 2, HS, HS), F32),
            pltpu.VMEM((8, 2, HS, HS), F32),
            pltpu.VMEM((16, HS, HS), F32),
            pltpu.VMEM((2, 16, HS, HS), F32),
            pltpu.VMEM((2, HS, HS), F32),
            pltpu.VMEM((8, 2, 16, HS), F32),
            pltpu.VMEM((8, 2, 16, HS), F32),
            pltpu.VMEM((8, 32, 768), F32),
            pltpu.VMEM((8, 32, 768), F32),
            pltpu.VMEM((256, 768), BF16),
            pltpu.VMEM((H, T, HS), F32),
            pltpu.VMEM((H, HS, 2 * HS), BF16),
            pltpu.VMEM((2, CH, H, HS), BF16),
            pltpu.VMEM((72, 2, 16, HS), F32),
            pltpu.VMEM((64, 2, 16, HS), F32),
            pltpu.VMEM((256, HS), F32),
            pltpu.VMEM((40, 256), F32),
            pltpu.VMEM((8, 40, 256), F32),
            pltpu.VMEM((2, 8, 16, 896), F32),
            pltpu.VMEM((8, 16, 896), F32),
            pltpu.VMEM((8, 16, 896), F32),
            pltpu.VMEM((8, 2, 768), F32),
            pltpu.VMEM((8, 2, 768), F32),
            pltpu.VMEM((4, 2, 16, 64), F32),
            pltpu.VMEM((8, 16, HS), F32),
            pltpu.VMEM((8, 16, HS), F32),
            pltpu.VMEM((16, HS), F32),
            pltpu.VMEM((8, 16, HS), F32),
            pltpu.VMEM((3, 256, HS), BF16),
            dma((3, 2)), dma, dma, dma((2,)),
            dma((2,)), dma((2,)), dma((8,)), dma((8,)), dma((8,)), dma((8,)),
            dma((4,)), dma((4,)), dma((8,)), dma((8,)), dma((8,)), dma((8,)),
            dma((8,)), dma((8,)), dma, dma, dma((8,)), dma((8,)), dma((8,)), dma((8,)),
            dma((8,)), dma((8,)), dma((8,)), dma((8,)),
        ],
        compiler_params=pltpu.CompilerParams(
            collective_id=0, has_side_effects=True, vmem_limit_bytes=VMEM_LIMIT
        ),
    )(
        slot_of_prompt,
        queries[0],
        keys[0],
        values[0],
        jnp.swapaxes(prefill_decay[0], 0, 1),
        start_states[0],
        out_weight.reshape(32, 6144),
        jnp.swapaxes(resident_states, 2, 3),
        decode_queries,
        decode_keys,
        jnp.transpose(decode_values, (1, 2, 3, 0)),
        jnp.transpose(decode_gate, (1, 2, 3, 0)),
        jnp.transpose(decode_decay, (1, 2, 0)).reshape(8, 64),
        norm_gain,
    )
    return prefill_out[None], jnp.swapaxes(cache, 2, 3), decoded


def solution(mesh):
    return jax.shard_map(
        per_device,
        mesh=mesh,
        in_specs=(
            P("grp", "ctx", None, None),
            P("grp", "ctx", None, None),
            P("grp", "ctx", None, None),
            P("grp", "ctx", None),
            P("grp", "ctx", None, None),
            P(None, "ctx", None, "grp"),
            P(),
            P(None, None, "ctx", None),
            P(None, None, "ctx", None),
            P(None, None, "ctx", "grp"),
            P(None, None, "ctx", "grp"),
            P(None, None, "ctx"),
            P("ctx", "grp"),
            P("ctx", "grp", None),
        ),
        out_specs=(
            P("grp", "ctx", None, None),
            P(None, "ctx", None, "grp"),
            P(("ctx", "grp"), None),
        ),
        check_vma=False,
    )
```

```python
import jax
import jax.numpy as jnp
from jax import lax
from jax.experimental import pallas as pl
from jax.experimental.pallas import tpu as pltpu
from jax.sharding import PartitionSpec as P

H = 32
HS = 128
LOG2E = 1.4426950408889634
MESH = pl.DeviceIdType.MESH
F32 = jnp.float32
BF16 = jnp.bfloat16
VMEM_LIMIT = 54 * 1024 * 1024
T = 512
CH = 128
ROWS = 136
HEADS_AT_SCAN = 8
HEADS_AT_GATHER = 16
HEADS_AT_SUM = 20
UNROLL = 4


def dot(a, b):
    return lax.dot_general(a, b, (((1,), (0,)), ((), ())), preferred_element_type=F32)


def split(x):
    hi = x.astype(BF16)
    return hi, (x - hi.astype(F32)).astype(BF16)


def head_of(half, i):
    return 4 * lax.div(i, 2) + 2 * half + lax.rem(i, 2)


def remote(src, dst, send, recv, where):
    return pltpu.make_async_remote_copy(
        src_ref=src, dst_ref=dst, send_sem=send, recv_sem=recv, device_id=where, device_id_type=MESH
    )


def kernel(
    slot_ref, q_hbm, k_hbm, v_hbm, dec_ref, start_ref, w_ref, cache_hbm, dq_ref, dk_ref, dv_ref, gate_ref, decay_ref, gain_ref,
    out_ref, new_ref, decoded_ref,
    raw, qh, kt, vh, cum2, cum, ec, s_ref, xbuf, tbuf, rbuf, pbuf, qbuf, obuf, states, pcur, fbuf, hbuf, wf, wr, wt, att,
    wide, cache, zrow, zmine, zbuf, part, half, take, done, last,
    gated, given, taken, ymine, ybuf, place,
    load_sem, cache_sem, sa, ra, s1, r1, s2, r2, sb, rb, sh, rh, sw, rw, sz, rz, sc, rc, sp, rp, sd, rd, sv, rv, sy, ry,
):
    c, g = lax.axis_index("ctx"), lax.axis_index("grp")
    core, chip = lax.rem(c, 2), lax.div(c, 2)
    other = 1 - core
    partner = (2 * chip + other, g)

    def peer(j):
        return (2 * j + core, g)

    x, own_row = lax.rem(chip, 4), lax.div(chip, 4)
    rows = (1 - own_row, own_row)

    def load(which, hbm, row):
        heads = pl.ds(pl.multiple_of(16 * row, 16), 16)
        return pltpu.make_async_copy(hbm.at[:, heads], raw.at[which % 2, row], load_sem.at[which, row])

    for row in rows:
        load(0, k_hbm, row).start()
        load(1, v_hbm, row).start()
    cache_load = pltpu.make_async_copy(cache_hbm, cache.at[pl.ds(0, 64)], cache_sem)
    cache_load.start()

    bar = pltpu.get_barrier_semaphore()
    pl.semaphore_signal(bar, inc=1, device_id=partner, device_id_type=MESH)

    def greet(d, _):
        pl.semaphore_signal(bar, inc=1, device_id=peer(lax.rem(chip + d, 8)), device_id_type=MESH)
        pl.semaphore_signal(bar, inc=1, device_id=(c, lax.rem(g + d, 8)), device_id_type=MESH)
        return 0

    lax.fori_loop(1, 8, greet, 0)

    lane = lax.broadcasted_iota(jnp.int32, (H, T), 1)
    total = dec_ref[...]
    step = 1
    while step < T:
        total = total + jnp.where(lane >= step, pltpu.roll(total, step, 1), 0.0)
        step *= 2
    cum[...] = total
    cum2[...] = total * LOG2E
    ec[...] = jnp.concatenate([jnp.exp(total), jnp.zeros((HS - H, T), F32)], axis=0).T

    def heads_first(which, row, at):
        return jnp.swapaxes(raw[which % 2, row, pl.ds(at * CH, CH)], 0, 1)

    def relay_kv(row):
        load(0, k_hbm, row).wait()
        load(1, v_hbm, row).wait()

        def chunk(at, _):
            span = pl.ds(pl.multiple_of(at * CH, CH), CH)
            vh[pl.ds(16 * row, 16), span, :] = heads_first(1, row, at)
            block = heads_first(0, row, at)
            for h in range(16):
                kt[16 * row + h, :, span] = block[h].T
            return 0

        lax.fori_loop(0, T // CH, chunk, 0)

    def local_state(half, i):
        h = head_of(half, i)
        row = cum[pl.ds(h, 1), :]
        end = row[:, T - 1 : T]
        hi, lo = split(kt[h].astype(F32) * jnp.exp(end - row))
        both = dot(jnp.concatenate([hi, lo], axis=0), vh[h])
        s_ref[half, i, 0:HS, :] = both[:HS] + both[HS:]
        s_ref[half, i, HS:ROWS, :] = jnp.broadcast_to(end, (ROWS - HS, HS))

    def copy_a(row):
        part = pl.ds(8 * row, 8)
        return remote(s_ref.at[other, part], xbuf.at[part], sa.at[row], ra.at[row], partner)

    def copy_1(j):
        return remote(tbuf.at[j], rbuf.at[chip], s1.at[j], r1.at[chip], peer(j))

    def arrival_1(j):
        return remote(tbuf.at[j], rbuf.at[j], s1.at[j], r1.at[j], peer(j))

    def chip_total(j):
        for r in range(2):
            i = 2 * j + r
            mine, theirs = s_ref[core, i], xbuf[i]
            end_mine, end_theirs = mine[HS : HS + 1], theirs[HS : HS + 1]
            on_mine = jnp.where(core == 0, jnp.exp(end_theirs), 1.0)
            on_theirs = jnp.where(core == 0, 1.0, jnp.exp(end_mine))
            tbuf[j, r, 0:HS, :] = on_mine * mine[:HS] + on_theirs * theirs[:HS]
            tbuf[j, r, HS:ROWS, :] = mine[HS:] + theirs[HS:]

    def send_total(row):
        def one(d, _):
            j = 4 * row + lax.rem(x + d, 4)
            chip_total(j)
            copy_1(j).start()
            return 0

        return one

    def local_states(row):
        for i in range(8):
            local_state(other, 8 * row + i)
        copy_a(row).start()
        for i in range(8):
            local_state(core, 8 * row + i)

    pl.semaphore_wait(bar, 15)
    for to in range(8):
        wf[to] = w_ref[:, to * 768 : (to + 1) * 768].astype(F32)

    def copy_w(to):
        return remote(wf.at[to], wr.at[g], sw.at[to], rw.at[g], (c, to))

    def arrival_w(frm):
        return remote(wf.at[frm], wr.at[frm], sw.at[frm], rw.at[frm], (c, frm))

    def send_w(d, _):
        copy_w(lax.rem(g + d, 8)).start()
        return 0

    lax.fori_loop(1, 8, send_w, 0)
    wr[g] = wf[g]

    relay_kv(rows[0])
    load(2, q_hbm, rows[0]).start()
    local_states(rows[0])
    relay_kv(rows[1])
    load(2, q_hbm, rows[1]).start()
    copy_a(rows[0]).wait_recv()
    lax.fori_loop(0, 4, send_total(rows[0]), 0)
    local_states(rows[1])
    copy_a(rows[1]).wait_recv()
    lax.fori_loop(1, 4, send_total(rows[1]), 0)
    chip_total(chip)
    rbuf[chip] = tbuf[chip]

    for row in rows:
        load(2, q_hbm, row).wait()

        def relay_q(at, _):
            span = pl.ds(pl.multiple_of(at * CH, CH), CH)
            qh[pl.ds(16 * row, 16), span, :] = heads_first(2, row, at)
            return 0

        lax.fori_loop(0, T // CH, relay_q, 0)

    lane = lax.broadcasted_iota(jnp.int32, (16, 64), 1)
    wide_lane = lax.broadcasted_iota(jnp.int32, (16, HS), 1)
    diagonal = lax.broadcasted_iota(jnp.int32, (16, 16), 0) == lax.broadcasted_iota(jnp.int32, (16, 16), 1)
    for h in range(2):
        spread_gain = jnp.broadcast_to(gain_ref[h : h + 1, :], (16, 16))
        gain = jnp.sum(jnp.where(diagonal, spread_gain, 0.0), axis=1, keepdims=True)
        for i in range(4):
            gated[i, h] = gain * jax.nn.sigmoid(gate_ref[i, h].astype(F32))

    def give(p, _):
        here = lane == slot_ref[p]
        message = jnp.zeros((16, HS), F32)
        for h in range(2):
            for i in range(4):
                value = jnp.sum(jnp.where(here, dv_ref[i, h].astype(F32), 0.0), axis=1, keepdims=True)
                factor = jnp.sum(jnp.where(here, gated[i, h], 0.0), axis=1, keepdims=True)
                message = jnp.where(wide_lane == 4 * h + i, value, message)
                message = jnp.where(wide_lane == 8 + 4 * h + i, factor, message)
        given[p] = message
        return 0

    lax.fori_loop(0, 8, give, 0)

    def copy_v(to):
        return remote(given.at[to], taken.at[g], sv.at[to], rv.at[g], (c, to))

    def arrival_v(frm):
        return remote(given.at[frm], taken.at[frm], sv.at[frm], rv.at[frm], (c, frm))

    def send_v(d, _):
        copy_v(lax.rem(g + d, 8)).start()
        return 0

    lax.fori_loop(1, 8, send_v, 0)
    taken[g] = given[g]

    pick = lax.broadcasted_iota(jnp.int32, (8, 64), 1)
    scale = jnp.exp(decay_ref[...])

    def decode_row(at, s, ys):
        here = lane == s
        q, k = dq_ref[s].astype(F32), dk_ref[s].astype(F32)
        factor = jnp.sum(jnp.where(pick == s, scale, 0.0), axis=1, keepdims=True)
        ys = list(ys)
        for h in range(2):
            state = cache[at, h]
            for i in range(4):
                value = jnp.sum(jnp.where(here, dv_ref[i, h].astype(F32), 0.0), axis=1, keepdims=True)
                state = factor[2 * i + h : 2 * i + h + 1] * state + value * k[i, h : h + 1, :]
                if ys:
                    y = jnp.sum(state * q[i, h : h + 1, :], axis=1, keepdims=True)
                    ys[2 * i + h] = jnp.where(here, y, ys[2 * i + h])
            cache[at, h] = state
        return tuple(ys)

    cache_load.wait()
    ys = lax.fori_loop(
        0, 64, lambda s, ys: decode_row(s, s, ys), tuple(jnp.zeros((16, 64), F32) for _ in range(8)), unroll=2
    )
    fresh = lane < 64
    for p in range(8):
        fresh = jnp.logical_and(fresh, lane != slot_ref[p])
    for i in range(4):
        squares = jnp.zeros((1, 64), F32)
        parts = []
        for h in range(2):
            y = jnp.where(fresh, ys[2 * i + h], 0.0)
            squares = squares + jnp.sum(y * y, axis=0, keepdims=True)
            parts.append(y * gated[i, h])
        parts.append(jnp.broadcast_to(squares, (8, 64)))
        parts.append(jnp.zeros((HS - 40, 64), F32))
        zrow[pl.ds(i, 64, stride=4), :] = jnp.concatenate(parts, axis=0).T
    zmine[...] = zrow[...].T[:40]

    def copy_z(to):
        return remote(zmine, zbuf.at[g], sz.at[to], rz.at[g], (c, to))

    def arrival_z(frm):
        return remote(zmine, zbuf.at[frm], sz.at[frm], rz.at[frm], (c, frm))

    def send_z(d, _):
        copy_z(lax.rem(g + d, 8)).start()
        return 0

    lax.fori_loop(1, 8, send_z, 0)
    zbuf[g] = zmine[...]

    to_row = lax.broadcasted_iota(jnp.int32, (256, HS), 0)
    from_row = lax.broadcasted_iota(jnp.int32, (256, HS), 1)
    target = jnp.zeros((256, HS), jnp.int32)
    for p in range(8):
        target = jnp.where(lax.div(from_row, 16) == p, 4 * slot_ref[p], target)
    hit = to_row == target + lax.rem(from_row, 4)
    for n in range(3):
        kind = lax.rem(lax.div(from_row, 4), 4) == n
        place[n] = jnp.where(jnp.logical_and(hit, kind), 1.0, 0.0).astype(BF16)

    causal = lax.broadcasted_iota(jnp.int32, (HS, HS), 0) >= lax.broadcasted_iota(jnp.int32, (HS, HS), 1)

    def attend(h):
        row = cum2[pl.ds(h, 1), :]
        col = jnp.broadcast_to(row, (HS, T)).T
        left = dot(qh[h], kt[h, :, 0:256])
        right = dot(qh[h, 256:512, :], kt[h, :, 256:512])

        def weigh(a, b):
            scores = left if b < 2 else right
            first = a if b < 2 else a - 2
            part = scores[first * HS : (first + 1) * HS, (b % 2) * HS : (b % 2 + 1) * HS]
            diff = col[a * HS : (a + 1) * HS] - row[:, b * HS : (b + 1) * HS]
            if a == b:
                diff = jnp.where(causal, diff, -1e30)
            return (part * jnp.exp2(diff)).astype(BF16)

        v = vh[h]
        none = jnp.zeros((HS, HS), BF16)
        top = jnp.concatenate([
            jnp.concatenate([weigh(0, 0), none], axis=1),
            jnp.concatenate([weigh(1, 0), weigh(1, 1)], axis=1),
        ], axis=0)
        low = jnp.concatenate([
            jnp.concatenate([weigh(2, 0), weigh(2, 1), weigh(2, 2), none], axis=1),
            jnp.concatenate([weigh(3, 0), weigh(3, 1), weigh(3, 2), weigh(3, 3)], axis=1),
        ], axis=0)
        att[h, 0:256, :] = dot(top, v[0:256])
        att[h, 256:512, :] = dot(low, v)

    def some(n, _):
        for u in range(UNROLL):
            attend(UNROLL * n + u)
        return 0

    lax.fori_loop(0, HEADS_AT_SCAN // UNROLL, some, 0)

    def copy_2(j):
        return remote(pbuf.at[j], qbuf.at[chip], s2.at[j], r2.at[chip], peer(j))

    def arrival_2(j):
        return remote(pbuf.at[j], qbuf.at[j], s2.at[j], r2.at[j], peer(j))

    pcur[...] = start_ref[...]

    def scan(j, _):
        pbuf[j] = pcur[...]

        @pl.when(j != chip)
        def _():
            arrival_1(j).wait_recv()

        for r in range(2):
            pcur[r] = jnp.exp(rbuf[j, r, HS : HS + 1, :]) * pcur[r] + rbuf[j, r, 0:HS, :]
        return 0

    lax.fori_loop(0, 8, scan, 0)
    qbuf[chip] = pbuf[chip]

    def wait_v(d, _):
        arrival_v(lax.rem(g + d, 8)).wait_recv()
        return 0

    lax.fori_loop(1, 8, wait_v, 0)
    columns = jnp.concatenate([taken[n] for n in range(8)], axis=0)
    mine = slot_ref[g]
    q, k = dq_ref[mine].astype(F32), dk_ref[mine].astype(F32)
    step_scale = jnp.sum(jnp.where(pick == mine, scale, 0.0), axis=1, keepdims=True)
    tall_lane = lax.broadcasted_iota(jnp.int32, (HS, HS), 1)
    tall = jnp.zeros((HS, HS), F32)
    for h in range(2):
        state = pcur[h].T
        fbuf[:, h] = state.reshape(8, 16, HS)
        for i in range(4):
            n = 4 * h + i
            state = step_scale[2 * i + h : 2 * i + h + 1] * state + columns[:, n : n + 1] * k[i, h : h + 1, :]
            y = jnp.sum(state * q[i, h : h + 1, :], axis=1, keepdims=True)
            tall = jnp.where(tall_lane == n, y * columns[:, 8 + n : 9 + n], tall)
            squares = jnp.sum(y * y, axis=0, keepdims=True)
            tall = jnp.where(tall_lane == 8 + i, tall + squares, tall)
    ymine[...] = tall.T[:16]

    def copy_y(to):
        return remote(ymine, ybuf.at[g], sy.at[to], ry.at[g], (c, to))

    def arrival_y(frm):
        return remote(ymine, ybuf.at[frm], sy.at[frm], ry.at[frm], (c, frm))

    def send_y(d, _):
        copy_y(lax.rem(g + d, 8)).start()
        return 0

    lax.fori_loop(1, 8, send_y, 0)

    def send_2(d, _):
        copy_2(4 * own_row + lax.rem(x + d, 4)).start()
        return 0

    def send_2_across(d, _):
        copy_2(4 * rows[0] + lax.rem(x + d, 4)).start()
        return 0

    lax.fori_loop(0, 4, send_2_across, 0)
    lax.fori_loop(1, 4, send_2, 0)
    ybuf[g] = ymine[...]

    def copy_h(to):
        return remote(fbuf.at[to], hbuf.at[g], sh.at[to], rh.at[g], (c, to))

    def arrival_h(frm):
        return remote(fbuf.at[frm], hbuf.at[frm], sh.at[frm], rh.at[frm], (c, frm))

    def send_h(d, _):
        copy_h(lax.rem(g + d, 8)).start()
        return 0

    lax.fori_loop(1, 8, send_h, 0)
    hbuf[g] = fbuf[g]

    def wait_z(d, _):
        frm = lax.rem(g + d, 8)
        arrival_z(frm).wait_recv()
        arrival_w(frm).wait_recv()
        return 0

    lax.fori_loop(1, 8, wait_z, 0)
    for h in range(2):
        for frm in range(8):
            at = h * HS + frm * 16
            wt[at : at + 16, :] = wr[frm, h * 16 : (h + 1) * 16, :].astype(BF16)
    z = jnp.concatenate([zbuf[n, 16 * h : 16 * h + 16, :] for h in range(2) for n in range(8)], axis=0).T
    squares = zbuf[0, 32:40, :]
    for n in range(1, 8):
        squares = squares + zbuf[n, 32:40, :]
    squares = jnp.concatenate([squares] * 16, axis=0).T
    hi, lo = split(z)
    for n in range(3):
        span = slice(n * 256, (n + 1) * 256)
        w = wt[:, span]
        both = (dot(hi, w) + dot(lo, w)).reshape(8, 2, 16, 256)
        for k in range(2):
            part[k, :, :, span] = both[:, k]
    both = squares.reshape(8, 2, 16, HS)
    for k in range(2):
        part[k, :, :, 768:896] = both[:, k]
    lax.fori_loop(HEADS_AT_SCAN // UNROLL, HEADS_AT_GATHER // UNROLL, some, 0)

    def wait_y(d, _):
        arrival_y(lax.rem(g + d, 8)).wait_recv()
        return 0

    lax.fori_loop(1, 8, wait_y, 0)
    hi, lo = split(ybuf[...].reshape(HS, HS))
    squares = (dot(place[2], hi) + dot(place[2], lo)).reshape(8, 2, 16, HS)
    hi = [dot(place[h], hi).astype(BF16) for h in range(2)]
    lo = [dot(place[h], lo).astype(BF16) for h in range(2)]
    z = jnp.concatenate([jnp.concatenate(hi, axis=1), jnp.concatenate(lo, axis=1)], axis=0)
    for n in range(3):
        span = slice(n * 256, (n + 1) * 256)
        both = dot(z, wt[:, span])
        both = (both[:256] + both[256:]).reshape(8, 2, 16, 256)
        for k in range(2):
            part[k, :, :, span] = part[k, :, :, span] + both[:, k]
    for k in range(2):
        part[k, :, :, 768:896] = part[k, :, :, 768:896] + squares[:, k]
    copy_c = remote(part.at[other], half, sc, rc, partner)
    copy_c.start()
    lax.fori_loop(HEADS_AT_GATHER // UNROLL, HEADS_AT_SUM // UNROLL, some, 0)

    def copy_b(m):
        return remote(obuf.at[pl.ds(4 * m, 4)], states.at[core, pl.ds(4 * m, 4)], sb.at[m], rb.at[m], partner)

    def arrival_b(m):
        return remote(obuf.at[pl.ds(4 * m, 4)], states.at[other, pl.ds(4 * m, 4)], sb.at[m], rb.at[m], partner)

    def spread(m, _):
        for n in range(2):
            j = 2 * m + n

            @pl.when(j != chip)
            def _():
                arrival_2(j).wait_recv()

            for r in range(2):
                i = 2 * j + r
                before = qbuf[j, r]
                first = jnp.where(core == 0, s_ref[core, i], xbuf[i])
                after = jnp.exp(first[HS : HS + 1]) * before + first[:HS]
                states[core, i] = jnp.where(core == 0, before, after)
                obuf[i] = jnp.where(core == 0, after, before)
        copy_b(m).start()
        return 0

    copy_c.wait_recv()
    half[...] = half[...] + part[core]

    def copy_p(to):
        return remote(half.at[to], take.at[chip], sp.at[to], rp.at[chip], peer(to))

    def arrival_p(frm):
        return remote(half.at[frm], take.at[frm], sp.at[frm], rp.at[frm], peer(frm))

    def send_p(d, _):
        copy_p(lax.rem(chip + d, 8)).start()
        return 0

    lax.fori_loop(1, 8, send_p, 0)
    take[chip] = half[chip]
    lax.fori_loop(0, 4, spread, 0)


    lax.fori_loop(HEADS_AT_SUM // UNROLL, H // UNROLL, some, 0)

    def take_b(m, _):
        arrival_b(m).wait_recv()
        return 0

    lax.fori_loop(0, 4, take_b, 0)
    for h in range(H):
        hi, lo = split(states[(h // 2) % 2, 2 * (h // 4) + h % 2])
        wide[h, :, 0:HS] = hi
        wide[h, :, HS:] = lo

    def finish_chunk(at):
        span = slice(at * CH, (at + 1) * CH)
        squares = jnp.zeros((CH, HS), F32)
        for h in range(H):
            both = dot(qh[h, span, :], wide[h])
            field = att[h, span, :] + (both[:, :HS] + both[:, HS:]) * ec[span, h : h + 1]
            att[h, span, :] = field
            squares = squares + field * field
        mean = jnp.sum(squares, axis=1, keepdims=True) / (H * HS)
        factor = jnp.broadcast_to(lax.rsqrt(mean + 1e-06), (CH, HS))
        out_ref[span] = jnp.swapaxes((att[:, span, :] * factor[None]).astype(BF16), 0, 1)

    for at in range(2):
        finish_chunk(at)

    def wait_p(d, _):
        arrival_p(lax.rem(chip + d, 8)).wait_recv()
        return 0

    lax.fori_loop(1, 8, wait_p, 0)
    total = take[0]
    for n in range(1, 8):
        total = total + take[n]
    total = total[:, :768] * lax.rsqrt(total[:, 768:769] / (H * HS) + 1e-06)
    for n in range(8):
        done[n] = total[2 * n : 2 * n + 2]

    def copy_d(to):
        return remote(done.at[to], last.at[g], sd.at[to], rd.at[g], (c, to))

    def arrival_d(frm):
        return remote(done.at[frm], last.at[frm], sd.at[frm], rd.at[frm], (c, frm))

    def send_d(d, _):
        copy_d(lax.rem(g + d, 8)).start()
        return 0

    lax.fori_loop(1, 8, send_d, 0)
    last[g] = done[g]

    for at in range(2, T // CH):
        finish_chunk(at)

    def take_h(d, _):
        arrival_h(lax.rem(g + d, 8)).wait_recv()
        return 0

    lax.fori_loop(1, 8, take_h, 0)
    cache[64:72] = hbuf[...]
    lax.fori_loop(0, 8, lambda p, ys: decode_row(64 + p, slot_ref[p], ys), ())

    def merge(s, _):
        at = s
        for p in range(8):
            at = jnp.where(slot_ref[p] == s, 64 + p, at)
        new_ref[s] = cache[at]
        return 0

    lax.fori_loop(0, 64, merge, 0)

    def wait_d(d, _):
        arrival_d(lax.rem(g + d, 8)).wait_recv()
        return 0

    lax.fori_loop(1, 8, wait_d, 0)
    for n in range(8):
        decoded_ref[:, n * 768 : (n + 1) * 768] = last[n]

    for row in rows:
        copy_a(row).wait_send()
    copy_c.wait_send()

    def finish_pair(m, _):
        copy_b(m).wait_send()
        return 0

    lax.fori_loop(0, 4, finish_pair, 0)

    def finish(d, _):
        j = lax.rem(chip + d, 8)
        copy_1(j).wait_send()
        copy_2(j).wait_send()
        copy_p(j).wait_send()
        to = lax.rem(g + d, 8)
        copy_w(to).wait_send()
        copy_h(to).wait_send()
        copy_z(to).wait_send()
        copy_d(to).wait_send()
        copy_v(to).wait_send()
        copy_y(to).wait_send()
        return 0

    lax.fori_loop(1, 8, finish, 0)


def per_device(
    queries, keys, values, prefill_decay, start_states, resident_states, slot_of_prompt,
    decode_queries, decode_keys, decode_values, decode_gate, decode_decay, norm_gain, out_weight,
):
    dma = pltpu.SemaphoreType.DMA
    hbm, vmem = pl.BlockSpec(memory_space=pl.ANY), pl.BlockSpec(memory_space=pltpu.VMEM)
    results = (
        jax.ShapeDtypeStruct((T, H, HS), BF16),
        jax.ShapeDtypeStruct((64, 2, 16, HS), F32),
        jax.ShapeDtypeStruct((2, 6144), F32),
    )
    prefill_out, cache, decoded = pl.pallas_call(
        kernel,
        name="lightning",
        out_shape=tuple(pltpu.VMEM(x.shape, x.dtype) for x in results),
        in_specs=[pl.BlockSpec(memory_space=pltpu.SMEM), hbm, hbm, hbm, vmem, vmem, vmem, hbm] + [vmem] * 6,
        out_specs=(vmem, vmem, vmem),
        scratch_shapes=[
            pltpu.VMEM((2, 2, T, 16, HS), BF16),
            pltpu.VMEM((H, T, HS), BF16),
            pltpu.VMEM((H, HS, T), BF16),
            pltpu.VMEM((H, T, HS), BF16),
            pltpu.VMEM((H, T), F32),
            pltpu.VMEM((H, T), F32),
            pltpu.VMEM((T, HS), F32),
            pltpu.VMEM((2, 16, ROWS, HS), F32),
            pltpu.VMEM((16, ROWS, HS), F32),
            pltpu.VMEM((8, 2, ROWS, HS), F32),
            pltpu.VMEM((8, 2, ROWS, HS), F32),
            pltpu.VMEM((8, 2, HS, HS), F32),
            pltpu.VMEM((8, 2, HS, HS), F32),
            pltpu.VMEM((16, HS, HS), F32),
            pltpu.VMEM((2, 16, HS, HS), F32),
            pltpu.VMEM((2, HS, HS), F32),
            pltpu.VMEM((8, 2, 16, HS), F32),
            pltpu.VMEM((8, 2, 16, HS), F32),
            pltpu.VMEM((8, 32, 768), F32),
            pltpu.VMEM((8, 32, 768), F32),
            pltpu.VMEM((256, 768), BF16),
            pltpu.VMEM((H, T, HS), F32),
            pltpu.VMEM((H, HS, 2 * HS), BF16),
            pltpu.VMEM((72, 2, 16, HS), F32),
            pltpu.VMEM((256, HS), F32),
            pltpu.VMEM((40, 256), F32),
            pltpu.VMEM((8, 40, 256), F32),
            pltpu.VMEM((2, 8, 16, 896), F32),
            pltpu.VMEM((8, 16, 896), F32),
            pltpu.VMEM((8, 16, 896), F32),
            pltpu.VMEM((8, 2, 768), F32),
            pltpu.VMEM((8, 2, 768), F32),
            pltpu.VMEM((4, 2, 16, 64), F32),
            pltpu.VMEM((8, 16, HS), F32),
            pltpu.VMEM((8, 16, HS), F32),
            pltpu.VMEM((16, HS), F32),
            pltpu.VMEM((8, 16, HS), F32),
            pltpu.VMEM((3, 256, HS), BF16),
            dma((3, 2)), dma,
            dma((2,)), dma((2,)), dma((8,)), dma((8,)), dma((8,)), dma((8,)),
            dma((4,)), dma((4,)), dma((8,)), dma((8,)), dma((8,)), dma((8,)),
            dma((8,)), dma((8,)), dma, dma, dma((8,)), dma((8,)), dma((8,)), dma((8,)),
            dma((8,)), dma((8,)), dma((8,)), dma((8,)),
        ],
        compiler_params=pltpu.CompilerParams(
            collective_id=0, has_side_effects=True, vmem_limit_bytes=VMEM_LIMIT
        ),
    )(
        slot_of_prompt,
        queries[0],
        keys[0],
        values[0],
        jnp.swapaxes(prefill_decay[0], 0, 1),
        start_states[0],
        out_weight.reshape(32, 6144),
        jnp.swapaxes(resident_states, 2, 3),
        decode_queries,
        decode_keys,
        jnp.transpose(decode_values, (1, 2, 3, 0)),
        jnp.transpose(decode_gate, (1, 2, 3, 0)),
        jnp.transpose(decode_decay, (1, 2, 0)).reshape(8, 64),
        norm_gain,
    )
    return prefill_out[None], jnp.swapaxes(cache, 2, 3), decoded


def solution(mesh):
    return jax.shard_map(
        per_device,
        mesh=mesh,
        in_specs=(
            P("grp", "ctx", None, None),
            P("grp", "ctx", None, None),
            P("grp", "ctx", None, None),
            P("grp", "ctx", None),
            P("grp", "ctx", None, None),
            P(None, "ctx", None, "grp"),
            P(),
            P(None, None, "ctx", None),
            P(None, None, "ctx", None),
            P(None, None, "ctx", "grp"),
            P(None, None, "ctx", "grp"),
            P(None, None, "ctx"),
            P("ctx", "grp"),
            P("ctx", "grp", None),
        ),
        out_specs=(
            P("grp", "ctx", None, None),
            P(None, "ctx", None, "grp"),
            P(("ctx", "grp"), None),
        ),
        check_vma=False,
    )
```

```python
import jax
import jax.numpy as jnp
from jax import lax
from jax.experimental import pallas as pl
from jax.experimental.pallas import tpu as pltpu
from jax.sharding import PartitionSpec as P

H = 32
HS = 128
LOG2E = 1.4426950408889634
MESH = pl.DeviceIdType.MESH
F32 = jnp.float32
BF16 = jnp.bfloat16
VMEM_LIMIT = 54 * 1024 * 1024
T = 512
CH = 128
ROWS = 136
HEADS_AT_SCAN = 8
HEADS_AT_GATHER = 16
HEADS_AT_SUM = 20
UNROLL = 4


def dot(a, b):
    return lax.dot_general(a, b, (((1,), (0,)), ((), ())), preferred_element_type=F32)


def split(x):
    hi = x.astype(BF16)
    return hi, (x - hi.astype(F32)).astype(BF16)


def head_of(half, i):
    return 4 * lax.div(i, 2) + 2 * half + lax.rem(i, 2)


def remote(src, dst, send, recv, where):
    return pltpu.make_async_remote_copy(
        src_ref=src, dst_ref=dst, send_sem=send, recv_sem=recv, device_id=where, device_id_type=MESH
    )


def kernel(
    slot_ref, q_hbm, k_hbm, v_hbm, dec_ref, start_ref, w_ref, cache_hbm, dq_ref, dk_ref, dv_ref, gate_ref, decay_ref, gain_ref,
    out_ref, new_ref, decoded_ref,
    raw, qh, kt, vh, cum2, cum, ec, s_ref, xbuf, tbuf, rbuf, pbuf, qbuf, obuf, states, pcur, fbuf, hbuf, wf, wr, wt, att,
    wide, cache, zrow, zmine, zbuf, part, half, take, done, last,
    gated, given, taken, ymine, ybuf, place, row_total, twin_total, start_all, row_start,
    load_sem, cache_sem, sa, ra, s1, r1, s2, r2, sb, rb, sh, rh, sw, rw, sz, rz, sc, rc, sp, rp, sd, rd, sv, rv, sy, ry, st, rt, ss, rs,
):
    c, g = lax.axis_index("ctx"), lax.axis_index("grp")
    core, chip = lax.rem(c, 2), lax.div(c, 2)
    other = 1 - core
    partner = (2 * chip + other, g)

    def peer(j):
        return (2 * j + core, g)

    x, own_row = lax.rem(chip, 4), lax.div(chip, 4)
    rows = (1 - own_row, own_row)
    twin = peer(4 * rows[0] + x)

    def in_row(j):
        return peer(4 * own_row + lax.rem(j, 4))

    def mine_of(j):
        return 4 * lax.div(j, 4) + x

    def load(which, hbm, row):
        heads = pl.ds(pl.multiple_of(16 * row, 16), 16)
        return pltpu.make_async_copy(hbm.at[:, heads], raw.at[which % 2, row], load_sem.at[which, row])

    for row in rows:
        load(0, k_hbm, row).start()
        load(1, v_hbm, row).start()
    cache_load = pltpu.make_async_copy(cache_hbm, cache.at[pl.ds(0, 64)], cache_sem)
    cache_load.start()

    bar = pltpu.get_barrier_semaphore()
    pl.semaphore_signal(bar, inc=1, device_id=partner, device_id_type=MESH)

    def greet(d, _):
        pl.semaphore_signal(bar, inc=1, device_id=peer(lax.rem(chip + d, 8)), device_id_type=MESH)
        pl.semaphore_signal(bar, inc=1, device_id=(c, lax.rem(g + d, 8)), device_id_type=MESH)
        return 0

    lax.fori_loop(1, 8, greet, 0)

    lane = lax.broadcasted_iota(jnp.int32, (H, T), 1)
    total = dec_ref[...]
    step = 1
    while step < T:
        total = total + jnp.where(lane >= step, pltpu.roll(total, step, 1), 0.0)
        step *= 2
    cum[...] = total
    cum2[...] = total * LOG2E
    ec[...] = jnp.concatenate([jnp.exp(total), jnp.zeros((HS - H, T), F32)], axis=0).T

    def heads_first(which, row, at):
        return jnp.swapaxes(raw[which % 2, row, pl.ds(at * CH, CH)], 0, 1)

    def relay_kv(row):
        load(0, k_hbm, row).wait()
        load(1, v_hbm, row).wait()

        def chunk(at, _):
            span = pl.ds(pl.multiple_of(at * CH, CH), CH)
            vh[pl.ds(16 * row, 16), span, :] = heads_first(1, row, at)
            block = heads_first(0, row, at)
            for h in range(16):
                kt[16 * row + h, :, span] = block[h].T
            return 0

        lax.fori_loop(0, T // CH, chunk, 0)

    def local_state(half, i):
        h = head_of(half, i)
        row = cum[pl.ds(h, 1), :]
        end = row[:, T - 1 : T]
        hi, lo = split(kt[h].astype(F32) * jnp.exp(end - row))
        both = dot(jnp.concatenate([hi, lo], axis=0), vh[h])
        s_ref[half, i, 0:HS, :] = both[:HS] + both[HS:]
        s_ref[half, i, HS:ROWS, :] = jnp.broadcast_to(end, (ROWS - HS, HS))

    def copy_a(row):
        part = pl.ds(8 * row, 8)
        return remote(s_ref.at[other, part], xbuf.at[part], sa.at[row], ra.at[row], partner)

    def copy_1(j):
        return remote(tbuf.at[j], rbuf.at[mine_of(j)], s1.at[j], r1.at[mine_of(j)], in_row(j))

    def arrival_1(j):
        return remote(tbuf.at[j], rbuf.at[j], s1.at[j], r1.at[j], in_row(j))

    def chip_total(j):
        for r in range(2):
            i = 2 * j + r
            mine, theirs = s_ref[core, i], xbuf[i]
            end_mine, end_theirs = mine[HS : HS + 1], theirs[HS : HS + 1]
            on_mine = jnp.where(core == 0, jnp.exp(end_theirs), 1.0)
            on_theirs = jnp.where(core == 0, 1.0, jnp.exp(end_mine))
            tbuf[j, r, 0:HS, :] = on_mine * mine[:HS] + on_theirs * theirs[:HS]
            tbuf[j, r, HS:ROWS, :] = mine[HS:] + theirs[HS:]

    def send_total(row):
        def one(d, _):
            j = 4 * row + lax.rem(x + d, 4)
            chip_total(j)
            copy_1(j).start()
            return 0

        return one

    def local_states(row):
        for i in range(8):
            local_state(other, 8 * row + i)
        copy_a(row).start()
        for i in range(8):
            local_state(core, 8 * row + i)

    pl.semaphore_wait(bar, 15)
    for to in range(8):
        wf[to] = w_ref[:, to * 768 : (to + 1) * 768].astype(F32)

    def copy_w(to):
        return remote(wf.at[to], wr.at[g], sw.at[to], rw.at[g], (c, to))

    def arrival_w(frm):
        return remote(wf.at[frm], wr.at[frm], sw.at[frm], rw.at[frm], (c, frm))

    def send_w(d, _):
        copy_w(lax.rem(g + d, 8)).start()
        return 0

    def send_w_odd(n, _):
        return send_w(2 * n + 1, 0)

    def send_w_even(n, _):
        return send_w(2 * n, 0)

    lax.fori_loop(0, 4, send_w_odd, 0)
    lax.fori_loop(1, 4, send_w_even, 0)
    copy_s = remote(start_ref, start_all.at[own_row], ss, rs, twin)
    copy_s.start()
    start_all[own_row] = start_ref[...]
    wr[g] = wf[g]

    relay_kv(rows[0])
    load(2, q_hbm, rows[0]).start()
    local_states(rows[0])
    relay_kv(rows[1])
    load(2, q_hbm, rows[1]).start()
    copy_a(rows[0]).wait_recv()
    lax.fori_loop(1, 4, send_total(rows[0]), 0)
    local_states(rows[1])
    copy_a(rows[1]).wait_recv()
    lax.fori_loop(1, 4, send_total(rows[1]), 0)
    for row in rows:
        chip_total(4 * row + x)
        rbuf[4 * row + x] = tbuf[4 * row + x]

    def fold(row):
        for d in range(1, 4):
            arrival_1(4 * row + lax.rem(x + d, 4)).wait_recv()
        for r in range(2):
            total = rbuf[4 * row, r]
            for n in range(1, 4):
                term = rbuf[4 * row + n, r]
                total = jnp.concatenate(
                    [jnp.exp(term[HS : HS + 1]) * total[:HS] + term[:HS], total[HS:] + term[HS:]], axis=0
                )
            row_total[row, r] = total

    def copy_t(row):
        return remote(row_total.at[row], twin_total.at[row], st.at[row], rt.at[row], twin)

    for row in rows:
        load(2, q_hbm, row).wait()

        def relay_q(at, _):
            span = pl.ds(pl.multiple_of(at * CH, CH), CH)
            qh[pl.ds(16 * row, 16), span, :] = heads_first(2, row, at)
            return 0

        lax.fori_loop(0, T // CH, relay_q, 0)

    lane = lax.broadcasted_iota(jnp.int32, (16, 64), 1)
    wide_lane = lax.broadcasted_iota(jnp.int32, (16, HS), 1)
    diagonal = lax.broadcasted_iota(jnp.int32, (16, 16), 0) == lax.broadcasted_iota(jnp.int32, (16, 16), 1)
    for h in range(2):
        spread_gain = jnp.broadcast_to(gain_ref[h : h + 1, :], (16, 16))
        gain = jnp.sum(jnp.where(diagonal, spread_gain, 0.0), axis=1, keepdims=True)
        for i in range(4):
            gated[i, h] = gain * jax.nn.sigmoid(gate_ref[i, h].astype(F32))

    def give(p, _):
        here = lane == slot_ref[p]
        message = jnp.zeros((16, HS), F32)
        for h in range(2):
            for i in range(4):
                value = jnp.sum(jnp.where(here, dv_ref[i, h].astype(F32), 0.0), axis=1, keepdims=True)
                factor = jnp.sum(jnp.where(here, gated[i, h], 0.0), axis=1, keepdims=True)
                message = jnp.where(wide_lane == 4 * h + i, value, message)
                message = jnp.where(wide_lane == 8 + 4 * h + i, factor, message)
        given[p] = message
        return 0

    lax.fori_loop(0, 8, give, 0)

    def copy_v(to):
        return remote(given.at[to], taken.at[g], sv.at[to], rv.at[g], (c, to))

    def arrival_v(frm):
        return remote(given.at[frm], taken.at[frm], sv.at[frm], rv.at[frm], (c, frm))

    def send_v(d, _):
        copy_v(lax.rem(g + d, 8)).start()
        return 0

    lax.fori_loop(1, 8, send_v, 0)
    taken[g] = given[g]

    pick = lax.broadcasted_iota(jnp.int32, (8, 64), 1)
    scale = jnp.exp(decay_ref[...])

    def decode_row(at, s, ys):
        here = lane == s
        q, k = dq_ref[s].astype(F32), dk_ref[s].astype(F32)
        factor = jnp.sum(jnp.where(pick == s, scale, 0.0), axis=1, keepdims=True)
        ys = list(ys)
        for h in range(2):
            state = cache[at, h]
            for i in range(4):
                value = jnp.sum(jnp.where(here, dv_ref[i, h].astype(F32), 0.0), axis=1, keepdims=True)
                state = factor[2 * i + h : 2 * i + h + 1] * state + value * k[i, h : h + 1, :]
                if ys:
                    y = jnp.sum(state * q[i, h : h + 1, :], axis=1, keepdims=True)
                    ys[2 * i + h] = jnp.where(here, y, ys[2 * i + h])
            cache[at, h] = state
        return tuple(ys)

    cache_load.wait()
    ys = lax.fori_loop(
        0, 32, lambda s, ys: decode_row(s, s, ys), tuple(jnp.zeros((16, 64), F32) for _ in range(8)), unroll=2
    )
    fold(rows[0])
    copy_t(rows[0]).start()
    ys = lax.fori_loop(32, 64, lambda s, ys: decode_row(s, s, ys), ys, unroll=2)
    fresh = lane < 64
    for p in range(8):
        fresh = jnp.logical_and(fresh, lane != slot_ref[p])
    for i in range(4):
        squares = jnp.zeros((1, 64), F32)
        parts = []
        for h in range(2):
            y = jnp.where(fresh, ys[2 * i + h], 0.0)
            squares = squares + jnp.sum(y * y, axis=0, keepdims=True)
            parts.append(y * gated[i, h])
        parts.append(jnp.broadcast_to(squares, (8, 64)))
        parts.append(jnp.zeros((HS - 40, 64), F32))
        zrow[pl.ds(i, 64, stride=4), :] = jnp.concatenate(parts, axis=0).T
    zmine[...] = zrow[...].T[:40]

    def copy_z(to):
        return remote(zmine, zbuf.at[g], sz.at[to], rz.at[g], (c, to))

    def arrival_z(frm):
        return remote(zmine, zbuf.at[frm], sz.at[frm], rz.at[frm], (c, frm))

    def send_z(d, _):
        copy_z(lax.rem(g + d, 8)).start()
        return 0

    lax.fori_loop(1, 8, send_z, 0)
    zbuf[g] = zmine[...]

    to_row = lax.broadcasted_iota(jnp.int32, (256, HS), 0)
    from_row = lax.broadcasted_iota(jnp.int32, (256, HS), 1)
    target = jnp.zeros((256, HS), jnp.int32)
    for p in range(8):
        target = jnp.where(lax.div(from_row, 16) == p, 4 * slot_ref[p], target)
    hit = to_row == target + lax.rem(from_row, 4)
    for n in range(3):
        kind = lax.rem(lax.div(from_row, 4), 4) == n
        place[n] = jnp.where(jnp.logical_and(hit, kind), 1.0, 0.0).astype(BF16)

    causal = lax.broadcasted_iota(jnp.int32, (HS, HS), 0) >= lax.broadcasted_iota(jnp.int32, (HS, HS), 1)

    def attend(h):
        row = cum2[pl.ds(h, 1), :]
        col = jnp.broadcast_to(row, (HS, T)).T
        left = dot(qh[h], kt[h, :, 0:256])
        right = dot(qh[h, 256:512, :], kt[h, :, 256:512])

        def weigh(a, b):
            scores = left if b < 2 else right
            first = a if b < 2 else a - 2
            part = scores[first * HS : (first + 1) * HS, (b % 2) * HS : (b % 2 + 1) * HS]
            diff = col[a * HS : (a + 1) * HS] - row[:, b * HS : (b + 1) * HS]
            if a == b:
                diff = jnp.where(causal, diff, -1e30)
            return (part * jnp.exp2(diff)).astype(BF16)

        v = vh[h]
        none = jnp.zeros((HS, HS), BF16)
        top = jnp.concatenate([
            jnp.concatenate([weigh(0, 0), none], axis=1),
            jnp.concatenate([weigh(1, 0), weigh(1, 1)], axis=1),
        ], axis=0)
        low = jnp.concatenate([
            jnp.concatenate([weigh(2, 0), weigh(2, 1), weigh(2, 2), none], axis=1),
            jnp.concatenate([weigh(3, 0), weigh(3, 1), weigh(3, 2), weigh(3, 3)], axis=1),
        ], axis=0)
        att[h, 0:256, :] = dot(top, v[0:256])
        att[h, 256:512, :] = dot(low, v)

    def some(n, _):
        for u in range(UNROLL):
            attend(UNROLL * n + u)
        return 0

    lax.fori_loop(0, HEADS_AT_SCAN // UNROLL, some, 0)

    def copy_2(j):
        return remote(pbuf.at[j], qbuf.at[mine_of(j)], s2.at[j], r2.at[mine_of(j)], in_row(j))

    def arrival_2(j):
        return remote(pbuf.at[j], qbuf.at[j], s2.at[j], r2.at[j], in_row(j))

    fold(rows[1])

    @pl.when(own_row == 0)
    def _():
        copy_t(0).start()

    copy_t(own_row).wait_recv()

    def through(total, state):
        return jnp.exp(total[HS : HS + 1]) * state + total[:HS]

    for r in range(2):

        @pl.when(own_row == 0)
        def _():
            pcur[r] = through(twin_total[own_row, r], through(row_total[own_row, r], start_ref[r]))

        @pl.when(own_row == 1)
        def _():
            pcur[r] = through(row_total[own_row, r], through(twin_total[own_row, r], start_ref[r]))

    def wait_v(d, _):
        arrival_v(lax.rem(g + d, 8)).wait_recv()
        return 0

    lax.fori_loop(1, 8, wait_v, 0)
    columns = jnp.concatenate([taken[n] for n in range(8)], axis=0)
    mine = slot_ref[g]
    q, k = dq_ref[mine].astype(F32), dk_ref[mine].astype(F32)
    step_scale = jnp.sum(jnp.where(pick == mine, scale, 0.0), axis=1, keepdims=True)
    tall_lane = lax.broadcasted_iota(jnp.int32, (HS, HS), 1)
    tall = jnp.zeros((HS, HS), F32)
    for h in range(2):
        state = pcur[h].T
        fbuf[:, h] = state.reshape(8, 16, HS)
        for i in range(4):
            n = 4 * h + i
            state = step_scale[2 * i + h : 2 * i + h + 1] * state + columns[:, n : n + 1] * k[i, h : h + 1, :]
            y = jnp.sum(state * q[i, h : h + 1, :], axis=1, keepdims=True)
            tall = jnp.where(tall_lane == n, y * columns[:, 8 + n : 9 + n], tall)
            squares = jnp.sum(y * y, axis=0, keepdims=True)
            tall = jnp.where(tall_lane == 8 + i, tall + squares, tall)
    ymine[...] = tall.T[:16]

    def copy_y(to):
        return remote(ymine, ybuf.at[g], sy.at[to], ry.at[g], (c, to))

    def arrival_y(frm):
        return remote(ymine, ybuf.at[frm], sy.at[frm], ry.at[frm], (c, frm))

    def send_y(d, _):
        copy_y(lax.rem(g + d, 8)).start()
        return 0

    lax.fori_loop(1, 8, send_y, 0)

    remote(start_ref, start_all.at[rows[0]], ss, rs, twin).wait_recv()

    @pl.when(own_row == 0)
    def _():
        row_start[...] = start_all[...]

    @pl.when(own_row == 1)
    def _():
        copy_t(0).wait_recv()
        for row in range(2):
            for r in range(2):
                row_start[row, r] = through(twin_total[row, r], start_all[row, r])

    def before_chip(j, _):
        row = lax.div(j, 4)
        pbuf[j] = row_start[row]

        @pl.when(lax.rem(j, 4) != x)
        def _():
            copy_2(j).start()

        for r in range(2):
            row_start[row, r] = through(rbuf[j, r], row_start[row, r])
        return 0

    lax.fori_loop(0, 8, before_chip, 0)
    for row in range(2):
        qbuf[4 * row + x] = pbuf[4 * row + x]
    ybuf[g] = ymine[...]

    def copy_h(to):
        return remote(fbuf.at[to], hbuf.at[g], sh.at[to], rh.at[g], (c, to))

    def arrival_h(frm):
        return remote(fbuf.at[frm], hbuf.at[frm], sh.at[frm], rh.at[frm], (c, frm))

    def send_h(d, _):
        copy_h(lax.rem(g + d, 8)).start()
        return 0

    lax.fori_loop(1, 8, send_h, 0)
    hbuf[g] = fbuf[g]

    def wait_z(d, _):
        frm = lax.rem(g + d, 8)
        arrival_z(frm).wait_recv()
        arrival_w(frm).wait_recv()
        return 0

    lax.fori_loop(1, 8, wait_z, 0)
    for h in range(2):
        for frm in range(8):
            at = h * HS + frm * 16
            wt[at : at + 16, :] = wr[frm, h * 16 : (h + 1) * 16, :].astype(BF16)
    z = jnp.concatenate([zbuf[n, 16 * h : 16 * h + 16, :] for h in range(2) for n in range(8)], axis=0).T
    squares = zbuf[0, 32:40, :]
    for n in range(1, 8):
        squares = squares + zbuf[n, 32:40, :]
    squares = jnp.concatenate([squares] * 16, axis=0).T
    hi, lo = split(z)
    for n in range(3):
        span = slice(n * 256, (n + 1) * 256)
        w = wt[:, span]
        both = (dot(hi, w) + dot(lo, w)).reshape(8, 2, 16, 256)
        for k in range(2):
            part[k, :, :, span] = both[:, k]
    both = squares.reshape(8, 2, 16, HS)
    for k in range(2):
        part[k, :, :, 768:896] = both[:, k]
    lax.fori_loop(HEADS_AT_SCAN // UNROLL, HEADS_AT_GATHER // UNROLL, some, 0)

    def wait_y(d, _):
        arrival_y(lax.rem(g + d, 8)).wait_recv()
        return 0

    lax.fori_loop(1, 8, wait_y, 0)
    hi, lo = split(ybuf[...].reshape(HS, HS))
    squares = (dot(place[2], hi) + dot(place[2], lo)).reshape(8, 2, 16, HS)
    hi = [dot(place[h], hi).astype(BF16) for h in range(2)]
    lo = [dot(place[h], lo).astype(BF16) for h in range(2)]
    z = jnp.concatenate([jnp.concatenate(hi, axis=1), jnp.concatenate(lo, axis=1)], axis=0)
    for n in range(3):
        span = slice(n * 256, (n + 1) * 256)
        both = dot(z, wt[:, span])
        both = (both[:256] + both[256:]).reshape(8, 2, 16, 256)
        for k in range(2):
            part[k, :, :, span] = part[k, :, :, span] + both[:, k]
    for k in range(2):
        part[k, :, :, 768:896] = part[k, :, :, 768:896] + squares[:, k]
    copy_c = remote(part.at[other], half, sc, rc, partner)
    copy_c.start()
    lax.fori_loop(HEADS_AT_GATHER // UNROLL, HEADS_AT_SUM // UNROLL, some, 0)

    def copy_b(m):
        return remote(obuf.at[pl.ds(4 * m, 4)], states.at[core, pl.ds(4 * m, 4)], sb.at[m], rb.at[m], partner)

    def arrival_b(m):
        return remote(obuf.at[pl.ds(4 * m, 4)], states.at[other, pl.ds(4 * m, 4)], sb.at[m], rb.at[m], partner)

    def spread(m, _):
        for n in range(2):
            j = 2 * m + n

            @pl.when(lax.rem(j, 4) != x)
            def _():
                arrival_2(j).wait_recv()

            for r in range(2):
                i = 2 * j + r
                before = qbuf[j, r]
                first = jnp.where(core == 0, s_ref[core, i], xbuf[i])
                after = jnp.exp(first[HS : HS + 1]) * before + first[:HS]
                states[core, i] = jnp.where(core == 0, before, after)
                obuf[i] = jnp.where(core == 0, after, before)
        copy_b(m).start()
        return 0

    copy_c.wait_recv()
    half[...] = half[...] + part[core]

    def copy_p(to):
        return remote(half.at[to], take.at[chip], sp.at[to], rp.at[chip], peer(to))

    def arrival_p(frm):
        return remote(half.at[frm], take.at[frm], sp.at[frm], rp.at[frm], peer(frm))

    def send_p(d, _):
        copy_p(lax.rem(chip + d, 8)).start()
        return 0

    lax.fori_loop(1, 8, send_p, 0)
    take[chip] = half[chip]
    lax.fori_loop(0, 4, spread, 0)


    lax.fori_loop(HEADS_AT_SUM // UNROLL, H // UNROLL, some, 0)

    def take_b(m, _):
        arrival_b(m).wait_recv()
        return 0

    lax.fori_loop(0, 4, take_b, 0)
    for h in range(H):
        hi, lo = split(states[(h // 2) % 2, 2 * (h // 4) + h % 2])
        wide[h, :, 0:HS] = hi
        wide[h, :, HS:] = lo

    def finish_chunk(at):
        span = slice(at * CH, (at + 1) * CH)
        squares = jnp.zeros((CH, HS), F32)
        for h in range(H):
            both = dot(qh[h, span, :], wide[h])
            field = att[h, span, :] + (both[:, :HS] + both[:, HS:]) * ec[span, h : h + 1]
            att[h, span, :] = field
            squares = squares + field * field
        mean = jnp.sum(squares, axis=1, keepdims=True) / (H * HS)
        factor = jnp.broadcast_to(lax.rsqrt(mean + 1e-06), (CH, HS))
        out_ref[span] = jnp.swapaxes((att[:, span, :] * factor[None]).astype(BF16), 0, 1)

    for at in range(2):
        finish_chunk(at)

    def wait_p(d, _):
        arrival_p(lax.rem(chip + d, 8)).wait_recv()
        return 0

    lax.fori_loop(1, 8, wait_p, 0)
    total = take[0]
    for n in range(1, 8):
        total = total + take[n]
    total = total[:, :768] * lax.rsqrt(total[:, 768:769] / (H * HS) + 1e-06)
    for n in range(8):
        done[n] = total[2 * n : 2 * n + 2]

    def copy_d(to):
        return remote(done.at[to], last.at[g], sd.at[to], rd.at[g], (c, to))

    def arrival_d(frm):
        return remote(done.at[frm], last.at[frm], sd.at[frm], rd.at[frm], (c, frm))

    def send_d(d, _):
        copy_d(lax.rem(g + d, 8)).start()
        return 0

    lax.fori_loop(1, 8, send_d, 0)
    last[g] = done[g]

    for at in range(2, T // CH):
        finish_chunk(at)

    def take_h(d, _):
        arrival_h(lax.rem(g + d, 8)).wait_recv()
        return 0

    lax.fori_loop(1, 8, take_h, 0)
    cache[64:72] = hbuf[...]
    lax.fori_loop(0, 8, lambda p, ys: decode_row(64 + p, slot_ref[p], ys), ())

    def merge(s, _):
        at = s
        for p in range(8):
            at = jnp.where(slot_ref[p] == s, 64 + p, at)
        new_ref[s] = cache[at]
        return 0

    lax.fori_loop(0, 64, merge, 0)

    def wait_d(d, _):
        arrival_d(lax.rem(g + d, 8)).wait_recv()
        return 0

    lax.fori_loop(1, 8, wait_d, 0)
    for n in range(8):
        decoded_ref[:, n * 768 : (n + 1) * 768] = last[n]

    for row in rows:
        copy_a(row).wait_send()
    copy_c.wait_send()

    def finish_pair(m, _):
        copy_b(m).wait_send()
        return 0

    lax.fori_loop(0, 4, finish_pair, 0)

    def finish(d, _):
        j = lax.rem(chip + d, 8)
        copy_p(j).wait_send()
        to = lax.rem(g + d, 8)
        copy_w(to).wait_send()
        copy_h(to).wait_send()
        copy_z(to).wait_send()
        copy_d(to).wait_send()
        copy_v(to).wait_send()
        copy_y(to).wait_send()
        return 0

    lax.fori_loop(1, 8, finish, 0)

    def finish_rows(d, _):
        for row in range(2):
            j = 4 * row + lax.rem(x + d, 4)
            copy_1(j).wait_send()
            copy_2(j).wait_send()
        return 0

    lax.fori_loop(1, 4, finish_rows, 0)
    copy_s.wait_send()
    copy_t(rows[0]).wait_send()

    @pl.when(own_row == 0)
    def _():
        copy_t(0).wait_send()


def per_device(
    queries, keys, values, prefill_decay, start_states, resident_states, slot_of_prompt,
    decode_queries, decode_keys, decode_values, decode_gate, decode_decay, norm_gain, out_weight,
):
    dma = pltpu.SemaphoreType.DMA
    hbm, vmem = pl.BlockSpec(memory_space=pl.ANY), pl.BlockSpec(memory_space=pltpu.VMEM)
    results = (
        jax.ShapeDtypeStruct((T, H, HS), BF16),
        jax.ShapeDtypeStruct((64, 2, 16, HS), F32),
        jax.ShapeDtypeStruct((2, 6144), F32),
    )
    prefill_out, cache, decoded = pl.pallas_call(
        kernel,
        name="lightning",
        out_shape=tuple(pltpu.VMEM(x.shape, x.dtype) for x in results),
        in_specs=[pl.BlockSpec(memory_space=pltpu.SMEM), hbm, hbm, hbm, vmem, vmem, vmem, hbm] + [vmem] * 6,
        out_specs=(vmem, vmem, vmem),
        scratch_shapes=[
            pltpu.VMEM((2, 2, T, 16, HS), BF16),
            pltpu.VMEM((H, T, HS), BF16),
            pltpu.VMEM((H, HS, T), BF16),
            pltpu.VMEM((H, T, HS), BF16),
            pltpu.VMEM((H, T), F32),
            pltpu.VMEM((H, T), F32),
            pltpu.VMEM((T, HS), F32),
            pltpu.VMEM((2, 16, ROWS, HS), F32),
            pltpu.VMEM((16, ROWS, HS), F32),
            pltpu.VMEM((8, 2, ROWS, HS), F32),
            pltpu.VMEM((8, 2, ROWS, HS), F32),
            pltpu.VMEM((8, 2, HS, HS), F32),
            pltpu.VMEM((8, 2, HS, HS), F32),
            pltpu.VMEM((16, HS, HS), F32),
            pltpu.VMEM((2, 16, HS, HS), F32),
            pltpu.VMEM((2, HS, HS), F32),
            pltpu.VMEM((8, 2, 16, HS), F32),
            pltpu.VMEM((8, 2, 16, HS), F32),
            pltpu.VMEM((8, 32, 768), F32),
            pltpu.VMEM((8, 32, 768), F32),
            pltpu.VMEM((256, 768), BF16),
            pltpu.VMEM((H, T, HS), F32),
            pltpu.VMEM((H, HS, 2 * HS), BF16),
            pltpu.VMEM((72, 2, 16, HS), F32),
            pltpu.VMEM((256, HS), F32),
            pltpu.VMEM((40, 256), F32),
            pltpu.VMEM((8, 40, 256), F32),
            pltpu.VMEM((2, 8, 16, 896), F32),
            pltpu.VMEM((8, 16, 896), F32),
            pltpu.VMEM((8, 16, 896), F32),
            pltpu.VMEM((8, 2, 768), F32),
            pltpu.VMEM((8, 2, 768), F32),
            pltpu.VMEM((4, 2, 16, 64), F32),
            pltpu.VMEM((8, 16, HS), F32),
            pltpu.VMEM((8, 16, HS), F32),
            pltpu.VMEM((16, HS), F32),
            pltpu.VMEM((8, 16, HS), F32),
            pltpu.VMEM((3, 256, HS), BF16),
            pltpu.VMEM((2, 2, ROWS, HS), F32),
            pltpu.VMEM((2, 2, ROWS, HS), F32),
            pltpu.VMEM((2, 2, HS, HS), F32),
            pltpu.VMEM((2, 2, HS, HS), F32),
            dma((3, 2)), dma,
            dma((2,)), dma((2,)), dma((8,)), dma((8,)), dma((8,)), dma((8,)),
            dma((4,)), dma((4,)), dma((8,)), dma((8,)), dma((8,)), dma((8,)),
            dma((8,)), dma((8,)), dma, dma, dma((8,)), dma((8,)), dma((8,)), dma((8,)),
            dma((8,)), dma((8,)), dma((8,)), dma((8,)), dma((2,)), dma((2,)), dma, dma,
        ],
        compiler_params=pltpu.CompilerParams(
            collective_id=0, has_side_effects=True, vmem_limit_bytes=VMEM_LIMIT
        ),
    )(
        slot_of_prompt,
        queries[0],
        keys[0],
        values[0],
        jnp.swapaxes(prefill_decay[0], 0, 1),
        start_states[0],
        out_weight.reshape(32, 6144),
        jnp.swapaxes(resident_states, 2, 3),
        decode_queries,
        decode_keys,
        jnp.transpose(decode_values, (1, 2, 3, 0)),
        jnp.transpose(decode_gate, (1, 2, 3, 0)),
        jnp.transpose(decode_decay, (1, 2, 0)).reshape(8, 64),
        norm_gain,
    )
    return prefill_out[None], jnp.swapaxes(cache, 2, 3), decoded


def solution(mesh):
    return jax.shard_map(
        per_device,
        mesh=mesh,
        in_specs=(
            P("grp", "ctx", None, None),
            P("grp", "ctx", None, None),
            P("grp", "ctx", None, None),
            P("grp", "ctx", None),
            P("grp", "ctx", None, None),
            P(None, "ctx", None, "grp"),
            P(),
            P(None, None, "ctx", None),
            P(None, None, "ctx", None),
            P(None, None, "ctx", "grp"),
            P(None, None, "ctx", "grp"),
            P(None, None, "ctx"),
            P("ctx", "grp"),
            P("ctx", "grp", None),
        ),
        out_specs=(
            P("grp", "ctx", None, None),
            P(None, "ctx", None, "grp"),
            P(("ctx", "grp"), None),
        ),
        check_vma=False,
    )
```

```python
import jax
import jax.numpy as jnp
from jax import lax
from jax.experimental import pallas as pl
from jax.experimental.pallas import tpu as pltpu
from jax.sharding import PartitionSpec as P

H = 32
HS = 128
LOG2E = 1.4426950408889634
MESH = pl.DeviceIdType.MESH
F32 = jnp.float32
BF16 = jnp.bfloat16
VMEM_LIMIT = 54 * 1024 * 1024
T = 512
CH = 128
ROWS = 136
HEADS_AT_SCAN = 8
HEADS_AT_GATHER = 16
HEADS_AT_SUM = 20
UNROLL = 4


def dot(a, b):
    return lax.dot_general(a, b, (((1,), (0,)), ((), ())), preferred_element_type=F32)


def split(x):
    hi = x.astype(BF16)
    return hi, (x - hi.astype(F32)).astype(BF16)


def head_of(half, i):
    return 4 * lax.div(i, 2) + 2 * half + lax.rem(i, 2)


def remote(src, dst, send, recv, where):
    return pltpu.make_async_remote_copy(
        src_ref=src, dst_ref=dst, send_sem=send, recv_sem=recv, device_id=where, device_id_type=MESH
    )


def kernel(
    slot_ref, q_hbm, k_hbm, v_hbm, dec_ref, start_ref, w_ref, cache_hbm, dq_ref, dk_ref, dv_ref, gate_ref, decay_ref, gain_ref,
    out_ref, new_ref, decoded_ref,
    raw, qh, kt, vh, cum2, cum, ec, s_ref, xbuf, tbuf, rbuf, pbuf, qbuf, obuf, states, pcur, fbuf, hbuf, wf, wr, wt, att,
    wide, cache, zrow, zmine, zbuf, part, half, take, done, last,
    gated, given, taken, ymine, ybuf, place, row_total, twin_total, start_all, row_start,
    load_sem, cache_sem, sa, ra, s1, r1, s2, r2, sb, rb, sh, rh, sw, rw, sz, rz, sc, rc, sp, rp, sd, rd, sv, rv, sy, ry, st, rt, ss, rs,
):
    c, g = lax.axis_index("ctx"), lax.axis_index("grp")
    core, chip = lax.rem(c, 2), lax.div(c, 2)
    other = 1 - core
    partner = (2 * chip + other, g)

    def peer(j):
        return (2 * j + core, g)

    x, own_row = lax.rem(chip, 4), lax.div(chip, 4)
    rows = (1 - own_row, own_row)
    twin = peer(4 * rows[0] + x)

    def in_row(j):
        return peer(4 * own_row + lax.rem(j, 4))

    def mine_of(j):
        return 4 * lax.div(j, 4) + x

    def load(which, hbm, row, at):
        heads = pl.ds(pl.multiple_of(16 * row, 16), 16)
        span = pl.ds(at * CH, CH)
        return pltpu.make_async_copy(
            hbm.at[span, heads], raw.at[which % 2, row, span], load_sem.at[which, row, at]
        )

    for row in rows:
        for at in range(T // CH):
            load(1, v_hbm, row, at).start()
            load(0, k_hbm, row, at).start()
    cache_load = pltpu.make_async_copy(cache_hbm, cache.at[pl.ds(0, 64)], cache_sem)
    cache_load.start()

    bar = pltpu.get_barrier_semaphore()
    pl.semaphore_signal(bar, inc=1, device_id=partner, device_id_type=MESH)

    def greet(d, _):
        pl.semaphore_signal(bar, inc=1, device_id=peer(lax.rem(chip + d, 8)), device_id_type=MESH)
        pl.semaphore_signal(bar, inc=1, device_id=(c, lax.rem(g + d, 8)), device_id_type=MESH)
        return 0

    lax.fori_loop(1, 8, greet, 0)

    lane = lax.broadcasted_iota(jnp.int32, (H, T), 1)
    total = dec_ref[...]
    step = 1
    while step < T:
        total = total + jnp.where(lane >= step, pltpu.roll(total, step, 1), 0.0)
        step *= 2
    cum[...] = total
    cum2[...] = total * LOG2E
    ec[...] = jnp.concatenate([jnp.exp(total), jnp.zeros((HS - H, T), F32)], axis=0).T

    def heads_first(which, row, at):
        return jnp.swapaxes(raw[which % 2, row, pl.ds(at * CH, CH)], 0, 1)

    def relay_kv(row):
        def chunk(at, _):
            load(1, v_hbm, row, at).wait()
            load(0, k_hbm, row, at).wait()
            span = pl.ds(pl.multiple_of(at * CH, CH), CH)
            vh[pl.ds(16 * row, 16), span, :] = heads_first(1, row, at)
            block = heads_first(0, row, at)
            for h in range(16):
                kt[16 * row + h, :, span] = block[h].T
            return 0

        lax.fori_loop(0, T // CH, chunk, 0)

    def local_state(half, i):
        h = head_of(half, i)
        row = cum[pl.ds(h, 1), :]
        end = row[:, T - 1 : T]
        hi, lo = split(kt[h].astype(F32) * jnp.exp(end - row))
        both = dot(jnp.concatenate([hi, lo], axis=0), vh[h])
        s_ref[half, i, 0:HS, :] = both[:HS] + both[HS:]
        s_ref[half, i, HS:ROWS, :] = jnp.broadcast_to(end, (ROWS - HS, HS))

    def copy_a(row):
        part = pl.ds(8 * row, 8)
        return remote(s_ref.at[other, part], xbuf.at[part], sa.at[row], ra.at[row], partner)

    def copy_1(j):
        return remote(tbuf.at[j], rbuf.at[mine_of(j)], s1.at[j], r1.at[mine_of(j)], in_row(j))

    def arrival_1(j):
        return remote(tbuf.at[j], rbuf.at[j], s1.at[j], r1.at[j], in_row(j))

    def chip_total(j):
        for r in range(2):
            i = 2 * j + r
            mine, theirs = s_ref[core, i], xbuf[i]
            end_mine, end_theirs = mine[HS : HS + 1], theirs[HS : HS + 1]
            on_mine = jnp.where(core == 0, jnp.exp(end_theirs), 1.0)
            on_theirs = jnp.where(core == 0, 1.0, jnp.exp(end_mine))
            tbuf[j, r, 0:HS, :] = on_mine * mine[:HS] + on_theirs * theirs[:HS]
            tbuf[j, r, HS:ROWS, :] = mine[HS:] + theirs[HS:]

    def send_total(row):
        def one(d, _):
            j = 4 * row + lax.rem(x + d, 4)
            chip_total(j)
            copy_1(j).start()
            return 0

        return one

    def local_states(row):
        for i in range(8):
            local_state(other, 8 * row + i)
        copy_a(row).start()
        for i in range(8):
            local_state(core, 8 * row + i)

    pl.semaphore_wait(bar, 15)
    for to in range(8):
        wf[to] = w_ref[:, to * 768 : (to + 1) * 768].astype(F32)

    def copy_w(to):
        return remote(wf.at[to], wr.at[g], sw.at[to], rw.at[g], (c, to))

    def arrival_w(frm):
        return remote(wf.at[frm], wr.at[frm], sw.at[frm], rw.at[frm], (c, frm))

    def send_w(d, _):
        copy_w(lax.rem(g + d, 8)).start()
        return 0

    def send_w_odd(n, _):
        return send_w(2 * n + 1, 0)

    def send_w_even(n, _):
        return send_w(2 * n, 0)

    lax.fori_loop(0, 4, send_w_odd, 0)
    lax.fori_loop(1, 4, send_w_even, 0)
    copy_s = remote(start_ref, start_all.at[own_row], ss, rs, twin)
    copy_s.start()
    start_all[own_row] = start_ref[...]
    wr[g] = wf[g]

    relay_kv(rows[0])
    for at in range(T // CH):
        load(2, q_hbm, rows[0], at).start()
    local_states(rows[0])
    relay_kv(rows[1])
    for at in range(T // CH):
        load(2, q_hbm, rows[1], at).start()
    copy_a(rows[0]).wait_recv()
    lax.fori_loop(1, 4, send_total(rows[0]), 0)
    local_states(rows[1])
    copy_a(rows[1]).wait_recv()
    lax.fori_loop(1, 4, send_total(rows[1]), 0)
    for row in rows:
        chip_total(4 * row + x)
        rbuf[4 * row + x] = tbuf[4 * row + x]

    def fold(row):
        for d in range(1, 4):
            arrival_1(4 * row + lax.rem(x + d, 4)).wait_recv()
        for r in range(2):
            total = rbuf[4 * row, r]
            for n in range(1, 4):
                term = rbuf[4 * row + n, r]
                total = jnp.concatenate(
                    [jnp.exp(term[HS : HS + 1]) * total[:HS] + term[:HS], total[HS:] + term[HS:]], axis=0
                )
            row_total[row, r] = total

    def copy_t(row):
        return remote(row_total.at[row], twin_total.at[row], st.at[row], rt.at[row], twin)

    for row in rows:

        def relay_q(at, _):
            load(2, q_hbm, row, at).wait()
            span = pl.ds(pl.multiple_of(at * CH, CH), CH)
            qh[pl.ds(16 * row, 16), span, :] = heads_first(2, row, at)
            return 0

        lax.fori_loop(0, T // CH, relay_q, 0)

    lane = lax.broadcasted_iota(jnp.int32, (16, 64), 1)
    wide_lane = lax.broadcasted_iota(jnp.int32, (16, HS), 1)
    diagonal = lax.broadcasted_iota(jnp.int32, (16, 16), 0) == lax.broadcasted_iota(jnp.int32, (16, 16), 1)
    for h in range(2):
        spread_gain = jnp.broadcast_to(gain_ref[h : h + 1, :], (16, 16))
        gain = jnp.sum(jnp.where(diagonal, spread_gain, 0.0), axis=1, keepdims=True)
        for i in range(4):
            gated[i, h] = gain * jax.nn.sigmoid(gate_ref[i, h].astype(F32))

    def give(p, _):
        here = lane == slot_ref[p]
        message = jnp.zeros((16, HS), F32)
        for h in range(2):
            for i in range(4):
                value = jnp.sum(jnp.where(here, dv_ref[i, h].astype(F32), 0.0), axis=1, keepdims=True)
                factor = jnp.sum(jnp.where(here, gated[i, h], 0.0), axis=1, keepdims=True)
                message = jnp.where(wide_lane == 4 * h + i, value, message)
                message = jnp.where(wide_lane == 8 + 4 * h + i, factor, message)
        given[p] = message
        return 0

    lax.fori_loop(0, 8, give, 0)

    def copy_v(to):
        return remote(given.at[to], taken.at[g], sv.at[to], rv.at[g], (c, to))

    def arrival_v(frm):
        return remote(given.at[frm], taken.at[frm], sv.at[frm], rv.at[frm], (c, frm))

    def send_v(d, _):
        copy_v(lax.rem(g + d, 8)).start()
        return 0

    lax.fori_loop(1, 8, send_v, 0)
    taken[g] = given[g]

    pick = lax.broadcasted_iota(jnp.int32, (8, 64), 1)
    scale = jnp.exp(decay_ref[...])

    def decode_row(at, s, ys):
        here = lane == s
        q, k = dq_ref[s].astype(F32), dk_ref[s].astype(F32)
        factor = jnp.sum(jnp.where(pick == s, scale, 0.0), axis=1, keepdims=True)
        ys = list(ys)
        for h in range(2):
            state = cache[at, h]
            for i in range(4):
                value = jnp.sum(jnp.where(here, dv_ref[i, h].astype(F32), 0.0), axis=1, keepdims=True)
                state = factor[2 * i + h : 2 * i + h + 1] * state + value * k[i, h : h + 1, :]
                if ys:
                    y = jnp.sum(state * q[i, h : h + 1, :], axis=1, keepdims=True)
                    ys[2 * i + h] = jnp.where(here, y, ys[2 * i + h])
            cache[at, h] = state
        return tuple(ys)

    cache_load.wait()
    ys = lax.fori_loop(
        0, 32, lambda s, ys: decode_row(s, s, ys), tuple(jnp.zeros((16, 64), F32) for _ in range(8)), unroll=2
    )
    fold(rows[0])
    copy_t(rows[0]).start()
    ys = lax.fori_loop(32, 64, lambda s, ys: decode_row(s, s, ys), ys, unroll=2)
    fresh = lane < 64
    for p in range(8):
        fresh = jnp.logical_and(fresh, lane != slot_ref[p])
    for i in range(4):
        squares = jnp.zeros((1, 64), F32)
        parts = []
        for h in range(2):
            y = jnp.where(fresh, ys[2 * i + h], 0.0)
            squares = squares + jnp.sum(y * y, axis=0, keepdims=True)
            parts.append(y * gated[i, h])
        parts.append(jnp.broadcast_to(squares, (8, 64)))
        parts.append(jnp.zeros((HS - 40, 64), F32))
        zrow[pl.ds(i, 64, stride=4), :] = jnp.concatenate(parts, axis=0).T
    zmine[...] = zrow[...].T[:40]

    def copy_z(to):
        return remote(zmine, zbuf.at[g], sz.at[to], rz.at[g], (c, to))

    def arrival_z(frm):
        return remote(zmine, zbuf.at[frm], sz.at[frm], rz.at[frm], (c, frm))

    def send_z(d, _):
        copy_z(lax.rem(g + d, 8)).start()
        return 0

    lax.fori_loop(1, 8, send_z, 0)
    zbuf[g] = zmine[...]

    to_row = lax.broadcasted_iota(jnp.int32, (256, HS), 0)
    from_row = lax.broadcasted_iota(jnp.int32, (256, HS), 1)
    target = jnp.zeros((256, HS), jnp.int32)
    for p in range(8):
        target = jnp.where(lax.div(from_row, 16) == p, 4 * slot_ref[p], target)
    hit = to_row == target + lax.rem(from_row, 4)
    for n in range(3):
        kind = lax.rem(lax.div(from_row, 4), 4) == n
        place[n] = jnp.where(jnp.logical_and(hit, kind), 1.0, 0.0).astype(BF16)

    causal = lax.broadcasted_iota(jnp.int32, (HS, HS), 0) >= lax.broadcasted_iota(jnp.int32, (HS, HS), 1)

    def attend(h):
        row = cum2[pl.ds(h, 1), :]
        col = jnp.broadcast_to(row, (HS, T)).T
        left = dot(qh[h], kt[h, :, 0:256])
        right = dot(qh[h, 256:512, :], kt[h, :, 256:512])

        def weigh(a, b):
            scores = left if b < 2 else right
            first = a if b < 2 else a - 2
            part = scores[first * HS : (first + 1) * HS, (b % 2) * HS : (b % 2 + 1) * HS]
            diff = col[a * HS : (a + 1) * HS] - row[:, b * HS : (b + 1) * HS]
            if a == b:
                diff = jnp.where(causal, diff, -1e30)
            return (part * jnp.exp2(diff)).astype(BF16)

        v = vh[h]
        none = jnp.zeros((HS, HS), BF16)
        top = jnp.concatenate([
            jnp.concatenate([weigh(0, 0), none], axis=1),
            jnp.concatenate([weigh(1, 0), weigh(1, 1)], axis=1),
        ], axis=0)
        low = jnp.concatenate([
            jnp.concatenate([weigh(2, 0), weigh(2, 1), weigh(2, 2), none], axis=1),
            jnp.concatenate([weigh(3, 0), weigh(3, 1), weigh(3, 2), weigh(3, 3)], axis=1),
        ], axis=0)
        att[h, 0:256, :] = dot(top, v[0:256])
        att[h, 256:512, :] = dot(low, v)

    def some(n, _):
        for u in range(UNROLL):
            attend(UNROLL * n + u)
        return 0

    lax.fori_loop(0, HEADS_AT_SCAN // UNROLL, some, 0)

    def copy_2(j):
        return remote(pbuf.at[j], qbuf.at[mine_of(j)], s2.at[j], r2.at[mine_of(j)], in_row(j))

    def arrival_2(j):
        return remote(pbuf.at[j], qbuf.at[j], s2.at[j], r2.at[j], in_row(j))

    fold(rows[1])

    @pl.when(own_row == 0)
    def _():
        copy_t(0).start()

    copy_t(own_row).wait_recv()

    def through(total, state):
        return jnp.exp(total[HS : HS + 1]) * state + total[:HS]

    for r in range(2):

        @pl.when(own_row == 0)
        def _():
            pcur[r] = through(twin_total[own_row, r], through(row_total[own_row, r], start_ref[r]))

        @pl.when(own_row == 1)
        def _():
            pcur[r] = through(row_total[own_row, r], through(twin_total[own_row, r], start_ref[r]))

    def wait_v(d, _):
        arrival_v(lax.rem(g + d, 8)).wait_recv()
        return 0

    lax.fori_loop(1, 8, wait_v, 0)
    columns = jnp.concatenate([taken[n] for n in range(8)], axis=0)
    mine = slot_ref[g]
    q, k = dq_ref[mine].astype(F32), dk_ref[mine].astype(F32)
    step_scale = jnp.sum(jnp.where(pick == mine, scale, 0.0), axis=1, keepdims=True)
    tall_lane = lax.broadcasted_iota(jnp.int32, (HS, HS), 1)
    tall = jnp.zeros((HS, HS), F32)
    for h in range(2):
        state = pcur[h].T
        fbuf[:, h] = state.reshape(8, 16, HS)
        for i in range(4):
            n = 4 * h + i
            state = step_scale[2 * i + h : 2 * i + h + 1] * state + columns[:, n : n + 1] * k[i, h : h + 1, :]
            y = jnp.sum(state * q[i, h : h + 1, :], axis=1, keepdims=True)
            tall = jnp.where(tall_lane == n, y * columns[:, 8 + n : 9 + n], tall)
            squares = jnp.sum(y * y, axis=0, keepdims=True)
            tall = jnp.where(tall_lane == 8 + i, tall + squares, tall)
    ymine[...] = tall.T[:16]

    def copy_y(to):
        return remote(ymine, ybuf.at[g], sy.at[to], ry.at[g], (c, to))

    def arrival_y(frm):
        return remote(ymine, ybuf.at[frm], sy.at[frm], ry.at[frm], (c, frm))

    def send_y(d, _):
        copy_y(lax.rem(g + d, 8)).start()
        return 0

    lax.fori_loop(1, 8, send_y, 0)

    remote(start_ref, start_all.at[rows[0]], ss, rs, twin).wait_recv()

    @pl.when(own_row == 0)
    def _():
        row_start[...] = start_all[...]

    @pl.when(own_row == 1)
    def _():
        copy_t(0).wait_recv()
        for row in range(2):
            for r in range(2):
                row_start[row, r] = through(twin_total[row, r], start_all[row, r])

    def before_chip(j, _):
        row = lax.div(j, 4)
        pbuf[j] = row_start[row]

        @pl.when(lax.rem(j, 4) != x)
        def _():
            copy_2(j).start()

        for r in range(2):
            row_start[row, r] = through(rbuf[j, r], row_start[row, r])
        return 0

    lax.fori_loop(0, 8, before_chip, 0)
    for row in range(2):
        qbuf[4 * row + x] = pbuf[4 * row + x]
    ybuf[g] = ymine[...]

    def copy_h(to):
        return remote(fbuf.at[to], hbuf.at[g], sh.at[to], rh.at[g], (c, to))

    def arrival_h(frm):
        return remote(fbuf.at[frm], hbuf.at[frm], sh.at[frm], rh.at[frm], (c, frm))

    def send_h(d, _):
        copy_h(lax.rem(g + d, 8)).start()
        return 0

    lax.fori_loop(1, 8, send_h, 0)
    hbuf[g] = fbuf[g]

    def wait_z(d, _):
        frm = lax.rem(g + d, 8)
        arrival_z(frm).wait_recv()
        arrival_w(frm).wait_recv()
        return 0

    lax.fori_loop(1, 8, wait_z, 0)
    for h in range(2):
        for frm in range(8):
            at = h * HS + frm * 16
            wt[at : at + 16, :] = wr[frm, h * 16 : (h + 1) * 16, :].astype(BF16)
    z = jnp.concatenate([zbuf[n, 16 * h : 16 * h + 16, :] for h in range(2) for n in range(8)], axis=0).T
    squares = zbuf[0, 32:40, :]
    for n in range(1, 8):
        squares = squares + zbuf[n, 32:40, :]
    squares = jnp.concatenate([squares] * 16, axis=0).T
    hi, lo = split(z)
    for n in range(3):
        span = slice(n * 256, (n + 1) * 256)
        w = wt[:, span]
        both = (dot(hi, w) + dot(lo, w)).reshape(8, 2, 16, 256)
        for k in range(2):
            part[k, :, :, span] = both[:, k]
    both = squares.reshape(8, 2, 16, HS)
    for k in range(2):
        part[k, :, :, 768:896] = both[:, k]
    lax.fori_loop(HEADS_AT_SCAN // UNROLL, HEADS_AT_GATHER // UNROLL, some, 0)

    def wait_y(d, _):
        arrival_y(lax.rem(g + d, 8)).wait_recv()
        return 0

    lax.fori_loop(1, 8, wait_y, 0)
    hi, lo = split(ybuf[...].reshape(HS, HS))
    squares = (dot(place[2], hi) + dot(place[2], lo)).reshape(8, 2, 16, HS)
    hi = [dot(place[h], hi).astype(BF16) for h in range(2)]
    lo = [dot(place[h], lo).astype(BF16) for h in range(2)]
    z = jnp.concatenate([jnp.concatenate(hi, axis=1), jnp.concatenate(lo, axis=1)], axis=0)
    for n in range(3):
        span = slice(n * 256, (n + 1) * 256)
        both = dot(z, wt[:, span])
        both = (both[:256] + both[256:]).reshape(8, 2, 16, 256)
        for k in range(2):
            part[k, :, :, span] = part[k, :, :, span] + both[:, k]
    for k in range(2):
        part[k, :, :, 768:896] = part[k, :, :, 768:896] + squares[:, k]
    copy_c = remote(part.at[other], half, sc, rc, partner)
    copy_c.start()
    lax.fori_loop(HEADS_AT_GATHER // UNROLL, HEADS_AT_SUM // UNROLL, some, 0)

    def copy_b(m):
        return remote(obuf.at[pl.ds(4 * m, 4)], states.at[core, pl.ds(4 * m, 4)], sb.at[m], rb.at[m], partner)

    def arrival_b(m):
        return remote(obuf.at[pl.ds(4 * m, 4)], states.at[other, pl.ds(4 * m, 4)], sb.at[m], rb.at[m], partner)

    def spread(m, _):
        for n in range(2):
            j = 2 * m + n

            @pl.when(lax.rem(j, 4) != x)
            def _():
                arrival_2(j).wait_recv()

            for r in range(2):
                i = 2 * j + r
                before = qbuf[j, r]
                first = jnp.where(core == 0, s_ref[core, i], xbuf[i])
                after = jnp.exp(first[HS : HS + 1]) * before + first[:HS]
                states[core, i] = jnp.where(core == 0, before, after)
                obuf[i] = jnp.where(core == 0, after, before)
        copy_b(m).start()
        return 0

    copy_c.wait_recv()
    half[...] = half[...] + part[core]

    def copy_p(to):
        return remote(half.at[to], take.at[chip], sp.at[to], rp.at[chip], peer(to))

    def arrival_p(frm):
        return remote(half.at[frm], take.at[frm], sp.at[frm], rp.at[frm], peer(frm))

    def send_p(d, _):
        copy_p(lax.rem(chip + d, 8)).start()
        return 0

    lax.fori_loop(1, 8, send_p, 0)
    take[chip] = half[chip]
    lax.fori_loop(HEADS_AT_SUM // UNROLL, H // UNROLL, some, 0)
    lax.fori_loop(0, 4, spread, 0)

    def take_b(m, _):
        arrival_b(m).wait_recv()
        return 0

    lax.fori_loop(0, 4, take_b, 0)
    for h in range(H):
        hi, lo = split(states[(h // 2) % 2, 2 * (h // 4) + h % 2])
        wide[h, :, 0:HS] = hi
        wide[h, :, HS:] = lo

    def finish_chunk(at):
        span = slice(at * CH, (at + 1) * CH)
        squares = jnp.zeros((CH, HS), F32)
        for h in range(H):
            both = dot(qh[h, span, :], wide[h])
            field = att[h, span, :] + (both[:, :HS] + both[:, HS:]) * ec[span, h : h + 1]
            att[h, span, :] = field
            squares = squares + field * field
        mean = jnp.sum(squares, axis=1, keepdims=True) / (H * HS)
        factor = jnp.broadcast_to(lax.rsqrt(mean + 1e-06), (CH, HS))
        out_ref[span] = jnp.swapaxes((att[:, span, :] * factor[None]).astype(BF16), 0, 1)

    for at in range(2):
        finish_chunk(at)

    def wait_p(d, _):
        arrival_p(lax.rem(chip + d, 8)).wait_recv()
        return 0

    lax.fori_loop(1, 8, wait_p, 0)
    total = take[0]
    for n in range(1, 8):
        total = total + take[n]
    total = total[:, :768] * lax.rsqrt(total[:, 768:769] / (H * HS) + 1e-06)
    for n in range(8):
        done[n] = total[2 * n : 2 * n + 2]

    def copy_d(to):
        return remote(done.at[to], last.at[g], sd.at[to], rd.at[g], (c, to))

    def arrival_d(frm):
        return remote(done.at[frm], last.at[frm], sd.at[frm], rd.at[frm], (c, frm))

    def send_d(d, _):
        copy_d(lax.rem(g + d, 8)).start()
        return 0

    lax.fori_loop(1, 8, send_d, 0)
    last[g] = done[g]

    for at in range(2, T // CH):
        finish_chunk(at)

    def take_h(d, _):
        arrival_h(lax.rem(g + d, 8)).wait_recv()
        return 0

    lax.fori_loop(1, 8, take_h, 0)
    cache[64:72] = hbuf[...]
    lax.fori_loop(0, 8, lambda p, ys: decode_row(64 + p, slot_ref[p], ys), ())

    def merge(s, _):
        at = s
        for p in range(8):
            at = jnp.where(slot_ref[p] == s, 64 + p, at)
        new_ref[s] = cache[at]
        return 0

    lax.fori_loop(0, 64, merge, 0)

    def wait_d(d, _):
        arrival_d(lax.rem(g + d, 8)).wait_recv()
        return 0

    lax.fori_loop(1, 8, wait_d, 0)
    for n in range(8):
        decoded_ref[:, n * 768 : (n + 1) * 768] = last[n]

    for row in rows:
        copy_a(row).wait_send()
    copy_c.wait_send()

    def finish_pair(m, _):
        copy_b(m).wait_send()
        return 0

    lax.fori_loop(0, 4, finish_pair, 0)

    def finish(d, _):
        j = lax.rem(chip + d, 8)
        copy_p(j).wait_send()
        to = lax.rem(g + d, 8)
        copy_w(to).wait_send()
        copy_h(to).wait_send()
        copy_z(to).wait_send()
        copy_d(to).wait_send()
        copy_v(to).wait_send()
        copy_y(to).wait_send()
        return 0

    lax.fori_loop(1, 8, finish, 0)

    def finish_rows(d, _):
        for row in range(2):
            j = 4 * row + lax.rem(x + d, 4)
            copy_1(j).wait_send()
            copy_2(j).wait_send()
        return 0

    lax.fori_loop(1, 4, finish_rows, 0)
    copy_s.wait_send()
    copy_t(rows[0]).wait_send()

    @pl.when(own_row == 0)
    def _():
        copy_t(0).wait_send()


def per_device(
    queries, keys, values, prefill_decay, start_states, resident_states, slot_of_prompt,
    decode_queries, decode_keys, decode_values, decode_gate, decode_decay, norm_gain, out_weight,
):
    dma = pltpu.SemaphoreType.DMA
    hbm, vmem = pl.BlockSpec(memory_space=pl.ANY), pl.BlockSpec(memory_space=pltpu.VMEM)
    results = (
        jax.ShapeDtypeStruct((T, H, HS), BF16),
        jax.ShapeDtypeStruct((64, 2, 16, HS), F32),
        jax.ShapeDtypeStruct((2, 6144), F32),
    )
    prefill_out, cache, decoded = pl.pallas_call(
        kernel,
        name="lightning",
        out_shape=tuple(pltpu.VMEM(x.shape, x.dtype) for x in results),
        in_specs=[pl.BlockSpec(memory_space=pltpu.SMEM), hbm, hbm, hbm, vmem, vmem, vmem, hbm] + [vmem] * 6,
        out_specs=(vmem, vmem, vmem),
        scratch_shapes=[
            pltpu.VMEM((2, 2, T, 16, HS), BF16),
            pltpu.VMEM((H, T, HS), BF16),
            pltpu.VMEM((H, HS, T), BF16),
            pltpu.VMEM((H, T, HS), BF16),
            pltpu.VMEM((H, T), F32),
            pltpu.VMEM((H, T), F32),
            pltpu.VMEM((T, HS), F32),
            pltpu.VMEM((2, 16, ROWS, HS), F32),
            pltpu.VMEM((16, ROWS, HS), F32),
            pltpu.VMEM((8, 2, ROWS, HS), F32),
            pltpu.VMEM((8, 2, ROWS, HS), F32),
            pltpu.VMEM((8, 2, HS, HS), F32),
            pltpu.VMEM((8, 2, HS, HS), F32),
            pltpu.VMEM((16, HS, HS), F32),
            pltpu.VMEM((2, 16, HS, HS), F32),
            pltpu.VMEM((2, HS, HS), F32),
            pltpu.VMEM((8, 2, 16, HS), F32),
            pltpu.VMEM((8, 2, 16, HS), F32),
            pltpu.VMEM((8, 32, 768), F32),
            pltpu.VMEM((8, 32, 768), F32),
            pltpu.VMEM((256, 768), BF16),
            pltpu.VMEM((H, T, HS), F32),
            pltpu.VMEM((H, HS, 2 * HS), BF16),
            pltpu.VMEM((72, 2, 16, HS), F32),
            pltpu.VMEM((256, HS), F32),
            pltpu.VMEM((40, 256), F32),
            pltpu.VMEM((8, 40, 256), F32),
            pltpu.VMEM((2, 8, 16, 896), F32),
            pltpu.VMEM((8, 16, 896), F32),
            pltpu.VMEM((8, 16, 896), F32),
            pltpu.VMEM((8, 2, 768), F32),
            pltpu.VMEM((8, 2, 768), F32),
            pltpu.VMEM((4, 2, 16, 64), F32),
            pltpu.VMEM((8, 16, HS), F32),
            pltpu.VMEM((8, 16, HS), F32),
            pltpu.VMEM((16, HS), F32),
            pltpu.VMEM((8, 16, HS), F32),
            pltpu.VMEM((3, 256, HS), BF16),
            pltpu.VMEM((2, 2, ROWS, HS), F32),
            pltpu.VMEM((2, 2, ROWS, HS), F32),
            pltpu.VMEM((2, 2, HS, HS), F32),
            pltpu.VMEM((2, 2, HS, HS), F32),
            dma((3, 2, T // CH)), dma,
            dma((2,)), dma((2,)), dma((8,)), dma((8,)), dma((8,)), dma((8,)),
            dma((4,)), dma((4,)), dma((8,)), dma((8,)), dma((8,)), dma((8,)),
            dma((8,)), dma((8,)), dma, dma, dma((8,)), dma((8,)), dma((8,)), dma((8,)),
            dma((8,)), dma((8,)), dma((8,)), dma((8,)), dma((2,)), dma((2,)), dma, dma,
        ],
        compiler_params=pltpu.CompilerParams(
            collective_id=0, has_side_effects=True, vmem_limit_bytes=VMEM_LIMIT
        ),
    )(
        slot_of_prompt,
        queries[0],
        keys[0],
        values[0],
        jnp.swapaxes(prefill_decay[0], 0, 1),
        start_states[0],
        out_weight.reshape(32, 6144),
        jnp.swapaxes(resident_states, 2, 3),
        decode_queries,
        decode_keys,
        jnp.transpose(decode_values, (1, 2, 3, 0)),
        jnp.transpose(decode_gate, (1, 2, 3, 0)),
        jnp.transpose(decode_decay, (1, 2, 0)).reshape(8, 64),
        norm_gain,
    )
    return prefill_out[None], jnp.swapaxes(cache, 2, 3), decoded


def solution(mesh):
    return jax.shard_map(
        per_device,
        mesh=mesh,
        in_specs=(
            P("grp", "ctx", None, None),
            P("grp", "ctx", None, None),
            P("grp", "ctx", None, None),
            P("grp", "ctx", None),
            P("grp", "ctx", None, None),
            P(None, "ctx", None, "grp"),
            P(),
            P(None, None, "ctx", None),
            P(None, None, "ctx", None),
            P(None, None, "ctx", "grp"),
            P(None, None, "ctx", "grp"),
            P(None, None, "ctx"),
            P("ctx", "grp"),
            P("ctx", "grp", None),
        ),
        out_specs=(
            P("grp", "ctx", None, None),
            P(None, "ctx", None, "grp"),
            P(("ctx", "grp"), None),
        ),
        check_vma=False,
    )
```

```python
import jax
import jax.numpy as jnp
from jax import lax
from jax.experimental import pallas as pl
from jax.experimental.pallas import tpu as pltpu
from jax.sharding import PartitionSpec as P

H = 32
HS = 128
LOG2E = 1.4426950408889634
MESH = pl.DeviceIdType.MESH
F32 = jnp.float32
BF16 = jnp.bfloat16
VMEM_LIMIT = 54 * 1024 * 1024
T = 512
CH = 128
ROWS = 136
HEADS_AT_SCAN = 8
HEADS_AT_GATHER = 16
HEADS_AT_SUM = 20
UNROLL = 4


def dot(a, b):
    return lax.dot_general(a, b, (((1,), (0,)), ((), ())), preferred_element_type=F32)


def split(x):
    hi = x.astype(BF16)
    return hi, (x - hi.astype(F32)).astype(BF16)


def head_of(half, i):
    return 4 * lax.div(i, 2) + 2 * half + lax.rem(i, 2)


def remote(src, dst, send, recv, where):
    return pltpu.make_async_remote_copy(
        src_ref=src, dst_ref=dst, send_sem=send, recv_sem=recv, device_id=where, device_id_type=MESH
    )


def kernel(
    slot_ref, q_hbm, k_hbm, v_hbm, dec_ref, start_ref, w_ref, cache_hbm, dq_ref, dk_ref, dv_ref, gate_ref, decay_ref, gain_ref,
    out_ref, new_ref, decoded_ref,
    raw, qh, kt, vh, cum2, cum, ec, s_ref, xbuf, tbuf, rbuf, pbuf, qbuf, obuf, states, pcur, fbuf, hbuf, wf, wr, wt, att,
    wide, cache, zrow, zmine, zbuf, part, half, take, done, last,
    gated, given, taken, ymine, ybuf, place, row_total, twin_total, start_all, row_start,
    load_sem, cache_sem, sa, ra, s1, r1, s2, r2, sb, rb, sh, rh, sw, rw, sz, rz, sc, rc, sp, rp, sd, rd, sv, rv, sy, ry, st, rt, ss, rs,
):
    c, g = lax.axis_index("ctx"), lax.axis_index("grp")
    core, chip = lax.rem(c, 2), lax.div(c, 2)
    other = 1 - core
    partner = (2 * chip + other, g)

    def peer(j):
        return (2 * j + core, g)

    x, own_row = lax.rem(chip, 4), lax.div(chip, 4)
    rows = (1 - own_row, own_row)
    twin = peer(4 * rows[0] + x)

    def in_row(j):
        return peer(4 * own_row + lax.rem(j, 4))

    def mine_of(j):
        return 4 * lax.div(j, 4) + x

    def load(which, hbm, row, at):
        heads = pl.ds(pl.multiple_of(16 * row, 16), 16)
        span = pl.ds(at * CH, CH)
        return pltpu.make_async_copy(
            hbm.at[span, heads], raw.at[which % 2, row, span], load_sem.at[which, row, at]
        )

    for row in rows:
        for at in range(T // CH):
            load(1, v_hbm, row, at).start()
            load(0, k_hbm, row, at).start()
    cache_load = pltpu.make_async_copy(cache_hbm, cache.at[pl.ds(0, 64)], cache_sem)
    cache_load.start()

    bar = pltpu.get_barrier_semaphore()
    pl.semaphore_signal(bar, inc=1, device_id=partner, device_id_type=MESH)

    def greet(d, _):
        pl.semaphore_signal(bar, inc=1, device_id=peer(lax.rem(chip + d, 8)), device_id_type=MESH)
        pl.semaphore_signal(bar, inc=1, device_id=(c, lax.rem(g + d, 8)), device_id_type=MESH)
        return 0

    lax.fori_loop(1, 8, greet, 0)

    lane = lax.broadcasted_iota(jnp.int32, (H, T), 1)
    total = dec_ref[...]
    step = 1
    while step < T:
        total = total + jnp.where(lane >= step, pltpu.roll(total, step, 1), 0.0)
        step *= 2
    cum[...] = total
    cum2[...] = total * LOG2E
    ec[...] = jnp.concatenate([jnp.exp(total), jnp.zeros((HS - H, T), F32)], axis=0).T

    def heads_first(which, row, at):
        return jnp.swapaxes(raw[which % 2, row, pl.ds(at * CH, CH)], 0, 1)

    def relay_kv(row):
        def chunk(at, _):
            load(1, v_hbm, row, at).wait()
            load(0, k_hbm, row, at).wait()
            span = pl.ds(pl.multiple_of(at * CH, CH), CH)
            vh[pl.ds(16 * row, 16), span, :] = heads_first(1, row, at)
            block = heads_first(0, row, at)
            for h in range(16):
                kt[16 * row + h, :, span] = block[h].T
            return 0

        lax.fori_loop(0, T // CH, chunk, 0)

    def local_state(half, i):
        h = head_of(half, i)
        row = cum[pl.ds(h, 1), :]
        end = row[:, T - 1 : T]
        hi, lo = split(kt[h].astype(F32) * jnp.exp(end - row))
        both = dot(jnp.concatenate([hi, lo], axis=0), vh[h])
        s_ref[half, i, 0:HS, :] = both[:HS] + both[HS:]
        s_ref[half, i, HS:ROWS, :] = jnp.broadcast_to(end, (ROWS - HS, HS))

    def copy_a(row):
        part = pl.ds(8 * row, 8)
        return remote(s_ref.at[other, part], xbuf.at[part], sa.at[row], ra.at[row], partner)

    def copy_1(j):
        return remote(tbuf.at[j], rbuf.at[mine_of(j)], s1.at[j], r1.at[mine_of(j)], in_row(j))

    def arrival_1(j):
        return remote(tbuf.at[j], rbuf.at[j], s1.at[j], r1.at[j], in_row(j))

    def chip_total(j):
        for r in range(2):
            i = 2 * j + r
            mine, theirs = s_ref[core, i], xbuf[i]
            end_mine, end_theirs = mine[HS : HS + 1], theirs[HS : HS + 1]
            on_mine = jnp.where(core == 0, jnp.exp(end_theirs), 1.0)
            on_theirs = jnp.where(core == 0, 1.0, jnp.exp(end_mine))
            tbuf[j, r, 0:HS, :] = on_mine * mine[:HS] + on_theirs * theirs[:HS]
            tbuf[j, r, HS:ROWS, :] = mine[HS:] + theirs[HS:]

    def send_total(row):
        def one(d, _):
            j = 4 * row + lax.rem(x + d, 4)
            chip_total(j)
            copy_1(j).start()
            return 0

        return one

    def local_states(row):
        for i in range(8):
            local_state(other, 8 * row + i)
        copy_a(row).start()
        for i in range(8):
            local_state(core, 8 * row + i)

    pl.semaphore_wait(bar, 15)
    for to in range(8):
        wf[to] = w_ref[:, to * 768 : (to + 1) * 768].astype(F32)

    def copy_w(to):
        return remote(wf.at[to], wr.at[g], sw.at[to], rw.at[g], (c, to))

    def arrival_w(frm):
        return remote(wf.at[frm], wr.at[frm], sw.at[frm], rw.at[frm], (c, frm))

    def send_w(d, _):
        copy_w(lax.rem(g + d, 8)).start()
        return 0

    def send_w_odd(n, _):
        return send_w(2 * n + 1, 0)

    def send_w_even(n, _):
        return send_w(2 * n, 0)

    lax.fori_loop(0, 4, send_w_odd, 0)
    lax.fori_loop(1, 4, send_w_even, 0)
    copy_s = remote(start_ref, start_all.at[own_row], ss, rs, twin)
    copy_s.start()
    start_all[own_row] = start_ref[...]
    wr[g] = wf[g]

    relay_kv(rows[0])
    for at in range(T // CH):
        load(2, q_hbm, rows[0], at).start()
    local_states(rows[0])
    relay_kv(rows[1])
    for at in range(T // CH):
        load(2, q_hbm, rows[1], at).start()
    copy_a(rows[0]).wait_recv()
    lax.fori_loop(1, 4, send_total(rows[0]), 0)
    local_states(rows[1])
    copy_a(rows[1]).wait_recv()
    lax.fori_loop(1, 4, send_total(rows[1]), 0)
    for row in rows:
        chip_total(4 * row + x)
        rbuf[4 * row + x] = tbuf[4 * row + x]

    def fold(row):
        for d in range(1, 4):
            arrival_1(4 * row + lax.rem(x + d, 4)).wait_recv()
        for r in range(2):
            total = rbuf[4 * row, r]
            for n in range(1, 4):
                term = rbuf[4 * row + n, r]
                total = jnp.concatenate(
                    [jnp.exp(term[HS : HS + 1]) * total[:HS] + term[:HS], total[HS:] + term[HS:]], axis=0
                )
            row_total[row, r] = total

    def copy_t(row):
        return remote(row_total.at[row], twin_total.at[row], st.at[row], rt.at[row], twin)

    for row in rows:

        def relay_q(at, _):
            load(2, q_hbm, row, at).wait()
            span = pl.ds(pl.multiple_of(at * CH, CH), CH)
            qh[pl.ds(16 * row, 16), span, :] = heads_first(2, row, at)
            return 0

        lax.fori_loop(0, T // CH, relay_q, 0)

    lane = lax.broadcasted_iota(jnp.int32, (16, 64), 1)
    wide_lane = lax.broadcasted_iota(jnp.int32, (16, HS), 1)
    diagonal = lax.broadcasted_iota(jnp.int32, (16, 16), 0) == lax.broadcasted_iota(jnp.int32, (16, 16), 1)
    for h in range(2):
        spread_gain = jnp.broadcast_to(gain_ref[h : h + 1, :], (16, 16))
        gain = jnp.sum(jnp.where(diagonal, spread_gain, 0.0), axis=1, keepdims=True)
        for i in range(4):
            gated[i, h] = gain * jax.nn.sigmoid(gate_ref[i, h].astype(F32))

    def give(p, _):
        here = lane == slot_ref[p]
        message = jnp.zeros((16, HS), F32)
        for h in range(2):
            for i in range(4):
                value = jnp.sum(jnp.where(here, dv_ref[i, h].astype(F32), 0.0), axis=1, keepdims=True)
                factor = jnp.sum(jnp.where(here, gated[i, h], 0.0), axis=1, keepdims=True)
                message = jnp.where(wide_lane == 4 * h + i, value, message)
                message = jnp.where(wide_lane == 8 + 4 * h + i, factor, message)
        given[p] = message
        return 0

    lax.fori_loop(0, 8, give, 0)

    def copy_v(to):
        return remote(given.at[to], taken.at[g], sv.at[to], rv.at[g], (c, to))

    def arrival_v(frm):
        return remote(given.at[frm], taken.at[frm], sv.at[frm], rv.at[frm], (c, frm))

    def send_v(d, _):
        copy_v(lax.rem(g + d, 8)).start()
        return 0

    lax.fori_loop(1, 8, send_v, 0)
    taken[g] = given[g]

    pick = lax.broadcasted_iota(jnp.int32, (8, 64), 1)
    scale = jnp.exp(decay_ref[...])

    def decode_row(at, s, ys):
        here = lane == s
        q, k = dq_ref[s].astype(F32), dk_ref[s].astype(F32)
        factor = jnp.sum(jnp.where(pick == s, scale, 0.0), axis=1, keepdims=True)
        ys = list(ys)
        for h in range(2):
            state = cache[at, h]
            for i in range(4):
                value = jnp.sum(jnp.where(here, dv_ref[i, h].astype(F32), 0.0), axis=1, keepdims=True)
                state = factor[2 * i + h : 2 * i + h + 1] * state + value * k[i, h : h + 1, :]
                if ys:
                    y = jnp.sum(state * q[i, h : h + 1, :], axis=1, keepdims=True)
                    ys[2 * i + h] = jnp.where(here, y, ys[2 * i + h])
            cache[at, h] = state
        return tuple(ys)

    cache_load.wait()
    ys = lax.fori_loop(
        0, 32, lambda s, ys: decode_row(s, s, ys), tuple(jnp.zeros((16, 64), F32) for _ in range(8)), unroll=2
    )
    fold(rows[0])
    copy_t(rows[0]).start()
    ys = lax.fori_loop(32, 64, lambda s, ys: decode_row(s, s, ys), ys, unroll=2)
    fresh = lane < 64
    for p in range(8):
        fresh = jnp.logical_and(fresh, lane != slot_ref[p])
    for i in range(4):
        squares = jnp.zeros((1, 64), F32)
        parts = []
        for h in range(2):
            y = jnp.where(fresh, ys[2 * i + h], 0.0)
            squares = squares + jnp.sum(y * y, axis=0, keepdims=True)
            parts.append(y * gated[i, h])
        parts.append(jnp.broadcast_to(squares, (8, 64)))
        parts.append(jnp.zeros((HS - 40, 64), F32))
        zrow[pl.ds(i, 64, stride=4), :] = jnp.concatenate(parts, axis=0).T
    zmine[...] = zrow[...].T[:40]

    def copy_z(to):
        return remote(zmine, zbuf.at[g], sz.at[to], rz.at[g], (c, to))

    def arrival_z(frm):
        return remote(zmine, zbuf.at[frm], sz.at[frm], rz.at[frm], (c, frm))

    def send_z(d, _):
        copy_z(lax.rem(g + d, 8)).start()
        return 0

    lax.fori_loop(1, 8, send_z, 0)
    zbuf[g] = zmine[...]

    to_row = lax.broadcasted_iota(jnp.int32, (256, HS), 0)
    from_row = lax.broadcasted_iota(jnp.int32, (256, HS), 1)
    target = jnp.zeros((256, HS), jnp.int32)
    for p in range(8):
        target = jnp.where(lax.div(from_row, 16) == p, 4 * slot_ref[p], target)
    hit = to_row == target + lax.rem(from_row, 4)
    for n in range(3):
        kind = lax.rem(lax.div(from_row, 4), 4) == n
        place[n] = jnp.where(jnp.logical_and(hit, kind), 1.0, 0.0).astype(BF16)

    causal = lax.broadcasted_iota(jnp.int32, (HS, HS), 0) >= lax.broadcasted_iota(jnp.int32, (HS, HS), 1)

    def attend(h):
        row = cum2[pl.ds(h, 1), :]
        col = jnp.broadcast_to(row, (HS, T)).T
        left = dot(qh[h], kt[h, :, 0:256])
        right = dot(qh[h, 256:512, :], kt[h, :, 256:512])

        def weigh(a, b):
            scores = left if b < 2 else right
            first = a if b < 2 else a - 2
            part = scores[first * HS : (first + 1) * HS, (b % 2) * HS : (b % 2 + 1) * HS]
            diff = col[a * HS : (a + 1) * HS] - row[:, b * HS : (b + 1) * HS]
            if a == b:
                diff = jnp.where(causal, diff, -1e30)
            return (part * jnp.exp2(diff)).astype(BF16)

        v = vh[h]
        none = jnp.zeros((HS, HS), BF16)
        top = jnp.concatenate([
            jnp.concatenate([weigh(0, 0), none], axis=1),
            jnp.concatenate([weigh(1, 0), weigh(1, 1)], axis=1),
        ], axis=0)
        low = jnp.concatenate([
            jnp.concatenate([weigh(2, 0), weigh(2, 1), weigh(2, 2), none], axis=1),
            jnp.concatenate([weigh(3, 0), weigh(3, 1), weigh(3, 2), weigh(3, 3)], axis=1),
        ], axis=0)
        att[h, 0:256, :] = dot(top, v[0:256])
        att[h, 256:512, :] = dot(low, v)

    def some(n, _):
        for u in range(UNROLL):
            attend(UNROLL * n + u)
        return 0

    lax.fori_loop(0, HEADS_AT_SCAN // UNROLL, some, 0)

    def copy_2(j):
        return remote(pbuf.at[j], qbuf.at[mine_of(j)], s2.at[j], r2.at[mine_of(j)], in_row(j))

    def arrival_2(j):
        return remote(pbuf.at[j], qbuf.at[j], s2.at[j], r2.at[j], in_row(j))

    fold(rows[1])

    @pl.when(own_row == 0)
    def _():
        copy_t(0).start()

    copy_t(own_row).wait_recv()

    def through(total, state):
        return jnp.exp(total[HS : HS + 1]) * state + total[:HS]

    for r in range(2):

        @pl.when(own_row == 0)
        def _():
            pcur[r] = through(twin_total[own_row, r], through(row_total[own_row, r], start_ref[r]))

        @pl.when(own_row == 1)
        def _():
            pcur[r] = through(row_total[own_row, r], through(twin_total[own_row, r], start_ref[r]))

    def before_chip(j, _):
        row = lax.div(j, 4)
        pbuf[j] = row_start[row]

        @pl.when(lax.rem(j, 4) != x)
        def _():
            copy_2(j).start()

        for r in range(2):
            row_start[row, r] = through(rbuf[j, r], row_start[row, r])
        return 0

    remote(start_ref, start_all.at[rows[0]], ss, rs, twin).wait_recv()

    @pl.when(own_row == 0)
    def _():
        row_start[...] = start_all[...]
        lax.fori_loop(0, 8, before_chip, 0)

    @pl.when(own_row == 1)
    def _():
        for r in range(2):
            row_start[1, r] = through(twin_total[1, r], start_all[1, r])
        lax.fori_loop(4, 8, before_chip, 0)

    def wait_v(d, _):
        arrival_v(lax.rem(g + d, 8)).wait_recv()
        return 0

    lax.fori_loop(1, 8, wait_v, 0)
    columns = jnp.concatenate([taken[n] for n in range(8)], axis=0)
    mine = slot_ref[g]
    q, k = dq_ref[mine].astype(F32), dk_ref[mine].astype(F32)
    step_scale = jnp.sum(jnp.where(pick == mine, scale, 0.0), axis=1, keepdims=True)
    tall_lane = lax.broadcasted_iota(jnp.int32, (HS, HS), 1)
    tall = jnp.zeros((HS, HS), F32)
    for h in range(2):
        state = pcur[h].T
        fbuf[:, h] = state.reshape(8, 16, HS)
        for i in range(4):
            n = 4 * h + i
            state = step_scale[2 * i + h : 2 * i + h + 1] * state + columns[:, n : n + 1] * k[i, h : h + 1, :]
            y = jnp.sum(state * q[i, h : h + 1, :], axis=1, keepdims=True)
            tall = jnp.where(tall_lane == n, y * columns[:, 8 + n : 9 + n], tall)
            squares = jnp.sum(y * y, axis=0, keepdims=True)
            tall = jnp.where(tall_lane == 8 + i, tall + squares, tall)
    ymine[...] = tall.T[:16]

    def copy_y(to):
        return remote(ymine, ybuf.at[g], sy.at[to], ry.at[g], (c, to))

    def arrival_y(frm):
        return remote(ymine, ybuf.at[frm], sy.at[frm], ry.at[frm], (c, frm))

    def send_y(d, _):
        copy_y(lax.rem(g + d, 8)).start()
        return 0

    lax.fori_loop(1, 8, send_y, 0)

    @pl.when(own_row == 1)
    def _():
        copy_t(0).wait_recv()
        for r in range(2):
            row_start[0, r] = through(twin_total[0, r], start_all[0, r])
        lax.fori_loop(0, 4, before_chip, 0)

    for row in range(2):
        qbuf[4 * row + x] = pbuf[4 * row + x]
    ybuf[g] = ymine[...]

    def copy_h(to):
        return remote(fbuf.at[to], hbuf.at[g], sh.at[to], rh.at[g], (c, to))

    def arrival_h(frm):
        return remote(fbuf.at[frm], hbuf.at[frm], sh.at[frm], rh.at[frm], (c, frm))

    def send_h(d, _):
        copy_h(lax.rem(g + d, 8)).start()
        return 0

    lax.fori_loop(1, 8, send_h, 0)
    hbuf[g] = fbuf[g]

    def wait_z(d, _):
        frm = lax.rem(g + d, 8)
        arrival_z(frm).wait_recv()
        arrival_w(frm).wait_recv()
        return 0

    lax.fori_loop(1, 8, wait_z, 0)
    for h in range(2):
        for frm in range(8):
            at = h * HS + frm * 16
            wt[at : at + 16, :] = wr[frm, h * 16 : (h + 1) * 16, :].astype(BF16)
    z = jnp.concatenate([zbuf[n, 16 * h : 16 * h + 16, :] for h in range(2) for n in range(8)], axis=0).T
    squares = zbuf[0, 32:40, :]
    for n in range(1, 8):
        squares = squares + zbuf[n, 32:40, :]
    squares = jnp.concatenate([squares] * 16, axis=0).T
    hi, lo = split(z)
    for n in range(3):
        span = slice(n * 256, (n + 1) * 256)
        w = wt[:, span]
        both = (dot(hi, w) + dot(lo, w)).reshape(8, 2, 16, 256)
        for k in range(2):
            part[k, :, :, span] = both[:, k]
    both = squares.reshape(8, 2, 16, HS)
    for k in range(2):
        part[k, :, :, 768:896] = both[:, k]
    lax.fori_loop(HEADS_AT_SCAN // UNROLL, HEADS_AT_GATHER // UNROLL, some, 0)

    def wait_y(d, _):
        arrival_y(lax.rem(g + d, 8)).wait_recv()
        return 0

    lax.fori_loop(1, 8, wait_y, 0)
    hi, lo = split(ybuf[...].reshape(HS, HS))
    squares = (dot(place[2], hi) + dot(place[2], lo)).reshape(8, 2, 16, HS)
    hi = [dot(place[h], hi).astype(BF16) for h in range(2)]
    lo = [dot(place[h], lo).astype(BF16) for h in range(2)]
    z = jnp.concatenate([jnp.concatenate(hi, axis=1), jnp.concatenate(lo, axis=1)], axis=0)
    for n in range(3):
        span = slice(n * 256, (n + 1) * 256)
        both = dot(z, wt[:, span])
        both = (both[:256] + both[256:]).reshape(8, 2, 16, 256)
        for k in range(2):
            part[k, :, :, span] = part[k, :, :, span] + both[:, k]
    for k in range(2):
        part[k, :, :, 768:896] = part[k, :, :, 768:896] + squares[:, k]
    copy_c = remote(part.at[other], half, sc, rc, partner)
    copy_c.start()
    lax.fori_loop(HEADS_AT_GATHER // UNROLL, HEADS_AT_SUM // UNROLL, some, 0)

    def copy_b(m):
        return remote(obuf.at[pl.ds(4 * m, 4)], states.at[core, pl.ds(4 * m, 4)], sb.at[m], rb.at[m], partner)

    def arrival_b(m):
        return remote(obuf.at[pl.ds(4 * m, 4)], states.at[other, pl.ds(4 * m, 4)], sb.at[m], rb.at[m], partner)

    def spread(m, _):
        for n in range(2):
            j = 2 * m + n

            @pl.when(lax.rem(j, 4) != x)
            def _():
                arrival_2(j).wait_recv()

            for r in range(2):
                i = 2 * j + r
                before = qbuf[j, r]
                first = jnp.where(core == 0, s_ref[core, i], xbuf[i])
                after = jnp.exp(first[HS : HS + 1]) * before + first[:HS]
                states[core, i] = jnp.where(core == 0, before, after)
                obuf[i] = jnp.where(core == 0, after, before)
        copy_b(m).start()
        return 0

    copy_c.wait_recv()
    half[...] = half[...] + part[core]

    def copy_p(to):
        return remote(half.at[to], take.at[chip], sp.at[to], rp.at[chip], peer(to))

    def arrival_p(frm):
        return remote(half.at[frm], take.at[frm], sp.at[frm], rp.at[frm], peer(frm))

    def send_p(d, _):
        copy_p(lax.rem(chip + d, 8)).start()
        return 0

    lax.fori_loop(1, 8, send_p, 0)
    take[chip] = half[chip]
    lax.fori_loop(HEADS_AT_SUM // UNROLL, H // UNROLL, some, 0)
    lax.fori_loop(0, 4, spread, 0)

    def take_b(m, _):
        arrival_b(m).wait_recv()
        return 0

    lax.fori_loop(0, 4, take_b, 0)
    for h in range(H):
        hi, lo = split(states[(h // 2) % 2, 2 * (h // 4) + h % 2])
        wide[h, :, 0:HS] = hi
        wide[h, :, HS:] = lo

    def finish_chunk(at):
        span = slice(at * CH, (at + 1) * CH)
        squares = jnp.zeros((CH, HS), F32)
        for h in range(H):
            both = dot(qh[h, span, :], wide[h])
            field = att[h, span, :] + (both[:, :HS] + both[:, HS:]) * ec[span, h : h + 1]
            att[h, span, :] = field
            squares = squares + field * field
        mean = jnp.sum(squares, axis=1, keepdims=True) / (H * HS)
        factor = jnp.broadcast_to(lax.rsqrt(mean + 1e-06), (CH, HS))
        out_ref[span] = jnp.swapaxes((att[:, span, :] * factor[None]).astype(BF16), 0, 1)

    for at in range(2):
        finish_chunk(at)

    def wait_p(d, _):
        arrival_p(lax.rem(chip + d, 8)).wait_recv()
        return 0

    lax.fori_loop(1, 8, wait_p, 0)
    total = take[0]
    for n in range(1, 8):
        total = total + take[n]
    total = total[:, :768] * lax.rsqrt(total[:, 768:769] / (H * HS) + 1e-06)
    for n in range(8):
        done[n] = total[2 * n : 2 * n + 2]

    def copy_d(to):
        return remote(done.at[to], last.at[g], sd.at[to], rd.at[g], (c, to))

    def arrival_d(frm):
        return remote(done.at[frm], last.at[frm], sd.at[frm], rd.at[frm], (c, frm))

    def send_d(d, _):
        copy_d(lax.rem(g + d, 8)).start()
        return 0

    lax.fori_loop(1, 8, send_d, 0)
    last[g] = done[g]

    for at in range(2, T // CH):
        finish_chunk(at)

    def take_h(d, _):
        arrival_h(lax.rem(g + d, 8)).wait_recv()
        return 0

    lax.fori_loop(1, 8, take_h, 0)
    cache[64:72] = hbuf[...]
    lax.fori_loop(0, 8, lambda p, ys: decode_row(64 + p, slot_ref[p], ys), ())

    def merge(s, _):
        at = s
        for p in range(8):
            at = jnp.where(slot_ref[p] == s, 64 + p, at)
        new_ref[s] = cache[at]
        return 0

    lax.fori_loop(0, 64, merge, 0)

    def wait_d(d, _):
        arrival_d(lax.rem(g + d, 8)).wait_recv()
        return 0

    lax.fori_loop(1, 8, wait_d, 0)
    for n in range(8):
        decoded_ref[:, n * 768 : (n + 1) * 768] = last[n]

    for row in rows:
        copy_a(row).wait_send()
    copy_c.wait_send()

    def finish_pair(m, _):
        copy_b(m).wait_send()
        return 0

    lax.fori_loop(0, 4, finish_pair, 0)

    def finish(d, _):
        j = lax.rem(chip + d, 8)
        copy_p(j).wait_send()
        to = lax.rem(g + d, 8)
        copy_w(to).wait_send()
        copy_h(to).wait_send()
        copy_z(to).wait_send()
        copy_d(to).wait_send()
        copy_v(to).wait_send()
        copy_y(to).wait_send()
        return 0

    lax.fori_loop(1, 8, finish, 0)

    def finish_rows(d, _):
        for row in range(2):
            j = 4 * row + lax.rem(x + d, 4)
            copy_1(j).wait_send()
            copy_2(j).wait_send()
        return 0

    lax.fori_loop(1, 4, finish_rows, 0)
    copy_s.wait_send()
    copy_t(rows[0]).wait_send()

    @pl.when(own_row == 0)
    def _():
        copy_t(0).wait_send()


def per_device(
    queries, keys, values, prefill_decay, start_states, resident_states, slot_of_prompt,
    decode_queries, decode_keys, decode_values, decode_gate, decode_decay, norm_gain, out_weight,
):
    dma = pltpu.SemaphoreType.DMA
    hbm, vmem = pl.BlockSpec(memory_space=pl.ANY), pl.BlockSpec(memory_space=pltpu.VMEM)
    results = (
        jax.ShapeDtypeStruct((T, H, HS), BF16),
        jax.ShapeDtypeStruct((64, 2, 16, HS), F32),
        jax.ShapeDtypeStruct((2, 6144), F32),
    )
    prefill_out, cache, decoded = pl.pallas_call(
        kernel,
        name="lightning",
        out_shape=tuple(pltpu.VMEM(x.shape, x.dtype) for x in results),
        in_specs=[pl.BlockSpec(memory_space=pltpu.SMEM), hbm, hbm, hbm, vmem, vmem, vmem, hbm] + [vmem] * 6,
        out_specs=(vmem, vmem, vmem),
        scratch_shapes=[
            pltpu.VMEM((2, 2, T, 16, HS), BF16),
            pltpu.VMEM((H, T, HS), BF16),
            pltpu.VMEM((H, HS, T), BF16),
            pltpu.VMEM((H, T, HS), BF16),
            pltpu.VMEM((H, T), F32),
            pltpu.VMEM((H, T), F32),
            pltpu.VMEM((T, HS), F32),
            pltpu.VMEM((2, 16, ROWS, HS), F32),
            pltpu.VMEM((16, ROWS, HS), F32),
            pltpu.VMEM((8, 2, ROWS, HS), F32),
            pltpu.VMEM((8, 2, ROWS, HS), F32),
            pltpu.VMEM((8, 2, HS, HS), F32),
            pltpu.VMEM((8, 2, HS, HS), F32),
            pltpu.VMEM((16, HS, HS), F32),
            pltpu.VMEM((2, 16, HS, HS), F32),
            pltpu.VMEM((2, HS, HS), F32),
            pltpu.VMEM((8, 2, 16, HS), F32),
            pltpu.VMEM((8, 2, 16, HS), F32),
            pltpu.VMEM((8, 32, 768), F32),
            pltpu.VMEM((8, 32, 768), F32),
            pltpu.VMEM((256, 768), BF16),
            pltpu.VMEM((H, T, HS), F32),
            pltpu.VMEM((H, HS, 2 * HS), BF16),
            pltpu.VMEM((72, 2, 16, HS), F32),
            pltpu.VMEM((256, HS), F32),
            pltpu.VMEM((40, 256), F32),
            pltpu.VMEM((8, 40, 256), F32),
            pltpu.VMEM((2, 8, 16, 896), F32),
            pltpu.VMEM((8, 16, 896), F32),
            pltpu.VMEM((8, 16, 896), F32),
            pltpu.VMEM((8, 2, 768), F32),
            pltpu.VMEM((8, 2, 768), F32),
            pltpu.VMEM((4, 2, 16, 64), F32),
            pltpu.VMEM((8, 16, HS), F32),
            pltpu.VMEM((8, 16, HS), F32),
            pltpu.VMEM((16, HS), F32),
            pltpu.VMEM((8, 16, HS), F32),
            pltpu.VMEM((3, 256, HS), BF16),
            pltpu.VMEM((2, 2, ROWS, HS), F32),
            pltpu.VMEM((2, 2, ROWS, HS), F32),
            pltpu.VMEM((2, 2, HS, HS), F32),
            pltpu.VMEM((2, 2, HS, HS), F32),
            dma((3, 2, T // CH)), dma,
            dma((2,)), dma((2,)), dma((8,)), dma((8,)), dma((8,)), dma((8,)),
            dma((4,)), dma((4,)), dma((8,)), dma((8,)), dma((8,)), dma((8,)),
            dma((8,)), dma((8,)), dma, dma, dma((8,)), dma((8,)), dma((8,)), dma((8,)),
            dma((8,)), dma((8,)), dma((8,)), dma((8,)), dma((2,)), dma((2,)), dma, dma,
        ],
        compiler_params=pltpu.CompilerParams(
            collective_id=0, has_side_effects=True, vmem_limit_bytes=VMEM_LIMIT
        ),
    )(
        slot_of_prompt,
        queries[0],
        keys[0],
        values[0],
        jnp.swapaxes(prefill_decay[0], 0, 1),
        start_states[0],
        out_weight.reshape(32, 6144),
        jnp.swapaxes(resident_states, 2, 3),
        decode_queries,
        decode_keys,
        jnp.transpose(decode_values, (1, 2, 3, 0)),
        jnp.transpose(decode_gate, (1, 2, 3, 0)),
        jnp.transpose(decode_decay, (1, 2, 0)).reshape(8, 64),
        norm_gain,
    )
    return prefill_out[None], jnp.swapaxes(cache, 2, 3), decoded


def solution(mesh):
    return jax.shard_map(
        per_device,
        mesh=mesh,
        in_specs=(
            P("grp", "ctx", None, None),
            P("grp", "ctx", None, None),
            P("grp", "ctx", None, None),
            P("grp", "ctx", None),
            P("grp", "ctx", None, None),
            P(None, "ctx", None, "grp"),
            P(),
            P(None, None, "ctx", None),
            P(None, None, "ctx", None),
            P(None, None, "ctx", "grp"),
            P(None, None, "ctx", "grp"),
            P(None, None, "ctx"),
            P("ctx", "grp"),
            P("ctx", "grp", None),
        ),
        out_specs=(
            P("grp", "ctx", None, None),
            P(None, "ctx", None, "grp"),
            P(("ctx", "grp"), None),
        ),
        check_vma=False,
    )
```
